32 devices in a mesh: dp: 8 (over z, x), fsdp: 4 (over y, core).
Axes of the slice: x: 2, y: 2, z: 4, core: 2. Of those that a mesh axis runs over, the one named last changes fastest.
Arguments:
- tokens: bfloat16 [16, 256, 1024], P('dp', 'fsdp'), may hold values from -6 to 6
- masks: int32 [16, 256], P('dp', 'fsdp'), may hold values from 0 to 1, as said below
- cotangent: bfloat16 [16, 256, 1024], P('dp', 'fsdp')
- w_in: float32 [1024, 10, 1024], P('dp', None, 'fsdp'), may hold values from -0.09375 to 0.09375
- w_out: float32 [6, 1024, 1024], P(None, 'fsdp', 'dp')
- vectors: float32 [4, 1024], P(None, 'dp')
- m_in: float32 [1024, 10, 1024], P('dp', None, 'fsdp'), may hold values from -0.0004272461 to 0.0004272461
- m_out: float32 [6, 1024, 1024], P(None, 'fsdp', 'dp'), may hold values from -0.0004272461 to 0.0004272461
- m_vec: float32 [4, 1024], P(None, 'dp'), may hold values from -0.0012207031 to 0.0012207031
- v_in: float32 [1024, 10, 1024], P('dp', None, 'fsdp'), may hold values from 1.5685433e-09 to 2.5096693e-08
- v_out: float32 [6, 1024, 1024], P(None, 'fsdp', 'dp'), may hold values from 1.5685433e-09 to 2.5096693e-08
- v_vec: float32 [4, 1024], P(None, 'dp'), may hold values from 4.6748743e-09 to 7.947286e-08
Outputs:
- output: bfloat16 [16, 256, 1024], P('dp', 'fsdp')
- token_grad: bfloat16 [16, 256, 1024], P('dp', 'fsdp')
- grad_norm: float32 [], replicated
- new_w_in: float32 [1024, 10, 1024], P('dp', None, 'fsdp')
- new_w_out: float32 [6, 1024, 1024], P(None, 'fsdp', 'dp')
- new_vectors: float32 [4, 1024], P(None, 'dp')
- new_m_in: float32 [1024, 10, 1024], P('dp', None, 'fsdp')
- new_m_out: float32 [6, 1024, 1024], P(None, 'fsdp', 'dp')
- new_m_vec: float32 [4, 1024], P(None, 'dp')
- new_v_in: float32 [1024, 10, 1024], P('dp', None, 'fsdp')
- new_v_out: float32 [6, 1024, 1024], P(None, 'fsdp', 'dp')
- new_v_vec: float32 [4, 1024], P(None, 'dp')
The draws below stay inside these ranges and needn't reach their ends.
Inputs may be any that keep to these rules, and one draw needn't show every extreme that they name: `masks`: each clip has its own masking rate, drawn between one half and 0.99; tokens are masked independently at that rate.
All inputs are finite; a program needn't handle non-finite values.
Results may differ from the reference program's by a relative error of at most 0.02.
The reference program's roundings to bfloat16 on the way count: a program that leaves them out, or rounds other values in their place, can miss the bound.
Values may be sent and summed in bfloat16 or wider, within the bound.
A program may use at most 128 MiB of HBM per device.

```python
import math
import jax
import jax.numpy as jnp
from jax import lax

D = 1024
HEADS = 16
FF = 4096
S = 256
FRAMES = 16
STEP = 10
HDIM = 64
CLIPS = 1
FRAME_ROWS = 16


def draw_masks(key, part):
    key = jax.random.fold_in(key, 11)
    ratio_key, token_key = jax.random.split(key)
    ratios = jax.random.randint(ratio_key, (CLIPS, 1, 1), 50, 100)
    rolls = jax.random.randint(token_key, (CLIPS, FRAMES, S), 0, 100)
    return (rolls < ratios).astype(jnp.int32).reshape(CLIPS * FRAMES, S)


def draw_cotangent(key, part):
    key = jax.random.fold_in(key, 12)
    column = jnp.arange(D, dtype=jnp.float32) / (D - 1)
    base = jax.random.normal(key, (CLIPS * FRAMES, S, D), jnp.float32)
    rising = 1.0 + 2.0 * column
    return (base * rising).astype(jnp.bfloat16)


def draw_w_out(key, part):
    key = jax.random.fold_in(key, 13)
    slot_ids = jnp.arange(6)[:, None, None]
    spatial_scale = 0.5 * math.sqrt(S / D)
    temporal_scale = 0.5 * math.sqrt(FRAMES / D)
    down_scale = 1.0 / math.sqrt(FF)
    scales = jnp.where(slot_ids == 0, spatial_scale, jnp.where(slot_ids == 1, temporal_scale, down_scale)).astype(jnp.float32)
    base = jax.random.normal(key, (6, D, D), jnp.float32)
    return base * scales


def draw_vectors(key, part):
    key = jax.random.fold_in(key, 14)
    gain_key, embed_key = jax.random.split(key)
    column = jnp.arange(D, dtype=jnp.float32) / (D - 1)
    gains = (1.0 + 2.0 * column) * jax.random.uniform(gain_key, (3, D), jnp.float32, 0.9, 1.1)
    embed = jax.random.normal(embed_key, (1, D), jnp.float32)
    return jnp.concatenate([gains, embed], axis=0)


def shard_levels(key, dims, shards, least, high):
    def one(dim, shards_of):
        draws = jax.random.uniform(jax.random.fold_in(jax.random.fold_in(key, 6), dim), (shards_of,), jnp.float32, least / len(shards), high / len(shards))
        return jnp.repeat(jnp.exp(draws), dims[dim] // shards_of).reshape((-1,) + (1,) * (len(dims) - dim - 1))

    level = one(*shards[0])
    for cut in shards[1:]:
        level = level * one(*cut)
    return level


def bell_draw(key, shape, scale, limit, shards=(), kind=jnp.bfloat16):
    level = shard_levels(key, shape, shards, -0.22, 0.18) if shards else 1.0
    array = jax.random.normal(key, shape, jnp.float32) * scale * level
    return jnp.minimum(jnp.maximum(array, -limit), limit).astype(kind)


def setup_inputs(seed: int = 0) -> dict:
    key_of = jax.random.split(jax.random.key(seed), 13)
    tokens = bell_draw(key_of[0], (FRAME_ROWS, S, D), 1.0, 6.0, ((0, 8), (1, 4)))
    masks = draw_masks(jax.random.fold_in(key_of[12], 71), 0)
    cotangent = draw_cotangent(jax.random.fold_in(key_of[12], 71), 0)
    w_in = bell_draw(key_of[3], (D, 10, D), (4 * D) ** -0.5, 0.09375, ((0, 8), (2, 4)), jnp.float32)
    w_out = draw_w_out(jax.random.fold_in(key_of[12], 71), 0)
    vectors = draw_vectors(jax.random.fold_in(key_of[12], 71), 0)
    m_in = bell_draw(key_of[6], (D, 10, D), ((36 * D) ** -1), 0.0004272461, ((0, 8), (2, 4)), jnp.float32)
    m_out = bell_draw(key_of[7], (6, D, D), ((36 * D) ** -1), 0.0004272461, ((1, 4), (2, 8)), jnp.float32)
    m_vec = bell_draw(key_of[8], (4, D), ((12 * D) ** -1), 0.0012207031, ((1, 8),), jnp.float32)
    v_in = jnp.clip(jnp.exp(math.log(2.509669272399151e-08) - 2.7725887 * jax.random.uniform(key_of[9], (D, 10, D), jnp.float32) ** shard_levels(key_of[9], (D, 10, D), ((0, 8), (2, 4)), -0.2, 0.2)), 1.5685432952494693e-09, 2.509669272399151e-08)
    v_out = jnp.clip(jnp.exp(math.log(2.509669272399151e-08) - 2.7725887 * jax.random.uniform(key_of[10], (6, D, D), jnp.float32) ** shard_levels(key_of[10], (6, D, D), ((1, 4), (2, 8)), -0.2, 0.2)), 1.5685432952494693e-09, 2.509669272399151e-08)
    v_vec = jnp.clip(jnp.exp(math.log(7.947286206899662e-08) - 2.8332133 * jax.random.uniform(key_of[11], (4, D), jnp.float32) ** shard_levels(key_of[11], (4, D), ((1, 8),), -0.2, 0.2)), 4.674874265475637e-09, 7.947286206899662e-08)
    return {"tokens": tokens, "masks": masks, "cotangent": cotangent, "w_in": w_in, "w_out": w_out, "vectors": vectors, "m_in": m_in, "m_out": m_out, "m_vec": m_vec, "v_in": v_in, "v_out": v_out, "v_vec": v_vec}


EPS_NORM = 1e-05
CLIP_AT = 1.0
BETA_FIRST = 0.9
BETA_SECOND = 0.95
ADAM_EPS = 1e-08
DECAY_RATE = 0.1
RATE_INPUT = 0.02
RATE_OUTPUT = 0.08
RATE_VECTOR = 1.0
NEG_FILL = -1e+30
HIGH = lax.Precision.HIGHEST

@jax.custom_vjp
def low(v):
    return lax.optimization_barrier(v.astype(jnp.bfloat16)).astype(jnp.float32)

@jax.custom_vjp
def low_back(v):
    return v

def low_keep(v):
    return (low(v), None)

def low_pass(kept, grad):
    return (grad,)

def back_keep(v):
    return (v, None)

def back_low(kept, grad):
    return (low(grad),)
low.defvjp(low_keep, low_pass)
low_back.defvjp(back_keep, back_low)

def layer_norm(values, gain):
    centered = values - lax.optimization_barrier(jnp.mean(values, axis=-1, keepdims=True))
    spread = lax.optimization_barrier(jnp.mean(centered * centered, axis=-1, keepdims=True))
    return centered * lax.rsqrt(spread + EPS_NORM) * gain

def softmax_of(scores, axis_at):
    peak = lax.optimization_barrier(jnp.max(scores, axis=axis_at, keepdims=True))
    expd = jnp.exp(scores - peak)
    return expd / lax.optimization_barrier(jnp.sum(expd, axis=axis_at, keepdims=True))

def rounded_both(values):
    return low(low_back(values))

def clip_forward(inputs, mask_rows, wide_in, wide_out, small):
    score_scale = HDIM ** (-0.5)
    heads_shape = (FRAMES, S, HEADS, HDIM)
    embedded = jnp.where(mask_rows[:, :, None] == 1, small[3], inputs)
    normed_one = low(layer_norm(embedded, small[0]))
    proj_one = jnp.einsum('fsd,dcn->fscn', normed_one, wide_in[:, 0:3], precision=HIGH)
    query_one = rounded_both(proj_one[:, :, 0]).reshape(heads_shape)
    key_one = rounded_both(proj_one[:, :, 1]).reshape(heads_shape)
    value_one = rounded_both(proj_one[:, :, 2]).reshape(heads_shape)
    scores_one = low_back(jnp.einsum('fqhe,fkhe->fhqk', query_one, key_one, precision=HIGH) * score_scale)
    mixed_one = rounded_both(jnp.einsum('fhqk,fkhe->fqhe', low(softmax_of(scores_one, 3)), value_one, precision=HIGH)).reshape(FRAMES, S, D)
    first_mid = embedded + low_back(jnp.einsum('fsn,nd->fsd', mixed_one, wide_out[0], precision=HIGH))
    normed_two = low(layer_norm(first_mid, small[1]))
    proj_two = jnp.einsum('fsd,dcn->fscn', normed_two, wide_in[:, 3:6], precision=HIGH)
    query_two = rounded_both(proj_two[:, :, 0]).reshape(heads_shape)
    key_two = rounded_both(proj_two[:, :, 1]).reshape(heads_shape)
    value_two = rounded_both(proj_two[:, :, 2]).reshape(heads_shape)
    frame_ids = jnp.arange(FRAMES)
    causal = (frame_ids[:, None] >= frame_ids[None, :])[None, :, :, None]
    scores_two = low_back(jnp.einsum('fshe,gshe->hfgs', query_two, key_two, precision=HIGH) * score_scale)
    scores_two = jnp.where(causal, scores_two, NEG_FILL)
    mixed_two = rounded_both(jnp.einsum('hfgs,gshe->fshe', low(softmax_of(scores_two, 2)), value_two, precision=HIGH)).reshape(FRAMES, S, D)
    second_mid = first_mid + low_back(jnp.einsum('fsn,nd->fsd', mixed_two, wide_out[1], precision=HIGH))
    normed_three = low(layer_norm(second_mid, small[2]))
    pre_act = low_back(jnp.einsum('fsd,dcn->fscn', normed_three, wide_in[:, 6:10], precision=HIGH))
    activated = low(jax.nn.gelu(pre_act))
    return second_mid + low_back(jnp.einsum('fscn,cnd->fsd', activated, wide_out[2:6], precision=HIGH))

def adamw_step(weight, first, second, grad, rate):
    first = BETA_FIRST * first + (1.0 - BETA_FIRST) * grad
    second = BETA_SECOND * second + (1.0 - BETA_SECOND) * grad * grad
    fix_first = 1.0 - BETA_FIRST ** STEP
    fix_second = 1.0 - BETA_SECOND ** STEP
    update = first / fix_first / (jnp.sqrt(second / fix_second) + ADAM_EPS)
    return (weight - rate * (update + DECAY_RATE * weight), first, second)

def reference(tokens, masks, cotangent, w_in, w_out, vectors, m_in, m_out, m_vec, v_in, v_out, v_vec):
    inputs = tokens.astype(jnp.float32).reshape(CLIPS, FRAMES, S, D)
    mask_clips = masks.reshape(CLIPS, FRAMES, S)

    def forward(inputs, w_in, w_out, vectors):
        wide_in = low(w_in)
        wide_out = low(w_out)
        small = low(vectors)

        def one_clip(clip_pair):
            return clip_forward(clip_pair[0], clip_pair[1], wide_in, wide_out, small)
        return lax.map(jax.checkpoint(one_clip), (inputs, mask_clips))
    result, pull_back = jax.vjp(forward, inputs, w_in, w_out, vectors)
    grad_tokens, grad_in, grad_out, grad_vec = pull_back(cotangent.astype(jnp.float32).reshape(CLIPS, FRAMES, S, D))
    total = jnp.sum(grad_in * grad_in) + jnp.sum(grad_out * grad_out) + jnp.sum(grad_vec * grad_vec)
    grad_norm = jnp.sqrt(total)
    factor = CLIP_AT / jnp.maximum(grad_norm, CLIP_AT)
    new_w_in, new_m_in, new_v_in = adamw_step(w_in, m_in, v_in, grad_in * factor, RATE_INPUT)
    new_w_out, new_m_out, new_v_out = adamw_step(w_out, m_out, v_out, grad_out * factor, RATE_OUTPUT)
    new_vectors, new_m_vec, new_v_vec = adamw_step(vectors, m_vec, v_vec, grad_vec * factor, RATE_VECTOR)
    output = result.reshape(FRAME_ROWS, S, D).astype(jnp.bfloat16)
    token_grad = grad_tokens.reshape(FRAME_ROWS, S, D).astype(jnp.bfloat16)
    return (output, token_grad, grad_norm, new_w_in, new_w_out, new_vectors, new_m_in, new_m_out, new_m_vec, new_v_in, new_v_out, new_v_vec)
```

```python
import functools
from types import SimpleNamespace

import jax
import jax.numpy as jnp
from jax import lax
from jax.experimental import pallas as pl
from jax.experimental.pallas import tpu as pltpu
from jax.sharding import PartitionSpec as P

FRAMES = 16
STEP = 10
HDIM = 64


EPS_NORM = 1e-05
CLIP_AT = 1.0
BETA_FIRST = 0.9
BETA_SECOND = 0.95
ADAM_EPS = 1e-08
DECAY_RATE = 0.1
RATE_INPUT = 0.02
RATE_OUTPUT = 0.08
RATE_VECTOR = 1.0
NEG_FILL = -1e30
GELU_A = 0.7978845608028654
GELU_B = 0.044715

F32 = jnp.float32
B16 = jnp.bfloat16
MESH = pl.DeviceIdType.MESH
CHUNK = 16
DP = "dp"
TP = "fsdp"
LANES = 128
VMEM_BYTES = 63 << 20


def at(dp, fsdp):
    return {DP: dp, TP: fsdp}


def nn(a, b):
    return lax.dot_general(a, b, (((1,), (0,)), ((), ())), preferred_element_type=F32)


def nt(a, b):
    return lax.dot_general(a, b, (((1,), (1,)), ((), ())), preferred_element_type=F32)


def tn(a, b):
    return lax.dot_general(a, b, (((0,), (0,)), ((), ())), preferred_element_type=F32)


def loop(low, high, step):
    def body(k, carry):
        step(k)
        return carry

    lax.fori_loop(low, high, body, 0)


def each(low, high, step):
    if high - low <= 8:
        for k in range(low, high):
            step(k)
    else:
        loop(low, high, step)


def scratch_of(z):
    rows, width, hidden, span = z.rows, z.width, z.hidden, z.span
    nd, nf, part, heads = z.nd, z.nf, z.part, z.heads
    outer = nd // 2
    flat = (nf, z.frames, z.here, hidden)
    vmem = pltpu.VMEM
    dma = pltpu.SemaphoreType.DMA
    return dict(
        weights=vmem((4, 4, width, hidden), B16),
        gathered=vmem((6, nf, rows, width), B16),
        gains=vmem((8, width), F32),
        tiles=vmem((nd, 8, LANES), F32),
        hats=vmem((3, rows, width), F32),
        rstds=vmem((3, rows, LANES), F32),
        work=vmem((rows, width), F32),
        mid=vmem((rows, width), F32),
        swap_out=vmem((5, span, CHUNK, width), B16),
        swap_in=vmem((5, span, CHUNK, width), B16),
        part_sum=vmem((2, 2, rows, width), F32),
        sib_out=vmem((2, 2, rows, width), B16),
        sib_in=vmem((2, 2, rows, width), B16),
        far_out=vmem((2, rows, width), B16),
        far_in=vmem((2, rows, width), B16),
        qkv=vmem((2, 3) + flat, B16),
        mixed=vmem((2,) + flat, B16),
        grad_mixed=vmem(flat, B16),
        grad_qkv=vmem((3,) + flat, B16),
        probs_a=vmem((z.frames * heads, nf * z.here, nf * z.here), F32),
        probs_b=vmem((nf * heads, rows, rows), F32),
        act=vmem((4,) + flat, B16),
        slope=vmem((4,) + flat, F32),
        grad_pre=vmem((4,) + flat, B16),
        product=vmem((outer, 2, part, hidden), F32),
        own_sum=vmem((16, outer, part, hidden), B16),
        pair_out=vmem((16, outer, part, hidden), B16),
        pair_in=vmem((16, outer, part, hidden), B16),
        line_in=vmem((16, outer, part, hidden), B16),
        vec_acc=vmem((8, width), F32),
        vec_out=vmem((width // LANES, 8, LANES), F32),
        vec_in=vmem((nd, 8, LANES), F32),
        vec_mine=vmem((8, LANES), F32),
        vec_side=vmem((nf, 8, LANES), F32),
        sq_mine=vmem((2, 8, LANES), F32),
        sq_side=vmem((nf, 8, LANES), F32),
        sq_all=vmem((nd, 8, LANES), F32),
        small_s=dma((5,)),
        small_r=dma((5,)),
        line_ws=dma((4,)),
        line_wr=dma((4, outer)),
        pair_ws=dma((4,)),
        pair_wr=dma((4,)),
        copy_w=dma((4,)),
        row_s=dma((6, 3)),
        row_r=dma((6, 3)),
        sum_s=dma((6, 3)),
        sum_r=dma((6, 3)),
        swap_s=dma((5,)),
        swap_r=dma((5,)),
        pair_gs=dma((16,)),
        pair_gr=dma((16,)),
        line_gs=dma((16,)),
        line_gr=dma((16,)),
    )


def layer(z, names, *refs):
    tok, msk, cot, shard, vec = refs[:5]
    out, tgr, nrm, gout, gvec = refs[5:10]
    s = SimpleNamespace(**dict(zip(names, refs[10:])))
    rows, width, hidden, span = z.rows, z.width, z.hidden, z.span
    nd, nf, part, heads = z.nd, z.nf, z.part, z.heads
    frames, here = z.frames, z.here
    outer = nd // 2
    piece = here // span
    n_pairs = heads // 2
    scale = HDIM**-0.5
    gathered, weights, gains = s.gathered, s.weights, s.gains
    work, mid = s.work, s.mid
    swap_out, swap_in = s.swap_out, s.swap_in

    d, f = lax.axis_index(DP), lax.axis_index(TP)
    o, i = d // 2, d % 2
    y, c = f // 2, f % 2
    place = d % span
    base = d - place
    f_sib, f_far, f_last = y * 2 + 1 - c, (1 - y) * 2 + c, (1 - y) * 2 + 1 - c
    mate = at(o * 2 + 1 - i, f)
    sib = at(d, f_sib)
    far = at(d, f_far)

    def rcopy(src, dst, ssem, rsem, dev):
        return pltpu.make_async_remote_copy(
            src_ref=src, dst_ref=dst, send_sem=ssem, recv_sem=rsem, device_id=dev, device_id_type=MESH
        )

    bar = pltpu.get_barrier_semaphore()

    def greet(q):
        dev = at((d + q) % nd, f)
        pl.semaphore_signal(bar, inc=1, device_id=dev, device_id_type=MESH)

    each(1, nd, greet)
    for q in range(1, nf):
        dev = at(d, (f + q) % nf)
        pl.semaphore_signal(bar, inc=1, device_id=dev, device_id_type=MESH)
    pl.semaphore_wait(bar, nd - 1 + nf - 1)

    def tell(n, src_of, dst, axis):
        count, me = (nd, d) if axis == DP else (nf, f)

        def go(q):
            to = (me + q) % count
            dev = at(to, f) if axis == DP else at(d, to)
            rcopy(src_of(to), dst.at[me], s.small_s.at[n], s.small_r.at[n], dev).start()

        each(1, count, go)

    def hear(n, dst, axis):
        count = nd if axis == DP else nf
        others = dst.at[pl.ds(0, count - 1)]
        cp = rcopy(others, others, s.small_s.at[n], s.small_r.at[n], mate)
        cp.wait_recv()
        cp.wait_send()

    def total_of(ref, count):
        total = ref[0]
        if count <= 8:
            for k in range(1, count):
                total = total + ref[k]
            return total
        return lax.fori_loop(1, count, lambda k, t: t + ref[k], total)

    tell(0, lambda to: vec, s.tiles, DP)

    def shard_rows(owner):
        return pl.ds(pl.multiple_of(owner * part, part), part)

    def gather_start(g):
        mine = weights.at[g, :, shard_rows(d), :]
        pltpu.make_async_copy(shard.at[g], mine, s.copy_w.at[g]).start()

        def go(q):
            dev = at(((o + q) % outer) * 2 + i, f)
            rcopy(shard.at[g], mine, s.line_ws.at[g], s.line_wr.at[g, q], dev).start()

        each(1, outer, go)
        rcopy(shard.at[g], mine, s.pair_ws.at[g], s.pair_wr.at[g], mate).start()

    def gather_pass(g):
        def go(q):
            block = weights.at[g, :, shard_rows(((o + outer - q) % outer) * 2 + i), :]
            rcopy(block, block, s.line_ws.at[g], s.line_wr.at[g, q], mate).wait_recv()
            rcopy(block, block, s.pair_ws.at[g], s.pair_wr.at[g], mate).start()

        each(1, outer, go)

    def gather_ready(g):
        mine = weights.at[g, :, shard_rows(d), :]
        pltpu.make_async_copy(shard.at[g], mine, s.copy_w.at[g]).wait()
        half = weights.at[g, :, pl.ds(0, outer * part), :]
        rcopy(half, half, s.pair_ws.at[g], s.pair_wr.at[g], mate).wait_recv()

    def gather_end(g):
        half = weights.at[g, :, pl.ds(0, outer * part), :]
        rcopy(half, half, s.pair_ws.at[g], s.pair_wr.at[g], mate).wait_send()
        rest = weights.at[g, :, pl.ds(0, (outer - 1) * part), :]
        rcopy(rest, rest, s.line_ws.at[g], s.line_wr.at[g, 0], mate).wait_send()

    def spread_start(k):
        block = gathered.at[k, f]
        rcopy(block, block, s.row_s.at[k, 1], s.row_r.at[k, 1], far).start()
        rcopy(block, block, s.row_s.at[k, 0], s.row_r.at[k, 0], sib).start()

    def spread_near(k):
        block = gathered.at[k, f_sib]
        rcopy(block, block, s.row_s.at[k, 0], s.row_r.at[k, 0], sib).wait_recv()

    def spread_pass(k):
        block = gathered.at[k, f_far]
        rcopy(block, block, s.row_s.at[k, 1], s.row_r.at[k, 1], far).wait_recv()
        rcopy(block, block, s.row_s.at[k, 2], s.row_r.at[k, 2], sib).start()

    def spread_far(k):
        block = gathered.at[k, f_last]
        rcopy(block, block, s.row_s.at[k, 2], s.row_r.at[k, 2], sib).wait_recv()

    def spread_end(k):
        block = gathered.at[k, f]
        for n in range(3):
            rcopy(block, block, s.row_s.at[k, n], s.row_r.at[k, n], sib).wait_send()

    def collect_start(k, terms):
        par = k % 2
        for slot in range(2):
            pair = (1 - y) if slot == 0 else y

            def tile(t, slot=slot, pair=pair):
                cols = pl.ds(pl.multiple_of(t * hidden, hidden), hidden)
                total = None
                for b_ref, g, j in terms:
                    value = nt(
                        b_ref[pl.ds(pair * 2, 2)].reshape(2 * rows, hidden), weights[g, j, cols, :]
                    )
                    total = value if total is None else total + value
                s.part_sum[slot, :, :, cols] = total.reshape(2, rows, hidden)

            loop(0, width // hidden, tile)
            s.sib_out[par, slot] = s.part_sum[slot, 1 - c].astype(B16)
            rcopy(
                s.sib_out.at[par, slot],
                s.sib_in.at[par, slot],
                s.sum_s.at[k, slot],
                s.sum_r.at[k, slot],
                sib,
            ).start()
        back = s.sib_in.at[par, 0]
        rcopy(back, back, s.sum_s.at[k, 0], s.sum_r.at[k, 0], sib).wait_recv()
        s.far_out[par] = (s.part_sum[0, c] + s.sib_in[par, 0].astype(F32)).astype(B16)
        rcopy(
            s.far_out.at[par], s.far_in.at[par], s.sum_s.at[k, 2], s.sum_r.at[k, 2], far
        ).start()

    def collect_end(k):
        par = k % 2
        near, away = s.sib_in.at[par, 1], s.far_in.at[par]
        rcopy(near, near, s.sum_s.at[k, 1], s.sum_r.at[k, 1], sib).wait_recv()
        rcopy(away, away, s.sum_s.at[k, 2], s.sum_r.at[k, 2], far).wait_recv()
        for n in range(3):
            rcopy(near, near, s.sum_s.at[k, n], s.sum_r.at[k, n], sib).wait_send()

        def get(block):
            return (
                s.part_sum[1, c, block]
                + s.sib_in[par, 1, block].astype(F32)
                + s.far_in[par, block].astype(F32)
            )

        return get

    def swap_start(k):
        def go(q):
            to = (place + q) % span
            rcopy(
                swap_out.at[k, to],
                swap_in.at[k, place],
                s.swap_s.at[k],
                s.swap_r.at[k],
                at(base + to, f),
            ).start()

        each(1, span, go)
        swap_in[k, place] = swap_out[k, place]

    def swap_wait(k):
        others = swap_in.at[k, pl.ds(0, span - 1)]
        rcopy(others, others, s.swap_s.at[k], s.swap_r.at[k], mate).wait_recv()

    def swap_end(k):
        others = swap_in.at[k, pl.ds(0, span - 1)]
        rcopy(others, others, s.swap_s.at[k], s.swap_r.at[k], mate).wait_send()

    def token_rows(fr, j):
        return pl.ds(pl.multiple_of(fr * here + j * piece, piece), piece)

    def pack(k, src):
        def step(j):
            parts = [src[token_rows(fr, j), :] for fr in range(frames)]
            swap_out[k, j] = jnp.concatenate(parts, axis=0).astype(B16)

        loop(0, span, step)

    def unpack(k, dst):
        def step(j):
            value = swap_in[k, j].astype(F32)
            for fr in range(frames):
                dst[token_rows(fr, j), :] = value[fr * piece : (fr + 1) * piece]

        loop(0, span, step)

    def chunks(step):
        loop(0, rows // CHUNK, lambda k: step(pl.ds(pl.multiple_of(k * CHUNK, CHUNK), CHUNK), k))

    def norm_rows(n, value, block):
        centered = value - jnp.mean(value, axis=-1, keepdims=True)
        rstd = lax.rsqrt(jnp.mean(centered * centered, axis=-1, keepdims=True) + EPS_NORM)
        hat = centered * rstd
        s.hats[n, block] = hat
        s.rstds[n, block] = jnp.broadcast_to(rstd, (CHUNK, LANES))
        return (hat * gains[n : n + 1, :]).astype(B16)

    def norm_back(n, grad, block):
        hat = s.hats[n, block]
        rstd = s.rstds[n, block][:, 0:1]
        grad_hat = grad * gains[n : n + 1, :]
        first = jnp.mean(grad_hat, axis=-1, keepdims=True)
        second = jnp.mean(grad_hat * hat, axis=-1, keepdims=True)
        s.vec_acc[n : n + 1, :] += jnp.sum(grad * hat, axis=0, keepdims=True)
        return rstd * (grad_hat - first - hat * second)

    def pair_rows(k, pair):
        return gathered[k, pl.ds(pair * 2, 2)].reshape(2 * rows, width)

    def as_flat(value):
        return value.reshape(2, frames, here, hidden)

    def project(k, g, dst, pair):
        def step(j):
            dst[j, pl.ds(pair * 2, 2)] = as_flat(nn(pair_rows(k, pair), weights[g, j]).astype(B16))

        loop(0, 3, step)

    def attend(block):
        spatial = block == 0
        n = nf * here if spatial else rows

        def load(ref, g, lanes):
            value = ref[:, g, :, lanes] if spatial else ref[g, :, :, lanes]
            return value.reshape(n, 2 * HDIM)

        def store(ref, g, lanes, value):
            if spatial:
                ref[:, g, :, lanes] = value.reshape(nf, here, 2 * HDIM)
            else:
                ref[g, :, :, lanes] = value.reshape(frames, here, 2 * HDIM)

        return n, load, store, (s.probs_a if spatial else s.probs_b)

    def head_lanes(n):
        return lax.broadcasted_iota(jnp.int32, (n, 2 * HDIM), 1) < HDIM

    def kept(n):
        query = lax.broadcasted_iota(jnp.int32, (n, n), 0)
        key = lax.broadcasted_iota(jnp.int32, (n, n), 1)
        return (query % piece == key % piece) & (key // piece <= query // piece)

    def each_pair(block, step):
        def go(k):
            lanes = pl.ds(pl.multiple_of((k % n_pairs) * 2 * HDIM, 2 * HDIM), 2 * HDIM)
            step(k, k // n_pairs, lanes)

        loop(0, (frames if block == 0 else nf) * n_pairs, go)

    def attention(block):
        n, load, store, probs = attend(block)
        qkv = s.qkv.at[block]

        def step(k, g, lanes):
            query, key, value = (load(qkv.at[j], g, lanes) for j in range(3))
            low = head_lanes(n)
            found = []
            for h in range(2):
                mine = jnp.where(low if h == 0 else ~low, query, jnp.zeros_like(query))
                scores = nt(mine, key) * scale
                if block == 1:
                    scores = jnp.where(kept(n), scores, NEG_FILL)
                expd = jnp.exp(scores - jnp.max(scores, axis=-1, keepdims=True))
                prob = expd / jnp.sum(expd, axis=-1, keepdims=True)
                probs[k * 2 + h] = prob
                found.append(nn(prob.astype(B16), value))
            store(s.mixed.at[block], g, lanes, jnp.where(low, found[0], found[1]).astype(B16))

        each_pair(block, step)

    def attention_back(block):
        n, load, store, probs = attend(block)
        qkv = s.qkv.at[block]

        def step(k, g, lanes):
            query, key, value = (load(qkv.at[j], g, lanes) for j in range(3))
            grad = load(s.grad_mixed, g, lanes)
            low = head_lanes(n)
            found = []
            for h in range(2):
                mine = jnp.where(low if h == 0 else ~low, grad, jnp.zeros_like(grad))
                prob = probs[k * 2 + h]
                grad_prob = nt(mine, value)
                inner = jnp.sum(prob * grad_prob, axis=-1, keepdims=True)
                grad_score = (prob * (grad_prob - inner)).astype(B16)
                found.append(
                    (
                        nn(grad_score, key) * scale,
                        tn(grad_score, query) * scale,
                        tn(prob.astype(B16), grad),
                    )
                )
            for j in range(3):
                both = jnp.where(low, found[0][j], found[1][j]).astype(B16)
                store(s.grad_qkv.at[j], g, lanes, both)

        each_pair(block, step)

    def mixed_back(k, g):
        def half(pair):
            value = nn(pair_rows(k, pair), weights[g, 3])
            s.grad_mixed[pl.ds(pair * 2, 2)] = as_flat(value.astype(B16))

        spread_near(k)
        half(y)
        spread_pass(k)
        spread_far(k)
        half(1 - y)

    def slot_grad(slot, k, b_ref):
        value = tn(gathered[k].reshape(nf * rows, width), b_ref[...].reshape(nf * rows, hidden))
        s.product[...] = value.reshape(outer, 2, part, hidden)
        s.pair_out[slot] = s.product[:, 1 - i].astype(B16)
        rcopy(
            s.pair_out.at[slot],
            s.pair_in.at[slot],
            s.pair_gs.at[slot],
            s.pair_gr.at[slot],
            mate,
        ).start()
        s.own_sum[slot] = s.product[:, i].astype(B16)

    def slot_pass(slot):
        block = s.pair_in.at[slot]
        cp = rcopy(block, block, s.pair_gs.at[slot], s.pair_gr.at[slot], mate)
        cp.wait_recv()
        cp.wait_send()

        def both(owner):
            return s.own_sum[slot, owner].astype(F32) + s.pair_in[slot, owner].astype(F32)

        def go(q):
            to = (o + q) % outer
            s.pair_out[slot, q] = both(to).astype(B16)
            rcopy(
                s.pair_out.at[slot, q],
                s.line_in.at[slot, q],
                s.line_gs.at[slot],
                s.line_gr.at[slot],
                at(to * 2 + i, f),
            ).start()

        each(1, outer, go)
        gout[slot] = both(o)

    def slot_end(slot):
        block = s.line_in.at[slot, pl.ds(1, outer - 1)]
        cp = rcopy(block, block, s.line_gs.at[slot], s.line_gr.at[slot], mate)
        cp.wait_recv()
        cp.wait_send()
        total = gout[slot]
        if outer <= 8:
            for q in range(1, outer):
                total = total + s.line_in[slot, q].astype(F32)
        else:
            total = lax.fori_loop(
                1, outer, lambda q, t: t + s.line_in[slot, q].astype(F32), total
            )
        gout[slot] = total
        folded = jnp.sum((total * total).reshape(part // 8, 8, hidden), axis=0)
        for k in range(hidden // LANES):
            s.sq_mine[0] += folded[:, k * LANES : (k + 1) * LANES]

    gather_start(0)
    hear(0, s.tiles, DP)
    s.tiles[d] = vec[...]
    per_tile = LANES // part
    for k in range(width // LANES):
        gains[:, k * LANES : (k + 1) * LANES] = total_of(
            s.tiles.at[pl.ds(k * per_tile, per_tile)], per_tile
        )
    s.vec_acc[...] = jnp.zeros_like(s.vec_acc)
    s.sq_mine[...] = jnp.zeros_like(s.sq_mine)

    def masked_rows(block):
        return jnp.broadcast_to(msk[block, :], (CHUNK, width)) > 0.5

    def first_norm(block, k):
        value = jnp.where(masked_rows(block), gains[3:4, :], tok[block, :].astype(F32))
        work[block, :] = value
        gathered[0, f, block] = norm_rows(0, value, block)

    chunks(first_norm)
    spread_start(0)
    pack(0, work)
    swap_start(0)
    gather_start(1)

    def widen(block, k):
        work[block, :] = cot[block, :].astype(F32)

    chunks(widen)
    pack(1, work)
    swap_start(1)

    spread_near(0)
    spread_pass(0)
    gather_pass(0)
    gather_start(2)
    gather_ready(0)
    project(0, 0, s.qkv.at[0], y)
    spread_far(0)
    project(0, 0, s.qkv.at[0], 1 - y)
    attention(0)
    collect_start(0, [(s.mixed.at[0], 0, 3)])
    swap_wait(1)
    gathered[1, f] = swap_in[1].reshape(rows, width)
    spread_start(1)
    gather_pass(1)
    gather_start(3)
    get = collect_end(0)

    def take_branch(block, k):
        work[block, :] = get(block)

    chunks(take_branch)
    pack(2, work)
    swap_start(2)

    swap_wait(0)
    swap_wait(2)

    def second_norm(block, k):
        value = swap_in[0, k].astype(F32) + swap_in[2, k].astype(F32)
        mid[block, :] = value
        gathered[2, f, block] = norm_rows(1, value, block)

    chunks(second_norm)
    spread_start(2)
    gather_ready(1)
    spread_near(2)
    project(2, 1, s.qkv.at[1], y)
    spread_pass(2)
    spread_far(2)
    project(2, 1, s.qkv.at[1], 1 - y)
    attention(1)
    collect_start(1, [(s.mixed.at[1], 1, 3)])
    gather_pass(2)
    spread_near(1)
    spread_pass(1)
    get = collect_end(1)

    def third_norm(block, k):
        value = mid[block, :] + get(block)
        mid[block, :] = value
        gathered[3, f, block] = norm_rows(2, value, block)

    chunks(third_norm)
    spread_start(3)

    gather_pass(3)
    gather_ready(2)
    gather_ready(3)

    def up(pair):
        def step(n):
            u = nn(pair_rows(3, pair), weights[2 + n // 2, n % 2])
            t = jnp.tanh(GELU_A * (u + GELU_B * u * u * u))
            half = 0.5 * (1.0 + t)
            s.act[n, pl.ds(pair * 2, 2)] = as_flat((u * half).astype(B16))
            bend = GELU_A * (1.0 + 3.0 * GELU_B * u * u)
            s.slope[n, pl.ds(pair * 2, 2)] = as_flat(half + 0.5 * u * (1.0 - t * t) * bend)

        loop(0, 4, step)

    spread_near(3)
    up(y)
    spread_pass(3)
    spread_far(3)
    up(1 - y)
    collect_start(2, [(s.act.at[n], 2 + n // 2, 2 + n % 2) for n in range(4)])

    spread_far(1)

    def down(pair):
        def step(n):
            grad = nn(pair_rows(1, pair), weights[2 + n // 2, 2 + n % 2])
            slope = s.slope[n, pl.ds(pair * 2, 2)].reshape(2 * rows, hidden)
            s.grad_pre[n, pl.ds(pair * 2, 2)] = as_flat((grad * slope).astype(B16))

        loop(0, 4, step)

    down(y)
    down(1 - y)
    get = collect_end(2)

    def take_output(block, k):
        swap_out[3, k] = (mid[block, :] + get(block)).astype(B16)

    chunks(take_output)
    swap_start(3)
    collect_start(3, [(s.grad_pre.at[n], 2 + n // 2, n % 2) for n in range(4)])

    def grad_up(n):
        slot_grad(8 + 4 * (n // 2) + n % 2, 3, s.grad_pre.at[n])

    def grad_down(n):
        slot_grad(10 + 4 * (n // 2) + n % 2, 1, s.act.at[n])

    loop(0, 2, grad_up)
    loop(0, 2, grad_down)
    get = collect_end(3)

    def third_back(block, k):
        value = swap_in[1, k].astype(F32) + norm_back(2, get(block), block)
        mid[block, :] = value
        gathered[4, f, block] = value.astype(B16)

    chunks(third_back)
    spread_start(4)
    loop(2, 4, grad_up)
    loop(2, 4, grad_down)

    mixed_back(4, 1)
    loop(8, 10, slot_pass)
    attention_back(1)
    collect_start(4, [(s.grad_qkv.at[j], 1, j) for j in range(3)])
    loop(0, 3, lambda j: slot_grad(4 + j, 2, s.grad_qkv.at[j]))
    slot_grad(7, 4, s.mixed.at[1])
    loop(10, 12, slot_pass)
    get = collect_end(4)

    def second_back(block, k):
        swap_out[4, k] = (mid[block, :] + norm_back(1, get(block), block)).astype(B16)

    chunks(second_back)
    swap_start(4)
    loop(12, 14, slot_pass)

    swap_wait(4)
    unpack(4, work)

    def take_carry(block, k):
        gathered[5, f, block] = work[block, :].astype(B16)

    chunks(take_carry)
    spread_start(5)
    loop(14, 16, slot_pass)
    mixed_back(5, 0)
    attention_back(0)
    collect_start(5, [(s.grad_qkv.at[j], 0, j) for j in range(3)])
    loop(0, 3, lambda j: slot_grad(j, 0, s.grad_qkv.at[j]))
    slot_grad(3, 5, s.mixed.at[0])
    loop(4, 8, slot_pass)
    get = collect_end(5)

    def first_back(block, k):
        value = work[block, :] + norm_back(0, get(block), block)
        masked = masked_rows(block)
        tgr[block, :] = jnp.where(masked, 0.0, value).astype(B16)
        s.vec_acc[3:4, :] += jnp.sum(jnp.where(masked, value, 0.0), axis=0, keepdims=True)

    chunks(first_back)

    for k in range(width // LANES):
        s.vec_out[k] = s.vec_acc[:, k * LANES : (k + 1) * LANES]
    tell(1, lambda to: s.vec_out.at[(to * part) // LANES], s.vec_in, DP)
    s.vec_in[d] = s.vec_out[(d * part) // LANES]
    swap_wait(3)
    unpack(3, mid)

    def give_output(block, k):
        out[block, :] = mid[block, :].astype(B16)

    chunks(give_output)
    loop(8, 16, slot_end)
    hear(1, s.vec_in, DP)
    s.vec_mine[...] = total_of(s.vec_in, nd)
    tell(2, lambda to: s.vec_mine, s.vec_side, TP)
    s.vec_side[f] = s.vec_mine[...]
    loop(0, 4, slot_pass)
    hear(2, s.vec_side, TP)
    grad_vec = total_of(s.vec_side, nf)
    gvec[...] = grad_vec
    loop(4, 8, slot_end)
    loop(0, 4, slot_end)

    lane = lax.broadcasted_iota(jnp.int32, (8, LANES), 1)
    first_lane = (d * part) % LANES
    owned = (lane >= first_lane) & (lane < first_lane + part)
    s.sq_mine[0] += jnp.where(owned, grad_vec * grad_vec, 0.0) * (1.0 / nf)
    tell(3, lambda to: s.sq_mine.at[0], s.sq_side, TP)
    s.sq_side[f] = s.sq_mine[0]
    hear(3, s.sq_side, TP)
    s.sq_mine[1] = total_of(s.sq_side, nf)
    tell(4, lambda to: s.sq_mine.at[1], s.sq_all, DP)
    s.sq_all[d] = s.sq_mine[1]
    for g in range(4):
        gather_end(g)
    for k in range(6):
        spread_end(k)
    for k in range(5):
        swap_end(k)
    hear(4, s.sq_all, DP)
    total = jnp.sum(total_of(s.sq_all, nd), keepdims=True)
    nrm[...] = jnp.broadcast_to(jnp.sqrt(total), (8, LANES))


def adamw_step(weight, first, second, grad, rate):
    first = BETA_FIRST * first + (1.0 - BETA_FIRST) * grad
    second = BETA_SECOND * second + (1.0 - BETA_SECOND) * grad * grad
    fix_first = 1.0 - BETA_FIRST**STEP
    fix_second = 1.0 - BETA_SECOND**STEP
    update = first / fix_first / (jnp.sqrt(second / fix_second) + ADAM_EPS)
    return (weight - rate * (update + DECAY_RATE * weight), first, second)


def local(tokens, masks, cotangent, w_in, w_out, vectors, m_in, m_out, m_vec, v_in, v_out, v_vec):
    frames, here, width = tokens.shape
    part, _, hidden = w_in.shape
    nd, nf = lax.axis_size(DP), lax.axis_size(TP)
    z = SimpleNamespace(
        rows=frames * here,
        width=width,
        hidden=hidden,
        span=FRAMES // frames,
        nd=nd,
        nf=nf,
        part=part,
        heads=hidden // HDIM,
        frames=frames,
        here=here,
    )
    rows = frames * here
    lane0 = (lax.axis_index(DP) * part) % LANES

    into = w_in.transpose(1, 0, 2).astype(B16)
    outof = w_out.transpose(0, 2, 1).astype(B16)
    shard = jnp.concatenate(
        [into[0:3], outof[0:1], into[3:6], outof[1:2], into[6:8], outof[2:4], into[8:10], outof[4:6]]
    ).reshape(4, 4, part, hidden)
    vec = lax.dynamic_update_slice(
        jnp.zeros((8, LANES), F32), vectors.astype(B16).astype(F32), (0, lane0)
    )
    scratch = scratch_of(z)
    in_vmem = pl.BlockSpec(memory_space=pltpu.VMEM)
    output, token_grad, norm, grads, grad_vec = pl.pallas_call(
        functools.partial(layer, z, list(scratch)),
        out_shape=(
            jax.ShapeDtypeStruct((rows, width), B16),
            jax.ShapeDtypeStruct((rows, width), B16),
            jax.ShapeDtypeStruct((8, LANES), F32),
            jax.ShapeDtypeStruct((16, part, hidden), F32),
            jax.ShapeDtypeStruct((8, LANES), F32),
        ),
        in_specs=[in_vmem] * 5,
        out_specs=[in_vmem] * 5,
        scratch_shapes=list(scratch.values()),
        compiler_params=pltpu.CompilerParams(
            collective_id=0, has_side_effects=True, vmem_limit_bytes=VMEM_BYTES
        ),
    )(
        tokens.reshape(rows, width),
        masks.reshape(rows, 1).astype(F32),
        cotangent.reshape(rows, width),
        shard,
        vec,
    )
    grad_norm = norm[0, 0]
    factor = CLIP_AT / jnp.maximum(grad_norm, CLIP_AT)
    grad_in = jnp.concatenate([grads[0:3], grads[4:7], grads[8:10], grads[12:14]]).transpose(1, 0, 2)
    grad_out = jnp.concatenate([grads[3:4], grads[7:8], grads[10:12], grads[14:16]]).transpose(
        0, 2, 1
    )
    grad_vec = lax.dynamic_slice(grad_vec, (0, lane0), (4, part))
    new_w_in, new_m_in, new_v_in = adamw_step(w_in, m_in, v_in, grad_in * factor, RATE_INPUT)
    new_w_out, new_m_out, new_v_out = adamw_step(
        w_out, m_out, v_out, grad_out * factor, RATE_OUTPUT
    )
    new_vectors, new_m_vec, new_v_vec = adamw_step(
        vectors, m_vec, v_vec, grad_vec * factor, RATE_VECTOR
    )
    return (
        output.reshape(frames, here, width),
        token_grad.reshape(frames, here, width),
        grad_norm,
        new_w_in,
        new_w_out,
        new_vectors,
        new_m_in,
        new_m_out,
        new_m_vec,
        new_v_in,
        new_v_out,
        new_v_vec,
    )


def solution(mesh):
    in_specs = (
        P(DP, TP, None),
        P(DP, TP),
        P(DP, TP, None),
        P(DP, None, TP),
        P(None, TP, DP),
        P(None, DP),
        P(DP, None, TP),
        P(None, TP, DP),
        P(None, DP),
        P(DP, None, TP),
        P(None, TP, DP),
        P(None, DP),
    )
    out_specs = (P(DP, TP, None), P(DP, TP, None), P()) + in_specs[3:]
    return jax.shard_map(local, mesh=mesh, in_specs=in_specs, out_specs=out_specs, check_vma=False)
```

```python
import functools
from types import SimpleNamespace

import jax
import jax.numpy as jnp
from jax import lax
from jax.experimental import pallas as pl
from jax.experimental.pallas import tpu as pltpu
from jax.sharding import PartitionSpec as P

FRAMES = 16
STEP = 10
HDIM = 64


EPS_NORM = 1e-05
CLIP_AT = 1.0
BETA_FIRST = 0.9
BETA_SECOND = 0.95
ADAM_EPS = 1e-08
DECAY_RATE = 0.1
RATE_INPUT = 0.02
RATE_OUTPUT = 0.08
RATE_VECTOR = 1.0
NEG_FILL = -1e30
GELU_A = 0.7978845608028654
GELU_B = 0.044715

F32 = jnp.float32
B16 = jnp.bfloat16
MESH = pl.DeviceIdType.MESH
CHUNK = 16
DP = "dp"
TP = "fsdp"
LANES = 128
VMEM_BYTES = 63 << 20


def at(dp, fsdp):
    return {DP: dp, TP: fsdp}


def nn(a, b):
    return lax.dot_general(a, b, (((1,), (0,)), ((), ())), preferred_element_type=F32)


def nt(a, b):
    return lax.dot_general(a, b, (((1,), (1,)), ((), ())), preferred_element_type=F32)


def tn(a, b):
    return lax.dot_general(a, b, (((0,), (0,)), ((), ())), preferred_element_type=F32)


def loop(low, high, step):
    def body(k, carry):
        step(k)
        return carry

    lax.fori_loop(low, high, body, 0)


def each(low, high, step):
    if high - low <= 8:
        for k in range(low, high):
            step(k)
    else:
        loop(low, high, step)


def scratch_of(z):
    rows, width, hidden, span = z.rows, z.width, z.hidden, z.span
    nd, nf, part, heads = z.nd, z.nf, z.part, z.heads
    outer = nd // 2
    flat = (nf, z.frames, z.here, hidden)
    vmem = pltpu.VMEM
    dma = pltpu.SemaphoreType.DMA
    return dict(
        stage_in=vmem((10, part, hidden), F32),
        stage_out=vmem((6, hidden, part), F32),
        shard=vmem((4, 4, part, hidden), B16),
        tile=vmem((8, LANES), F32),
        weights=vmem((4, 4, width, hidden), B16),
        gathered=vmem((6, nf, rows, width), B16),
        gains=vmem((8, width), F32),
        tiles=vmem((nd, 8, LANES), F32),
        hats=vmem((3, rows, width), F32),
        rstds=vmem((3, rows, LANES), F32),
        work=vmem((rows, width), F32),
        mid=vmem((rows, width), F32),
        swap_out=vmem((4, span, CHUNK, width), B16),
        swap_in=vmem((4, span, CHUNK, width), B16),
        part_sum=vmem((2, 2, rows, width), F32),
        sib_out=vmem((2, 2, rows, width), B16),
        sib_in=vmem((2, 2, rows, width), B16),
        far_out=vmem((2, rows, width), B16),
        far_in=vmem((2, rows, width), B16),
        qkv=vmem((2, 3) + flat, B16),
        mixed=vmem((2,) + flat, B16),
        grad_mixed=vmem(flat, B16),
        grad_qkv=vmem((3,) + flat, B16),
        probs_a=vmem((z.frames * heads, nf * z.here, nf * z.here), F32),
        probs_b=vmem((nf * heads, rows, rows), F32),
        act=vmem((4,) + flat, B16),
        slope=vmem((4,) + flat, F32),
        grad_pre=vmem((4,) + flat, B16),
        product=vmem((outer, 2, part, hidden), F32),
        own_sum=vmem((16, outer, part, hidden), B16),
        pair_out=vmem((16, outer, part, hidden), B16),
        pair_in=vmem((16, outer, part, hidden), B16),
        line_in=vmem((16, outer, part, hidden), B16),
        vec_acc=vmem((8, width), F32),
        vec_out=vmem((width // LANES, 8, LANES), F32),
        vec_in=vmem((nd, 8, LANES), F32),
        vec_mine=vmem((8, LANES), F32),
        vec_side=vmem((nf, 8, LANES), F32),
        sq_mine=vmem((2, 8, LANES), F32),
        sq_side=vmem((nf, 8, LANES), F32),
        sq_all=vmem((nd, 8, LANES), F32),
        small_s=dma((5,)),
        small_r=dma((5,)),
        line_ws=dma((4,)),
        line_wr=dma((4, outer)),
        pair_ws=dma((4,)),
        pair_wr=dma((4,)),
        copy_w=dma((4,)),
        row_s=dma((6, 3)),
        row_r=dma((6, 3)),
        sum_s=dma((6, 3)),
        sum_r=dma((6, 3)),
        swap_s=dma((4,)),
        swap_r=dma((4,)),
        stage_s=dma((16,)),
        pair_gs=dma((16,)),
        pair_gr=dma((16,)),
        line_gs=dma((16,)),
        line_gr=dma((16,)),
    )


def layer(z, names, *refs):
    tok, msk, cot, w_in, w_out, vec = refs[:6]
    out, tgr, nrm, gout, gvec = refs[6:11]
    s = SimpleNamespace(**dict(zip(names, refs[11:])))
    rows, width, hidden, span = z.rows, z.width, z.hidden, z.span
    nd, nf, part, heads = z.nd, z.nf, z.part, z.heads
    frames, here = z.frames, z.here
    outer = nd // 2
    piece = here // span
    n_pairs = heads // 2
    scale = HDIM**-0.5
    gathered, weights, gains = s.gathered, s.weights, s.gains
    work, mid, shard = s.work, s.mid, s.shard
    swap_out, swap_in = s.swap_out, s.swap_in

    d, f = lax.axis_index(DP), lax.axis_index(TP)
    o, i = d // 2, d % 2
    y, c = f // 2, f % 2
    place = d % span
    base = d - place
    f_sib, f_far, f_last = y * 2 + 1 - c, (1 - y) * 2 + c, (1 - y) * 2 + 1 - c
    mate = at(o * 2 + 1 - i, f)
    sib = at(d, f_sib)
    far = at(d, f_far)

    def rcopy(src, dst, ssem, rsem, dev):
        return pltpu.make_async_remote_copy(
            src_ref=src, dst_ref=dst, send_sem=ssem, recv_sem=rsem, device_id=dev, device_id_type=MESH
        )

    in_slots = {0: [0, 1, 2], 1: [3, 4, 5], 2: [6, 7, 8, 9], 3: []}
    out_slots = {0: [0], 1: [1], 2: [], 3: [2, 3, 4, 5]}

    def stage(g):
        for n in in_slots[g]:
            yield pltpu.make_async_copy(w_in.at[n], s.stage_in.at[n], s.stage_s.at[n])
        for n in out_slots[g]:
            yield pltpu.make_async_copy(w_out.at[n], s.stage_out.at[n], s.stage_s.at[10 + n])

    def round_group(g):
        for cp in stage(g):
            cp.wait()
        for j, n in enumerate(in_slots[g]):
            shard[g, j] = s.stage_in[n].astype(B16)
        for j, n in enumerate(out_slots[g]):
            shard[g, len(in_slots[g]) + j] = s.stage_out[n].T.astype(B16)

    for g in range(4):
        for cp in stage(g):
            cp.start()
    s.tile[...] = jnp.zeros_like(s.tile)
    s.tile[0:4, :] = vec[...].astype(B16).astype(F32)

    bar = pltpu.get_barrier_semaphore()

    def greet(q):
        dev = at((d + q) % nd, f)
        pl.semaphore_signal(bar, inc=1, device_id=dev, device_id_type=MESH)

    each(1, nd, greet)
    for q in range(1, nf):
        dev = at(d, (f + q) % nf)
        pl.semaphore_signal(bar, inc=1, device_id=dev, device_id_type=MESH)
    pl.semaphore_wait(bar, nd - 1 + nf - 1)

    def tell(n, src_of, dst, axis):
        count, me = (nd, d) if axis == DP else (nf, f)

        def go(q):
            to = (me + q) % count
            dev = at(to, f) if axis == DP else at(d, to)
            rcopy(src_of(to), dst.at[me], s.small_s.at[n], s.small_r.at[n], dev).start()

        each(1, count, go)

    def hear(n, dst, axis):
        count = nd if axis == DP else nf
        others = dst.at[pl.ds(0, count - 1)]
        cp = rcopy(others, others, s.small_s.at[n], s.small_r.at[n], mate)
        cp.wait_recv()
        cp.wait_send()

    def total_of(ref, count):
        total = ref[0]
        if count <= 8:
            for k in range(1, count):
                total = total + ref[k]
            return total
        return lax.fori_loop(1, count, lambda k, t: t + ref[k], total)

    tell(0, lambda to: s.tile, s.tiles, DP)

    def shard_rows(owner):
        return pl.ds(pl.multiple_of(owner * part, part), part)

    def gather_own(g):
        mine = weights.at[g, :, shard_rows(d), :]
        pltpu.make_async_copy(shard.at[g], mine, s.copy_w.at[g]).start()
        rcopy(shard.at[g], mine, s.pair_ws.at[g], s.pair_wr.at[g], mate).start()

    def gather_line(g, low, high):
        mine = weights.at[g, :, shard_rows(d), :]

        def go(q):
            dev = at(((o + q) % outer) * 2 + i, f)
            rcopy(shard.at[g], mine, s.line_ws.at[g], s.line_wr.at[g, q], dev).start()

        each(low, high, go)

    def gather_pass(g, low, high):
        def go(q):
            block = weights.at[g, :, shard_rows(((o + outer - q) % outer) * 2 + i), :]
            rcopy(block, block, s.line_ws.at[g], s.line_wr.at[g, q], mate).wait_recv()
            rcopy(block, block, s.pair_ws.at[g], s.pair_wr.at[g], mate).start()

        each(low, high, go)

    def gather_ready(g):
        mine = weights.at[g, :, shard_rows(d), :]
        pltpu.make_async_copy(shard.at[g], mine, s.copy_w.at[g]).wait()
        half = weights.at[g, :, pl.ds(0, outer * part), :]
        rcopy(half, half, s.pair_ws.at[g], s.pair_wr.at[g], mate).wait_recv()

    def gather_end(g):
        half = weights.at[g, :, pl.ds(0, outer * part), :]
        rcopy(half, half, s.pair_ws.at[g], s.pair_wr.at[g], mate).wait_send()
        rest = weights.at[g, :, pl.ds(0, (outer - 1) * part), :]
        rcopy(rest, rest, s.line_ws.at[g], s.line_wr.at[g, 0], mate).wait_send()

    def spread_start(k):
        block = gathered.at[k, f]
        rcopy(block, block, s.row_s.at[k, 1], s.row_r.at[k, 1], far).start()
        rcopy(block, block, s.row_s.at[k, 0], s.row_r.at[k, 0], sib).start()

    def spread_near(k):
        block = gathered.at[k, f_sib]
        rcopy(block, block, s.row_s.at[k, 0], s.row_r.at[k, 0], sib).wait_recv()

    def spread_pass(k):
        block = gathered.at[k, f_far]
        rcopy(block, block, s.row_s.at[k, 1], s.row_r.at[k, 1], far).wait_recv()
        rcopy(block, block, s.row_s.at[k, 2], s.row_r.at[k, 2], sib).start()

    def spread_far(k):
        block = gathered.at[k, f_last]
        rcopy(block, block, s.row_s.at[k, 2], s.row_r.at[k, 2], sib).wait_recv()

    def spread_end(k):
        block = gathered.at[k, f]
        for n in range(3):
            rcopy(block, block, s.row_s.at[k, n], s.row_r.at[k, n], sib).wait_send()

    def collect_start(k, terms):
        par = k % 2
        for slot in range(2):
            pair = (1 - y) if slot == 0 else y

            def tile(t, slot=slot, pair=pair):
                cols = pl.ds(pl.multiple_of(t * hidden, hidden), hidden)
                total = None
                for b_ref, g, j in terms:
                    value = nt(
                        b_ref[pl.ds(pair * 2, 2)].reshape(2 * rows, hidden), weights[g, j, cols, :]
                    )
                    total = value if total is None else total + value
                s.part_sum[slot, :, :, cols] = total.reshape(2, rows, hidden)

            loop(0, width // hidden, tile)
            s.sib_out[par, slot] = s.part_sum[slot, 1 - c].astype(B16)
            rcopy(
                s.sib_out.at[par, slot],
                s.sib_in.at[par, slot],
                s.sum_s.at[k, slot],
                s.sum_r.at[k, slot],
                sib,
            ).start()
        back = s.sib_in.at[par, 0]
        rcopy(back, back, s.sum_s.at[k, 0], s.sum_r.at[k, 0], sib).wait_recv()
        s.far_out[par] = (s.part_sum[0, c] + s.sib_in[par, 0].astype(F32)).astype(B16)
        rcopy(
            s.far_out.at[par], s.far_in.at[par], s.sum_s.at[k, 2], s.sum_r.at[k, 2], far
        ).start()

    def collect_end(k):
        par = k % 2
        near, away = s.sib_in.at[par, 1], s.far_in.at[par]
        rcopy(near, near, s.sum_s.at[k, 1], s.sum_r.at[k, 1], sib).wait_recv()
        rcopy(away, away, s.sum_s.at[k, 2], s.sum_r.at[k, 2], far).wait_recv()
        for n in range(3):
            rcopy(near, near, s.sum_s.at[k, n], s.sum_r.at[k, n], sib).wait_send()

        def get(block):
            return (
                s.part_sum[1, c, block]
                + s.sib_in[par, 1, block].astype(F32)
                + s.far_in[par, block].astype(F32)
            )

        return get

    def swap_start(k):
        def go(q):
            to = (place + q) % span
            rcopy(
                swap_out.at[k, to],
                swap_in.at[k, place],
                s.swap_s.at[k],
                s.swap_r.at[k],
                at(base + to, f),
            ).start()

        each(1, span, go)
        swap_in[k, place] = swap_out[k, place]

    def swap_wait(k):
        others = swap_in.at[k, pl.ds(0, span - 1)]
        rcopy(others, others, s.swap_s.at[k], s.swap_r.at[k], mate).wait_recv()

    def swap_end(k):
        others = swap_in.at[k, pl.ds(0, span - 1)]
        rcopy(others, others, s.swap_s.at[k], s.swap_r.at[k], mate).wait_send()

    def token_rows(fr, j):
        return pl.ds(pl.multiple_of(fr * here + j * piece, piece), piece)

    def pack(k, src):
        def step(j):
            parts = [src[token_rows(fr, j), :] for fr in range(frames)]
            swap_out[k, j] = jnp.concatenate(parts, axis=0).astype(B16)

        loop(0, span, step)

    def unpack(k, dst):
        def step(j):
            value = swap_in[k, j].astype(F32)
            for fr in range(frames):
                dst[token_rows(fr, j), :] = value[fr * piece : (fr + 1) * piece]

        loop(0, span, step)

    def chunks(step):
        loop(0, rows // CHUNK, lambda k: step(pl.ds(pl.multiple_of(k * CHUNK, CHUNK), CHUNK), k))

    def norm_rows(n, value, block):
        centered = value - jnp.mean(value, axis=-1, keepdims=True)
        rstd = lax.rsqrt(jnp.mean(centered * centered, axis=-1, keepdims=True) + EPS_NORM)
        hat = centered * rstd
        s.hats[n, block] = hat
        s.rstds[n, block] = jnp.broadcast_to(rstd, (CHUNK, LANES))
        return (hat * gains[n : n + 1, :]).astype(B16)

    def norm_back(n, grad, block):
        hat = s.hats[n, block]
        rstd = s.rstds[n, block][:, 0:1]
        grad_hat = grad * gains[n : n + 1, :]
        first = jnp.mean(grad_hat, axis=-1, keepdims=True)
        second = jnp.mean(grad_hat * hat, axis=-1, keepdims=True)
        s.vec_acc[n : n + 1, :] += jnp.sum(grad * hat, axis=0, keepdims=True)
        return rstd * (grad_hat - first - hat * second)

    def pair_rows(k, pair):
        return gathered[k, pl.ds(pair * 2, 2)].reshape(2 * rows, width)

    def as_flat(value):
        return value.reshape(2, frames, here, hidden)

    def project(k, g, dst, pair):
        def step(j):
            dst[j, pl.ds(pair * 2, 2)] = as_flat(nn(pair_rows(k, pair), weights[g, j]).astype(B16))

        loop(0, 3, step)

    def attend(block):
        spatial = block == 0
        n = nf * here if spatial else rows

        def load(ref, g, lanes):
            value = ref[:, g, :, lanes] if spatial else ref[g, :, :, lanes]
            return value.reshape(n, 2 * HDIM)

        def store(ref, g, lanes, value):
            if spatial:
                ref[:, g, :, lanes] = value.reshape(nf, here, 2 * HDIM)
            else:
                ref[g, :, :, lanes] = value.reshape(frames, here, 2 * HDIM)

        return n, load, store, (s.probs_a if spatial else s.probs_b)

    def head_lanes(n):
        return lax.broadcasted_iota(jnp.int32, (n, 2 * HDIM), 1) < HDIM

    def kept(n):
        query = lax.broadcasted_iota(jnp.int32, (n, n), 0)
        key = lax.broadcasted_iota(jnp.int32, (n, n), 1)
        return (query % piece == key % piece) & (key // piece <= query // piece)

    def each_pair(block, step):
        def go(k):
            lanes = pl.ds(pl.multiple_of((k % n_pairs) * 2 * HDIM, 2 * HDIM), 2 * HDIM)
            step(k, k // n_pairs, lanes)

        loop(0, (frames if block == 0 else nf) * n_pairs, go)

    def attention(block):
        n, load, store, probs = attend(block)
        qkv = s.qkv.at[block]

        def step(k, g, lanes):
            query, key, value = (load(qkv.at[j], g, lanes) for j in range(3))
            low = head_lanes(n)
            found = []
            for h in range(2):
                mine = jnp.where(low if h == 0 else ~low, query, jnp.zeros_like(query))
                scores = nt(mine, key) * scale
                if block == 1:
                    scores = jnp.where(kept(n), scores, NEG_FILL)
                expd = jnp.exp(scores - jnp.max(scores, axis=-1, keepdims=True))
                prob = expd / jnp.sum(expd, axis=-1, keepdims=True)
                probs[k * 2 + h] = prob
                found.append(nn(prob.astype(B16), value))
            store(s.mixed.at[block], g, lanes, jnp.where(low, found[0], found[1]).astype(B16))

        each_pair(block, step)

    def attention_back(block):
        n, load, store, probs = attend(block)
        qkv = s.qkv.at[block]

        def step(k, g, lanes):
            query, key, value = (load(qkv.at[j], g, lanes) for j in range(3))
            grad = load(s.grad_mixed, g, lanes)
            low = head_lanes(n)
            found = []
            for h in range(2):
                mine = jnp.where(low if h == 0 else ~low, grad, jnp.zeros_like(grad))
                prob = probs[k * 2 + h]
                grad_prob = nt(mine, value)
                inner = jnp.sum(prob * grad_prob, axis=-1, keepdims=True)
                grad_score = (prob * (grad_prob - inner)).astype(B16)
                found.append(
                    (
                        nn(grad_score, key) * scale,
                        tn(grad_score, query) * scale,
                        tn(prob.astype(B16), grad),
                    )
                )
            for j in range(3):
                both = jnp.where(low, found[0][j], found[1][j]).astype(B16)
                store(s.grad_qkv.at[j], g, lanes, both)

        each_pair(block, step)

    def mixed_back(k, g):
        def half(pair):
            value = nn(pair_rows(k, pair), weights[g, 3])
            s.grad_mixed[pl.ds(pair * 2, 2)] = as_flat(value.astype(B16))

        spread_near(k)
        half(y)
        spread_pass(k)
        spread_far(k)
        half(1 - y)

    def slot_make(slot, k, b_ref):
        value = tn(gathered[k].reshape(nf * rows, width), b_ref[...].reshape(nf * rows, hidden))
        s.product[...] = value.reshape(outer, 2, part, hidden)
        s.pair_out[slot] = s.product[:, 1 - i].astype(B16)
        s.own_sum[slot] = s.product[:, i].astype(B16)

    def slot_send(slot):
        rcopy(
            s.pair_out.at[slot],
            s.pair_in.at[slot],
            s.pair_gs.at[slot],
            s.pair_gr.at[slot],
            mate,
        ).start()

    def slot_pass(slot):
        block = s.pair_in.at[slot]
        cp = rcopy(block, block, s.pair_gs.at[slot], s.pair_gr.at[slot], mate)
        cp.wait_recv()
        cp.wait_send()

        def both(owner):
            return s.own_sum[slot, owner].astype(F32) + s.pair_in[slot, owner].astype(F32)

        def go(q):
            to = (o + q) % outer
            s.pair_out[slot, q] = both(to).astype(B16)
            rcopy(
                s.pair_out.at[slot, q],
                s.line_in.at[slot, q],
                s.line_gs.at[slot],
                s.line_gr.at[slot],
                at(to * 2 + i, f),
            ).start()

        each(1, outer, go)
        gout[slot] = both(o)

    def slot_end(slot):
        block = s.line_in.at[slot, pl.ds(1, outer - 1)]
        cp = rcopy(block, block, s.line_gs.at[slot], s.line_gr.at[slot], mate)
        cp.wait_recv()
        cp.wait_send()
        total = gout[slot]
        if outer <= 8:
            for q in range(1, outer):
                total = total + s.line_in[slot, q].astype(F32)
        else:
            total = lax.fori_loop(
                1, outer, lambda q, t: t + s.line_in[slot, q].astype(F32), total
            )
        gout[slot] = total
        folded = jnp.sum((total * total).reshape(part // 8, 8, hidden), axis=0)
        for k in range(hidden // LANES):
            s.sq_mine[0] += folded[:, k * LANES : (k + 1) * LANES]

    round_group(0)
    gather_line(0, 1, outer)
    gather_own(0)
    hear(0, s.tiles, DP)
    s.tiles[d] = s.tile[...]
    per_tile = LANES // part
    for k in range(width // LANES):
        gains[:, k * LANES : (k + 1) * LANES] = total_of(
            s.tiles.at[pl.ds(k * per_tile, per_tile)], per_tile
        )
    s.vec_acc[...] = jnp.zeros_like(s.vec_acc)
    s.sq_mine[...] = jnp.zeros_like(s.sq_mine)

    def masked_rows(block):
        return jnp.broadcast_to(msk[block, :], (CHUNK, width)) > 0.5

    def first_norm(block, k):
        value = jnp.where(masked_rows(block), gains[3:4, :], tok[block, :].astype(F32))
        work[block, :] = value
        gathered[0, f, block] = norm_rows(0, value, block)

    chunks(first_norm)
    spread_start(0)
    round_group(1)
    gather_line(1, 1, outer)
    gather_pass(0, 1, 2)

    def widen(block, k):
        s.part_sum[0, 0, block, :] = cot[block, :].astype(F32)

    chunks(widen)
    pack(0, s.part_sum.at[0, 0])
    swap_start(0)

    gather_pass(0, 2, outer - 1)
    spread_near(0)
    spread_pass(0)
    gather_pass(0, outer - 1, outer)
    gather_own(1)
    round_group(2)
    gather_line(2, 1, 2)
    gather_ready(0)
    project(0, 0, s.qkv.at[0], y)
    spread_far(0)
    project(0, 0, s.qkv.at[0], 1 - y)
    gather_pass(1, 1, 2)
    attention(0)
    gather_pass(1, 2, outer - 1)
    collect_start(0, [(s.mixed.at[0], 0, 3)])
    gather_pass(1, outer - 1, outer)
    round_group(3)
    get = collect_end(0)

    def take_branch(block, k):
        work[block, :] = work[block, :] + get(block)

    chunks(take_branch)
    pack(1, work)
    swap_start(1)
    gather_line(2, 2, outer)
    gather_line(3, 1, outer)
    gather_own(2)

    swap_wait(0)
    gathered[1, f] = swap_in[0].reshape(rows, width)
    spread_start(1)
    gather_pass(2, 1, 2)
    gather_own(3)
    swap_wait(1)

    def second_norm(block, k):
        value = swap_in[1, k].astype(F32)
        mid[block, :] = value
        gathered[2, f, block] = norm_rows(1, value, block)

    chunks(second_norm)
    spread_start(2)
    spread_near(1)
    spread_pass(1)
    gather_ready(1)
    spread_near(2)
    project(2, 1, s.qkv.at[1], y)
    spread_pass(2)
    spread_far(2)
    project(2, 1, s.qkv.at[1], 1 - y)
    gather_pass(2, 2, outer - 1)
    attention(1)
    gather_pass(2, outer - 1, outer)
    collect_start(1, [(s.mixed.at[1], 1, 3)])
    gather_pass(3, 1, 2)
    get = collect_end(1)

    def third_norm(block, k):
        value = mid[block, :] + get(block)
        mid[block, :] = value
        gathered[3, f, block] = norm_rows(2, value, block)

    chunks(third_norm)
    spread_start(3)
    spread_far(1)
    gather_pass(3, 2, outer - 1)


    def up(pair):
        def step(n):
            u = nn(pair_rows(3, pair), weights[2, n])
            t = jnp.tanh(GELU_A * (u + GELU_B * u * u * u))
            half = 0.5 * (1.0 + t)
            s.act[n, pl.ds(pair * 2, 2)] = as_flat((u * half).astype(B16))
            bend = GELU_A * (1.0 + 3.0 * GELU_B * u * u)
            s.slope[n, pl.ds(pair * 2, 2)] = as_flat(half + 0.5 * u * (1.0 - t * t) * bend)

        loop(0, 4, step)

    def down(pair):
        def step(n):
            grad = nn(pair_rows(1, pair), weights[3, n])
            slope = s.slope[n, pl.ds(pair * 2, 2)].reshape(2 * rows, hidden)
            s.grad_pre[n, pl.ds(pair * 2, 2)] = as_flat((grad * slope).astype(B16))

        loop(0, 4, step)

    gather_ready(2)
    spread_near(3)
    up(y)
    spread_pass(3)
    gather_pass(3, outer - 1, outer)
    spread_far(3)
    up(1 - y)
    loop(0, 4, lambda n: slot_make(12 + n, 1, s.act.at[n]))
    slot_send(12)
    slot_send(13)
    gather_ready(3)

    down(1 - y)
    down(y)
    slot_make(8, 3, s.grad_pre.at[0])
    slot_send(8)
    collect_start(2, [(s.grad_pre.at[n], 2, n) for n in range(4)])
    slot_pass(12)
    loop(1, 4, lambda n: slot_make(8 + n, 3, s.grad_pre.at[n]))
    slot_send(9)
    slot_send(14)
    slot_pass(13)
    get = collect_end(2)

    def third_back(block, k):
        value = swap_in[0, k].astype(F32) + norm_back(2, get(block), block)
        work[block, :] = value
        gathered[4, f, block] = value.astype(B16)

    chunks(third_back)
    spread_start(4)
    slot_pass(8)
    slot_send(10)
    slot_send(15)
    collect_start(3, [(s.act.at[n], 3, n) for n in range(4)])
    slot_pass(9)

    mixed_back(4, 1)
    slot_make(7, 4, s.mixed.at[1])
    slot_pass(14)
    slot_send(11)
    slot_send(7)
    get_output = collect_end(3)

    def take_output(block, k):
        swap_out[2, k] = (mid[block, :] + get_output(block)).astype(B16)

    chunks(take_output)
    swap_start(2)
    attention_back(1)
    slot_pass(10)
    collect_start(4, [(s.grad_qkv.at[j], 1, j) for j in range(3)])
    slot_pass(15)
    loop(0, 3, lambda j: slot_make(4 + j, 2, s.grad_qkv.at[j]))
    slot_pass(11)
    get = collect_end(4)

    def second_back(block, k):
        swap_out[3, k] = (work[block, :] + norm_back(1, get(block), block)).astype(B16)

    chunks(second_back)
    swap_start(3)
    slot_send(4)
    slot_send(5)
    slot_send(6)

    swap_wait(3)
    unpack(3, work)

    def take_carry(block, k):
        gathered[5, f, block] = work[block, :].astype(B16)

    chunks(take_carry)
    spread_start(5)
    slot_pass(7)
    mixed_back(5, 0)
    slot_make(3, 5, s.mixed.at[0])
    slot_send(3)
    slot_pass(4)
    attention_back(0)

    def spatial_slot(j):
        slot_make(j, 0, s.grad_qkv.at[j])
        slot_send(j)

    loop(0, 3, spatial_slot)
    slot_pass(5)
    collect_start(5, [(s.grad_qkv.at[j], 0, j) for j in range(3)])
    slot_pass(6)
    slot_pass(3)
    get = collect_end(5)

    def first_back(block, k):
        value = work[block, :] + norm_back(0, get(block), block)
        masked = masked_rows(block)
        tgr[block, :] = jnp.where(masked, 0.0, value).astype(B16)
        s.vec_acc[3:4, :] += jnp.sum(jnp.where(masked, value, 0.0), axis=0, keepdims=True)

    chunks(first_back)

    for k in range(width // LANES):
        s.vec_out[k] = s.vec_acc[:, k * LANES : (k + 1) * LANES]
    tell(1, lambda to: s.vec_out.at[(to * part) // LANES], s.vec_in, DP)
    s.vec_in[d] = s.vec_out[(d * part) // LANES]
    slot_pass(0)
    swap_wait(2)
    unpack(2, mid)

    def give_output(block, k):
        out[block, :] = mid[block, :].astype(B16)

    chunks(give_output)
    loop(8, 16, slot_end)
    slot_pass(1)
    hear(1, s.vec_in, DP)
    s.vec_mine[...] = total_of(s.vec_in, nd)
    tell(2, lambda to: s.vec_mine, s.vec_side, TP)
    s.vec_side[f] = s.vec_mine[...]
    loop(4, 8, slot_end)
    slot_end(3)
    slot_pass(2)
    hear(2, s.vec_side, TP)
    grad_vec = total_of(s.vec_side, nf)
    gvec[...] = grad_vec
    loop(0, 3, slot_end)

    lane = lax.broadcasted_iota(jnp.int32, (8, LANES), 1)
    first_lane = (d * part) % LANES
    owned = (lane >= first_lane) & (lane < first_lane + part)
    s.sq_mine[0] += jnp.where(owned, grad_vec * grad_vec, 0.0) * (1.0 / nf)
    tell(3, lambda to: s.sq_mine.at[0], s.sq_side, TP)
    s.sq_side[f] = s.sq_mine[0]
    hear(3, s.sq_side, TP)
    s.sq_mine[1] = total_of(s.sq_side, nf)
    tell(4, lambda to: s.sq_mine.at[1], s.sq_all, DP)
    s.sq_all[d] = s.sq_mine[1]
    for g in range(4):
        gather_end(g)
    for k in range(6):
        spread_end(k)
    for k in range(4):
        swap_end(k)
    hear(4, s.sq_all, DP)
    total = jnp.sum(total_of(s.sq_all, nd), keepdims=True)
    nrm[...] = jnp.broadcast_to(jnp.sqrt(total), (8, LANES))


def adamw_step(weight, first, second, grad, rate):
    first = BETA_FIRST * first + (1.0 - BETA_FIRST) * grad
    second = BETA_SECOND * second + (1.0 - BETA_SECOND) * grad * grad
    fix_first = 1.0 - BETA_FIRST**STEP
    fix_second = 1.0 - BETA_SECOND**STEP
    update = first / fix_first / (jnp.sqrt(second / fix_second) + ADAM_EPS)
    return (weight - rate * (update + DECAY_RATE * weight), first, second)


def in_slot(j):
    return jnp.where(j < 3, j, jnp.where(j < 6, j + 1, j + 2))


def out_slot(j):
    k = jnp.minimum(j, 5)
    return jnp.where(k == 0, 3, jnp.where(k == 1, 7, k + 10))


def updates(*refs):
    grad_in, grad_out, grad_vec, norm, out, tgr = refs[:6]
    state = refs[6:15]
    new = refs[15:24]
    new_out, new_tgr, new_norm = refs[24:]
    j = pl.program_id(0)
    grad_norm = norm[0:1, 0:1]
    factor = CLIP_AT / jnp.maximum(grad_norm, CLIP_AT)

    def update(n, grad, rate):
        values = adamw_step(*(state[3 * n + k][...] for k in range(3)), grad * factor, rate)
        for k in range(3):
            new[3 * n + k][...] = values[k]

    update(0, grad_in[...], RATE_INPUT)

    @pl.when(j < 6)
    def _():
        update(1, grad_out[0].T[None], RATE_OUTPUT)

    @pl.when(j == 9)
    def _():
        update(2, grad_vec[0:4, :], RATE_VECTOR)
        new_out[...] = out[...]
        new_tgr[...] = tgr[...]
        new_norm[...] = grad_norm


def local(tokens, masks, cotangent, w_in, w_out, vectors, m_in, m_out, m_vec, v_in, v_out, v_vec):
    frames, here, width = tokens.shape
    part, _, hidden = w_in.shape
    nd, nf = lax.axis_size(DP), lax.axis_size(TP)
    z = SimpleNamespace(
        rows=frames * here,
        width=width,
        hidden=hidden,
        span=FRAMES // frames,
        nd=nd,
        nf=nf,
        part=part,
        heads=hidden // HDIM,
        frames=frames,
        here=here,
    )
    rows = frames * here
    lane0 = (lax.axis_index(DP) * part) % LANES

    def as_tile(value):
        if part == LANES:
            return value
        return lax.dynamic_update_slice(jnp.zeros((4, LANES), F32), value, (0, lane0))

    def of_tile(value):
        return value if part == LANES else lax.dynamic_slice(value, (0, lane0), (4, part))

    def by_slot(value):
        return value.transpose(1, 0, 2)

    vec = as_tile(vectors)
    scratch = scratch_of(z)
    in_vmem = pl.BlockSpec(memory_space=pltpu.VMEM)
    output, token_grad, norm, grads, grad_vec = pl.pallas_call(
        functools.partial(layer, z, list(scratch)),
        out_shape=(
            jax.ShapeDtypeStruct((rows, width), B16),
            jax.ShapeDtypeStruct((rows, width), B16),
            jax.ShapeDtypeStruct((8, LANES), F32),
            jax.ShapeDtypeStruct((16, part, hidden), F32),
            jax.ShapeDtypeStruct((8, LANES), F32),
        ),
        in_specs=[in_vmem] * 3 + [pl.BlockSpec(memory_space=pl.ANY)] * 2 + [in_vmem],
        out_specs=[in_vmem] * 5,
        scratch_shapes=list(scratch.values()),
        compiler_params=pltpu.CompilerParams(
            collective_id=0, has_side_effects=True, vmem_limit_bytes=VMEM_BYTES
        ),
    )(
        tokens.reshape(rows, width),
        masks.reshape(rows, 1).astype(F32),
        cotangent.reshape(rows, width),
        by_slot(w_in),
        w_out,
        vec,
    )

    def whole(shape):
        return pl.BlockSpec(shape, lambda j: (0,) * len(shape))

    slot_in = pl.BlockSpec((1, part, hidden), lambda j: (j, 0, 0))
    slot_out = pl.BlockSpec((1, hidden, part), lambda j: (jnp.minimum(j, 5), 0, 0))
    state_specs = [slot_in] * 3 + [slot_out] * 3 + [whole((4, LANES))] * 3
    row_specs = [whole((rows, width))] * 2
    state = (
        by_slot(w_in),
        by_slot(m_in),
        by_slot(v_in),
        w_out,
        m_out,
        v_out,
        vec,
        as_tile(m_vec),
        as_tile(v_vec),
    )
    new = pl.pallas_call(
        updates,
        grid=(10,),
        out_shape=tuple(jax.ShapeDtypeStruct(a.shape, F32) for a in state)
        + (jax.ShapeDtypeStruct((rows, width), B16),) * 2
        + (jax.ShapeDtypeStruct((1, 1), F32),),
        in_specs=[
            pl.BlockSpec((1, part, hidden), lambda j: (in_slot(j), 0, 0)),
            pl.BlockSpec((1, part, hidden), lambda j: (out_slot(j), 0, 0)),
            whole((8, LANES)),
            whole((8, LANES)),
        ]
        + row_specs
        + state_specs,
        out_specs=state_specs + row_specs + [whole((1, 1))],
    )(grads, grads, grad_vec, norm, output, token_grad, *state)
    new_w_in, new_m_in, new_v_in, new_w_out, new_m_out, new_v_out = new[:6]
    new_vectors, new_m_vec, new_v_vec, output, token_grad, norm = new[6:]
    return (
        output.reshape(frames, here, width),
        token_grad.reshape(frames, here, width),
        norm.reshape(()),
        by_slot(new_w_in),
        new_w_out,
        of_tile(new_vectors),
        by_slot(new_m_in),
        new_m_out,
        of_tile(new_m_vec),
        by_slot(new_v_in),
        new_v_out,
        of_tile(new_v_vec),
    )


def solution(mesh):
    in_specs = (
        P(DP, TP, None),
        P(DP, TP),
        P(DP, TP, None),
        P(DP, None, TP),
        P(None, TP, DP),
        P(None, DP),
        P(DP, None, TP),
        P(None, TP, DP),
        P(None, DP),
        P(DP, None, TP),
        P(None, TP, DP),
        P(None, DP),
    )
    out_specs = (P(DP, TP, None), P(DP, TP, None), P()) + in_specs[3:]
    return jax.shard_map(local, mesh=mesh, in_specs=in_specs, out_specs=out_specs, check_vma=False)
```

```python
import functools
from types import SimpleNamespace

import jax
import jax.numpy as jnp
from jax import lax
from jax.experimental import pallas as pl
from jax.experimental.pallas import tpu as pltpu
from jax.sharding import PartitionSpec as P

FRAMES = 16
STEP = 10
HDIM = 64


EPS_NORM = 1e-05
CLIP_AT = 1.0
BETA_FIRST = 0.9
BETA_SECOND = 0.95
ADAM_EPS = 1e-08
DECAY_RATE = 0.1
RATE_INPUT = 0.02
RATE_OUTPUT = 0.08
RATE_VECTOR = 1.0
NEG_FILL = -1e30
GELU_A = 0.7978845608028654
GELU_B = 0.044715

F32 = jnp.float32
B16 = jnp.bfloat16
MESH = pl.DeviceIdType.MESH
CHUNK = 16
DP = "dp"
TP = "fsdp"
LANES = 128
VMEM_BYTES = 63 << 20


def at(dp, fsdp):
    return {DP: dp, TP: fsdp}


def nn(a, b):
    return lax.dot_general(a, b, (((1,), (0,)), ((), ())), preferred_element_type=F32)


def nt(a, b):
    return lax.dot_general(a, b, (((1,), (1,)), ((), ())), preferred_element_type=F32)


def tn(a, b):
    return lax.dot_general(a, b, (((0,), (0,)), ((), ())), preferred_element_type=F32)


def loop(low, high, step):
    def body(k, carry):
        step(k)
        return carry

    lax.fori_loop(low, high, body, 0)


def each(low, high, step):
    if high - low <= 8:
        for k in range(low, high):
            step(k)
    else:
        loop(low, high, step)


def scratch_of(z):
    rows, width, hidden, span = z.rows, z.width, z.hidden, z.span
    nd, nf, part, heads = z.nd, z.nf, z.part, z.heads
    outer = nd // 2
    flat = (nf, z.frames, z.here, hidden)
    vmem = pltpu.VMEM
    dma = pltpu.SemaphoreType.DMA
    return dict(
        stage_in=vmem((10, part, hidden), F32),
        stage_out=vmem((6, hidden, part), F32),
        shard=vmem((4, 4, part, hidden), B16),
        tile=vmem((8, LANES), F32),
        masked=vmem((rows, LANES), F32),
        weights=vmem((4, 4, width, hidden), B16),
        gathered=vmem((6, nf, rows, width), B16),
        gains=vmem((8, width), F32),
        tiles=vmem((nd, 8, LANES), F32),
        hats=vmem((3, rows, width), F32),
        rstds=vmem((3, rows, LANES), F32),
        work=vmem((rows, width), F32),
        mid=vmem((rows, width), F32),
        swap_out=vmem((4, span, CHUNK, width), B16),
        swap_in=vmem((4, span, CHUNK, width), B16),
        part_sum=vmem((2, 2, rows, width), F32),
        sib_out=vmem((2, 2, rows, width), B16),
        sib_in=vmem((2, 2, rows, width), B16),
        far_out=vmem((2, rows, width), B16),
        far_in=vmem((2, rows, width), B16),
        qkv=vmem((2, 3) + flat, B16),
        mixed=vmem((2,) + flat, B16),
        grad_mixed=vmem(flat, B16),
        grad_qkv=vmem((3,) + flat, B16),
        probs_a=vmem((z.frames * heads, nf * z.here, nf * z.here), F32),
        probs_b=vmem((nf * heads, rows, rows), F32),
        act=vmem((4,) + flat, B16),
        slope=vmem((4,) + flat, F32),
        grad_pre=vmem((4,) + flat, B16),
        product=vmem((outer, 2, part, hidden), F32),
        own_sum=vmem((16, outer, part, hidden), B16),
        pair_out=vmem((16, outer, part, hidden), B16),
        pair_in=vmem((16, outer, part, hidden), B16),
        line_in=vmem((16, outer, part, hidden), B16),
        vec_acc=vmem((8, width), F32),
        vec_out=vmem((width // LANES, 8, LANES), F32),
        vec_in=vmem((nd, 8, LANES), F32),
        vec_mine=vmem((8, LANES), F32),
        vec_side=vmem((nf, 8, LANES), F32),
        sq_mine=vmem((2, 8, LANES), F32),
        sq_side=vmem((nf, 8, LANES), F32),
        sq_all=vmem((nd, 8, LANES), F32),
        small_s=dma((5,)),
        small_r=dma((5,)),
        line_ws=dma((4,)),
        line_wr=dma((4, outer)),
        pair_ws=dma((4,)),
        pair_wr=dma((4,)),
        pair_wo=dma((4,)),
        own_ws=dma((4,)),
        near_ws=dma((4,)),
        near_wr=dma((4,)),
        far_ws=dma((4,)),
        copy_w=dma((4,)),
        row_s=dma((6, 3)),
        row_r=dma((6, 3)),
        sum_s=dma((6, 3)),
        sum_r=dma((6, 3)),
        swap_s=dma((4,)),
        swap_r=dma((4,)),
        stage_s=dma((16,)),
        pair_gs=dma((16,)),
        pair_gr=dma((16,)),
        line_gs=dma((16,)),
        line_gr=dma((16,)),
    )


def layer(z, names, *refs):
    tok, msk, cot, w_in, w_out, vec = refs[:6]
    out, tgr, nrm, gin, gout, gvec = refs[6:12]
    s = SimpleNamespace(**dict(zip(names, refs[12:])))
    rows, width, hidden, span = z.rows, z.width, z.hidden, z.span
    nd, nf, part, heads = z.nd, z.nf, z.part, z.heads
    frames, here = z.frames, z.here
    outer = nd // 2
    piece = here // span
    n_pairs = heads // 2
    scale = HDIM**-0.5
    gathered, weights, gains = s.gathered, s.weights, s.gains
    work, mid, shard = s.work, s.mid, s.shard
    swap_out, swap_in = s.swap_out, s.swap_in

    d, f = lax.axis_index(DP), lax.axis_index(TP)
    o, i = d // 2, d % 2
    y, c = f // 2, f % 2
    place = d % span
    base = d - place
    f_sib, f_far, f_last = y * 2 + 1 - c, (1 - y) * 2 + c, (1 - y) * 2 + 1 - c
    mate = at(o * 2 + 1 - i, f)
    sib = at(d, f_sib)
    far = at(d, f_far)

    def rcopy(src, dst, ssem, rsem, dev):
        return pltpu.make_async_remote_copy(
            src_ref=src, dst_ref=dst, send_sem=ssem, recv_sem=rsem, device_id=dev, device_id_type=MESH
        )

    in_slots = {0: [0, 1, 2], 1: [3, 4, 5], 2: [6, 7, 8, 9], 3: []}
    out_slots = {0: [0], 1: [1], 2: [], 3: [2, 3, 4, 5]}

    def stage(g):
        for n in in_slots[g]:
            yield pltpu.make_async_copy(w_in.at[n], s.stage_in.at[n], s.stage_s.at[n])
        for n in out_slots[g]:
            yield pltpu.make_async_copy(w_out.at[n], s.stage_out.at[n], s.stage_s.at[10 + n])

    def round_group(g):
        for cp in stage(g):
            cp.wait()
        for j, n in enumerate(in_slots[g]):
            shard[g, j] = s.stage_in[n].astype(B16)
        for j, n in enumerate(out_slots[g]):
            shard[g, len(in_slots[g]) + j] = s.stage_out[n].T.astype(B16)

    for g in range(4):
        for cp in stage(g):
            cp.start()
    s.tile[...] = jnp.zeros_like(s.tile)
    s.tile[0:4, :] = vec[...].astype(B16).astype(F32)

    same = lax.broadcasted_iota(jnp.int32, (here, here), 0) == lax.broadcasted_iota(
        jnp.int32, (here, here), 1
    )
    for fr in range(frames):
        line = jnp.broadcast_to(msk[fr : fr + 1, :], (here, here)).astype(F32)
        column = jnp.sum(jnp.where(same, line, 0.0), axis=1, keepdims=True)
        s.masked[fr * here : (fr + 1) * here, :] = jnp.broadcast_to(column, (here, LANES))

    bar = pltpu.get_barrier_semaphore()

    def greet(q):
        dev = at((d + q) % nd, f)
        pl.semaphore_signal(bar, inc=1, device_id=dev, device_id_type=MESH)

    each(1, nd, greet)
    for q in range(1, nf):
        dev = at(d, (f + q) % nf)
        pl.semaphore_signal(bar, inc=1, device_id=dev, device_id_type=MESH)
    pl.semaphore_wait(bar, nd - 1 + nf - 1)

    def tell(n, src_of, dst, axis):
        count, me = (nd, d) if axis == DP else (nf, f)

        def go(q):
            to = (me + q) % count
            dev = at(to, f) if axis == DP else at(d, to)
            rcopy(src_of(to), dst.at[me], s.small_s.at[n], s.small_r.at[n], dev).start()

        each(1, count, go)

    def hear(n, dst, axis):
        count = nd if axis == DP else nf
        others = dst.at[pl.ds(0, count - 1)]
        cp = rcopy(others, others, s.small_s.at[n], s.small_r.at[n], mate)
        cp.wait_recv()
        cp.wait_send()

    def total_of(ref, count):
        total = ref[0]
        if count <= 8:
            for k in range(1, count):
                total = total + ref[k]
            return total
        return lax.fori_loop(1, count, lambda k, t: t + ref[k], total)

    tell(0, lambda to: s.tile, s.tiles, DP)

    four = outer == 4
    near_row = o + 1 - 2 * (o % 2)
    next_row = jnp.where(o < 2, 2, 1)
    last_row = jnp.where(o < 2, 3, 0)
    middle = (o == 1) | (o == 2)

    def shard_rows(owner):
        return pl.ds(pl.multiple_of(owner * part, part), part)

    def shard_of(g, row, col):
        return weights.at[g, :, shard_rows(row * 2 + col), :]

    def gather_own(g):
        mine = shard_of(g, o, i)
        pltpu.make_async_copy(shard.at[g], mine, s.copy_w.at[g]).start()
        rcopy(shard.at[g], mine, s.own_ws.at[g], s.pair_wo.at[g], mate).start()

    def gather_line(g, low, high):
        def go(q):
            to = (o + q) % outer

            def start():
                rcopy(
                    shard.at[g],
                    shard_of(g, o, i),
                    s.line_ws.at[g],
                    s.line_wr.at[g, o],
                    at(to * 2 + i, f),
                ).start()

            if four:
                pl.when(jnp.abs(to - o) < 3)(start)
            else:
                start()

        each(low, high, go)

    def gather_from(g, row):
        block = shard_of(g, row, i)
        rcopy(block, block, s.line_ws.at[g], s.line_wr.at[g, row], mate).wait_recv()
        return block

    def gather_pass(g, low, high):
        if not four:

            def go(q):
                block = gather_from(g, (o + outer - q) % outer)
                rcopy(block, block, s.pair_ws.at[g], s.pair_wr.at[g], mate).start()

            each(low, high, go)
            return
        for q in range(low, high):
            if q == 1:
                block = shard_of(g, o, 1 - i)
                rcopy(block, block, s.pair_ws.at[g], s.pair_wo.at[g], mate).wait_recv()
                half = block.at[pl.ds(2, 2)]
                dev = at(near_row * 2 + i, f)
                rcopy(half, half, s.near_ws.at[g], s.near_wr.at[g], dev).start()
                half = gather_from(g, near_row).at[pl.ds(0, 2)]
                rcopy(half, half, s.pair_ws.at[g], s.pair_wr.at[g], mate).start()
            else:
                row = next_row if q == 2 else last_row
                block = gather_from(g, row)

                @pl.when(middle & (row == last_row))
                def _():
                    dev = at((3 - last_row) * 2 + i, f)
                    rcopy(block, block, s.far_ws.at[g], s.line_wr.at[g, row], dev).start()

                rcopy(block, block, s.pair_ws.at[g], s.pair_wr.at[g], mate).start()

    def gather_ready(g):
        mine = shard_of(g, o, i)
        pltpu.make_async_copy(shard.at[g], mine, s.copy_w.at[g]).wait()
        if not four:
            block = shard_of(g, o, 1 - i)
            rcopy(block, block, s.pair_ws.at[g], s.pair_wo.at[g], mate).wait_recv()
        if four:
            half = weights.at[g, pl.ds(0, 2), pl.ds(0, part), :]
            rcopy(half, half, s.near_ws.at[g], s.near_wr.at[g], mate).wait_recv()
        halves = 5 if four else 2 * (outer - 1)
        both = half_shards(g, halves)
        rcopy(both, both, s.pair_ws.at[g], s.pair_wr.at[g], mate).wait_recv()

    def half_shards(g, count):
        return weights.at[g, pl.ds(0, 2), pl.ds(0, count * part), :]

    def gather_end(g):
        def sent(sem, halves):
            both = half_shards(g, halves)
            rcopy(both, both, sem.at[g], s.pair_wr.at[g], mate).wait_send()

        if not four:
            sent(s.pair_ws, nd - 2)
            sent(s.line_ws, nd - 2)
            rest = shard_of(g, o, i)
            rcopy(rest, rest, s.own_ws.at[g], s.pair_wr.at[g], mate).wait_send()
            return
        sent(s.own_ws, 2)
        sent(s.pair_ws, 5)
        sent(s.near_ws, 1)

        @pl.when(middle)
        def _():
            sent(s.line_ws, 6)
            sent(s.far_ws, 2)

        @pl.when(jnp.logical_not(middle))
        def _():
            sent(s.line_ws, 4)

    def spread_start(k):
        block = gathered.at[k, f]
        rcopy(block, block, s.row_s.at[k, 1], s.row_r.at[k, 1], far).start()
        rcopy(block, block, s.row_s.at[k, 0], s.row_r.at[k, 0], sib).start()

    def spread_near(k):
        block = gathered.at[k, f_sib]
        rcopy(block, block, s.row_s.at[k, 0], s.row_r.at[k, 0], sib).wait_recv()

    def spread_pass(k):
        block = gathered.at[k, f_far]
        rcopy(block, block, s.row_s.at[k, 1], s.row_r.at[k, 1], far).wait_recv()
        rcopy(block, block, s.row_s.at[k, 2], s.row_r.at[k, 2], sib).start()

    def spread_far(k):
        block = gathered.at[k, f_last]
        rcopy(block, block, s.row_s.at[k, 2], s.row_r.at[k, 2], sib).wait_recv()

    def spread_end(k):
        block = gathered.at[k, f]
        for n in range(3):
            rcopy(block, block, s.row_s.at[k, n], s.row_r.at[k, n], sib).wait_send()

    def collect_start(k, terms):
        par = k % 2
        for slot in range(2):
            pair = (1 - y) if slot == 0 else y

            for t in range(width // hidden):
                cols = slice(t * hidden, (t + 1) * hidden)
                total = None
                for b_ref, g, j in terms:
                    value = nt(
                        b_ref[pl.ds(pair * 2, 2)].reshape(2 * rows, hidden), weights[g, j, cols, :]
                    )
                    total = value if total is None else total + value
                s.part_sum[slot, :, :, cols] = total.reshape(2, rows, hidden)
            s.sib_out[par, slot] = s.part_sum[slot, 1 - c].astype(B16)
            rcopy(
                s.sib_out.at[par, slot],
                s.sib_in.at[par, slot],
                s.sum_s.at[k, slot],
                s.sum_r.at[k, slot],
                sib,
            ).start()
        back = s.sib_in.at[par, 0]
        rcopy(back, back, s.sum_s.at[k, 0], s.sum_r.at[k, 0], sib).wait_recv()
        s.far_out[par] = (s.part_sum[0, c] + s.sib_in[par, 0].astype(F32)).astype(B16)
        rcopy(
            s.far_out.at[par], s.far_in.at[par], s.sum_s.at[k, 2], s.sum_r.at[k, 2], far
        ).start()

    def collect_end(k):
        par = k % 2
        near, away = s.sib_in.at[par, 1], s.far_in.at[par]
        rcopy(near, near, s.sum_s.at[k, 1], s.sum_r.at[k, 1], sib).wait_recv()
        rcopy(away, away, s.sum_s.at[k, 2], s.sum_r.at[k, 2], far).wait_recv()
        for n in range(3):
            rcopy(near, near, s.sum_s.at[k, n], s.sum_r.at[k, n], sib).wait_send()

        def get(block):
            return (
                s.part_sum[1, c, block]
                + s.sib_in[par, 1, block].astype(F32)
                + s.far_in[par, block].astype(F32)
            )

        return get

    def swap_start(k):
        def go(q):
            to = (place + q) % span
            rcopy(
                swap_out.at[k, to],
                swap_in.at[k, place],
                s.swap_s.at[k],
                s.swap_r.at[k],
                at(base + to, f),
            ).start()

        each(1, span, go)
        swap_in[k, place] = swap_out[k, place]

    def swap_wait(k):
        others = swap_in.at[k, pl.ds(0, span - 1)]
        rcopy(others, others, s.swap_s.at[k], s.swap_r.at[k], mate).wait_recv()

    def swap_end(k):
        others = swap_in.at[k, pl.ds(0, span - 1)]
        rcopy(others, others, s.swap_s.at[k], s.swap_r.at[k], mate).wait_send()

    def token_rows(fr, j):
        return pl.ds(pl.multiple_of(fr * here + j * piece, piece), piece)

    def pack(k, src):
        def step(j):
            parts = [src[token_rows(fr, j), :] for fr in range(frames)]
            swap_out[k, j] = jnp.concatenate(parts, axis=0).astype(B16)

        loop(0, span, step)

    def unpack(k, dst):
        def step(j):
            value = swap_in[k, j].astype(F32)
            for fr in range(frames):
                dst[token_rows(fr, j), :] = value[fr * piece : (fr + 1) * piece]

        loop(0, span, step)

    def chunks(step):
        loop(0, rows // CHUNK, lambda k: step(pl.ds(pl.multiple_of(k * CHUNK, CHUNK), CHUNK), k))

    def norm_rows(n, value, block):
        centered = value - jnp.mean(value, axis=-1, keepdims=True)
        rstd = lax.rsqrt(jnp.mean(centered * centered, axis=-1, keepdims=True) + EPS_NORM)
        hat = centered * rstd
        s.hats[n, block] = hat
        s.rstds[n, block] = jnp.broadcast_to(rstd, (CHUNK, LANES))
        return (hat * gains[n : n + 1, :]).astype(B16)

    def norm_back(n, grad, block):
        hat = s.hats[n, block]
        rstd = s.rstds[n, block][:, 0:1]
        grad_hat = grad * gains[n : n + 1, :]
        first = jnp.mean(grad_hat, axis=-1, keepdims=True)
        second = jnp.mean(grad_hat * hat, axis=-1, keepdims=True)
        s.vec_acc[n : n + 1, :] += jnp.sum(grad * hat, axis=0, keepdims=True)
        return rstd * (grad_hat - first - hat * second)

    def pair_rows(k, pair):
        return gathered[k, pl.ds(pair * 2, 2)].reshape(2 * rows, width)

    def as_flat(value):
        return value.reshape(2, frames, here, hidden)

    def project(k, g, dst, pair):
        def step(j):
            dst[j, pl.ds(pair * 2, 2)] = as_flat(nn(pair_rows(k, pair), weights[g, j]).astype(B16))

        each(0, 3, step)

    def attend(block):
        spatial = block == 0
        n = nf * here if spatial else rows

        def load(ref, g, lanes):
            value = ref[:, g, :, lanes] if spatial else ref[g, :, :, lanes]
            return value.reshape(n, 2 * HDIM)

        def store(ref, g, lanes, value):
            if spatial:
                ref[:, g, :, lanes] = value.reshape(nf, here, 2 * HDIM)
            else:
                ref[g, :, :, lanes] = value.reshape(frames, here, 2 * HDIM)

        return n, load, store, (s.probs_a if spatial else s.probs_b)

    def head_lanes(n):
        return lax.broadcasted_iota(jnp.int32, (n, 2 * HDIM), 1) < HDIM

    def kept(n):
        query = lax.broadcasted_iota(jnp.int32, (n, n), 0)
        key = lax.broadcasted_iota(jnp.int32, (n, n), 1)
        return (query % piece == key % piece) & (key // piece <= query // piece)

    def each_pair(block, step):
        def go(k):
            first = (k % n_pairs) * 2 * HDIM
            step(k, k // n_pairs, slice(first, first + 2 * HDIM))

        each(0, (frames if block == 0 else nf) * n_pairs, go)

    def attention(block):
        n, load, store, probs = attend(block)
        qkv = s.qkv.at[block]

        def step(k, g, lanes):
            query, key, value = (load(qkv.at[j], g, lanes) for j in range(3))
            low = head_lanes(n)
            found = []
            for h in range(2):
                mine = jnp.where(low if h == 0 else ~low, query, jnp.zeros_like(query))
                scores = nt(mine, key) * scale
                if block == 1:
                    scores = jnp.where(kept(n), scores, NEG_FILL)
                expd = jnp.exp(scores - jnp.max(scores, axis=-1, keepdims=True))
                prob = expd / jnp.sum(expd, axis=-1, keepdims=True)
                probs[k * 2 + h] = prob
                found.append(nn(prob.astype(B16), value))
            store(s.mixed.at[block], g, lanes, jnp.where(low, found[0], found[1]).astype(B16))

        each_pair(block, step)

    def attention_back(block):
        n, load, store, probs = attend(block)
        qkv = s.qkv.at[block]

        def step(k, g, lanes):
            query, key, value = (load(qkv.at[j], g, lanes) for j in range(3))
            grad = load(s.grad_mixed, g, lanes)
            low = head_lanes(n)
            found = []
            for h in range(2):
                mine = jnp.where(low if h == 0 else ~low, grad, jnp.zeros_like(grad))
                prob = probs[k * 2 + h]
                grad_prob = nt(mine, value)
                inner = jnp.sum(prob * grad_prob, axis=-1, keepdims=True)
                grad_score = (prob * (grad_prob - inner)).astype(B16)
                found.append(
                    (
                        nn(grad_score, key) * scale,
                        tn(grad_score, query) * scale,
                        tn(prob.astype(B16), grad),
                    )
                )
            for j in range(3):
                both = jnp.where(low, found[0][j], found[1][j]).astype(B16)
                store(s.grad_qkv.at[j], g, lanes, both)

        each_pair(block, step)

    def mixed_back(k, g):
        def half(pair):
            value = nn(pair_rows(k, pair), weights[g, 3])
            s.grad_mixed[pl.ds(pair * 2, 2)] = as_flat(value.astype(B16))

        spread_near(k)
        half(y)
        spread_pass(k)
        spread_far(k)
        half(1 - y)

    def slot_make(slot, k, b_ref):
        value = tn(gathered[k].reshape(nf * rows, width), b_ref[...].reshape(nf * rows, hidden))
        s.product[...] = value.reshape(outer, 2, part, hidden)
        s.pair_out[slot] = s.product[:, 1 - i].astype(B16)
        s.own_sum[slot] = s.product[:, i].astype(B16)

    def slot_send(slot):
        rcopy(
            s.pair_out.at[slot],
            s.pair_in.at[slot],
            s.pair_gs.at[slot],
            s.pair_gr.at[slot],
            mate,
        ).start()

    def slot_sum(slot):
        g, j = slot // 4, slot % 4
        if g < 2:
            return gin.at[g * 3 + j] if j < 3 else gout.at[g]
        return gin.at[6 + j] if g == 2 else gout.at[2 + j]

    def slot_pass(slot):
        block = s.pair_in.at[slot]
        cp = rcopy(block, block, s.pair_gs.at[slot], s.pair_gr.at[slot], mate)
        cp.wait_recv()
        cp.wait_send()

        def both(owner):
            return s.own_sum[slot, owner].astype(F32) + s.pair_in[slot, owner].astype(F32)

        def go(q):
            to = (o + q) % outer
            s.pair_out[slot, q] = both(to).astype(B16)
            rcopy(
                s.pair_out.at[slot, q],
                s.line_in.at[slot, q],
                s.line_gs.at[slot],
                s.line_gr.at[slot],
                at(to * 2 + i, f),
            ).start()

        each(1, outer, go)
        slot_sum(slot)[...] = both(o)

    def slot_end(slot):
        block = s.line_in.at[slot, pl.ds(1, outer - 1)]
        cp = rcopy(block, block, s.line_gs.at[slot], s.line_gr.at[slot], mate)
        cp.wait_recv()
        cp.wait_send()
        total = slot_sum(slot)[...]
        if outer <= 8:
            for q in range(1, outer):
                total = total + s.line_in[slot, q].astype(F32)
        else:
            total = lax.fori_loop(
                1, outer, lambda q, t: t + s.line_in[slot, q].astype(F32), total
            )
        slot_sum(slot)[...] = total
        folded = jnp.sum((total * total).reshape(part // 8, 8, hidden), axis=0)
        for k in range(hidden // LANES):
            s.sq_mine[0] += folded[:, k * LANES : (k + 1) * LANES]

    round_group(0)
    gather_line(0, 1, outer)
    gather_own(0)
    hear(0, s.tiles, DP)
    s.tiles[d] = s.tile[...]
    per_tile = LANES // part
    for k in range(width // LANES):
        gains[:, k * LANES : (k + 1) * LANES] = total_of(
            s.tiles.at[pl.ds(k * per_tile, per_tile)], per_tile
        )
    s.vec_acc[...] = jnp.zeros_like(s.vec_acc)
    s.sq_mine[...] = jnp.zeros_like(s.sq_mine)

    def masked_rows(block):
        return jnp.broadcast_to(s.masked[block, 0:1], (CHUNK, width)) > 0.5

    def first_norm(block, k):
        value = jnp.where(masked_rows(block), gains[3:4, :], tok[block, :].astype(F32))
        work[block, :] = value
        gathered[0, f, block] = norm_rows(0, value, block)

    chunks(first_norm)
    spread_start(0)
    round_group(1)
    gather_line(1, 1, outer)
    gather_own(1)
    gather_pass(0, 1, 2)

    def widen(block, k):
        s.part_sum[0, 0, block, :] = cot[block, :].astype(F32)

    chunks(widen)
    pack(0, s.part_sum.at[0, 0])
    swap_start(0)

    gather_pass(0, 2, outer - 1)
    spread_near(0)
    spread_pass(0)
    gather_pass(0, outer - 1, outer)
    round_group(2)
    gather_ready(0)
    project(0, 0, s.qkv.at[0], y)
    spread_far(0)
    project(0, 0, s.qkv.at[0], 1 - y)
    gather_pass(1, 1, 2)
    attention(0)
    gather_pass(1, 2, outer - 1)
    collect_start(0, [(s.mixed.at[0], 0, 3)])
    gather_pass(1, outer - 1, outer)
    round_group(3)
    get = collect_end(0)

    def take_branch(block, k):
        work[block, :] = work[block, :] + get(block)

    chunks(take_branch)
    pack(1, work)
    swap_start(1)
    gather_line(2, 1, outer)
    gather_line(3, 1, outer)
    gather_own(2)
    gather_own(3)

    swap_wait(0)
    gathered[1, f] = swap_in[0].reshape(rows, width)
    spread_start(1)
    swap_wait(1)

    def second_norm(block, k):
        value = swap_in[1, k].astype(F32)
        mid[block, :] = value
        gathered[2, f, block] = norm_rows(1, value, block)

    chunks(second_norm)
    spread_start(2)
    spread_near(1)
    spread_pass(1)
    gather_ready(1)
    spread_near(2)
    project(2, 1, s.qkv.at[1], y)
    gather_pass(2, 1, 2)
    spread_pass(2)
    gather_pass(2, 2, outer - 1)
    spread_far(2)
    project(2, 1, s.qkv.at[1], 1 - y)
    attention(1)
    gather_pass(2, outer - 1, outer)
    collect_start(1, [(s.mixed.at[1], 1, 3)])
    gather_pass(3, 1, 2)
    get = collect_end(1)

    def third_norm(block, k):
        value = mid[block, :] + get(block)
        mid[block, :] = value
        gathered[3, f, block] = norm_rows(2, value, block)

    chunks(third_norm)
    spread_start(3)
    spread_far(1)
    gather_pass(3, 2, outer - 1)


    def up(pair):
        def step(n):
            u = nn(pair_rows(3, pair), weights[2, n])
            t = jnp.tanh(GELU_A * (u + GELU_B * u * u * u))
            half = 0.5 * (1.0 + t)
            s.act[n, pl.ds(pair * 2, 2)] = as_flat((u * half).astype(B16))
            bend = GELU_A * (1.0 + 3.0 * GELU_B * u * u)
            s.slope[n, pl.ds(pair * 2, 2)] = as_flat(half + 0.5 * u * (1.0 - t * t) * bend)

        each(0, 4, step)

    def down(pair):
        def step(n):
            grad = nn(pair_rows(1, pair), weights[3, n])
            slope = s.slope[n, pl.ds(pair * 2, 2)].reshape(2 * rows, hidden)
            s.grad_pre[n, pl.ds(pair * 2, 2)] = as_flat((grad * slope).astype(B16))

        each(0, 4, step)

    gather_ready(2)
    spread_near(3)
    up(y)
    spread_pass(3)
    gather_pass(3, outer - 1, outer)
    spread_far(3)
    up(1 - y)
    each(0, 4, lambda n: slot_make(12 + n, 1, s.act.at[n]))
    slot_send(12)
    slot_send(13)
    gather_ready(3)

    down(1 - y)
    down(y)
    slot_make(8, 3, s.grad_pre.at[0])
    slot_send(8)
    collect_start(2, [(s.grad_pre.at[n], 2, n) for n in range(4)])
    slot_pass(12)
    each(1, 4, lambda n: slot_make(8 + n, 3, s.grad_pre.at[n]))
    slot_send(9)
    slot_send(14)
    slot_pass(13)
    get = collect_end(2)

    def third_back(block, k):
        value = swap_in[0, k].astype(F32) + norm_back(2, get(block), block)
        work[block, :] = value
        gathered[4, f, block] = value.astype(B16)

    chunks(third_back)
    spread_start(4)
    slot_pass(8)
    slot_send(10)
    slot_send(15)
    collect_start(3, [(s.act.at[n], 3, n) for n in range(4)])
    slot_pass(9)

    mixed_back(4, 1)
    slot_make(7, 4, s.mixed.at[1])
    slot_pass(14)
    slot_send(11)
    slot_send(7)
    get_output = collect_end(3)

    def take_output(block, k):
        swap_out[2, k] = (mid[block, :] + get_output(block)).astype(B16)

    chunks(take_output)
    swap_start(2)
    attention_back(1)
    slot_pass(10)
    collect_start(4, [(s.grad_qkv.at[j], 1, j) for j in range(3)])
    slot_pass(15)
    each(0, 3, lambda j: slot_make(4 + j, 2, s.grad_qkv.at[j]))
    slot_pass(11)
    get = collect_end(4)

    def second_back(block, k):
        swap_out[3, k] = (work[block, :] + norm_back(1, get(block), block)).astype(B16)

    chunks(second_back)
    swap_start(3)
    slot_send(4)
    slot_send(5)
    slot_send(6)

    swap_wait(3)
    unpack(3, work)

    def take_carry(block, k):
        gathered[5, f, block] = work[block, :].astype(B16)

    chunks(take_carry)
    spread_start(5)
    slot_pass(7)
    mixed_back(5, 0)
    slot_make(3, 5, s.mixed.at[0])
    slot_send(3)
    slot_pass(4)
    attention_back(0)

    def spatial_slot(j):
        slot_make(j, 0, s.grad_qkv.at[j])
        slot_send(j)

    loop(0, 3, spatial_slot)
    slot_pass(5)
    collect_start(5, [(s.grad_qkv.at[j], 0, j) for j in range(3)])
    slot_pass(6)
    slot_pass(3)
    get = collect_end(5)

    def first_back(block, k):
        value = work[block, :] + norm_back(0, get(block), block)
        masked = masked_rows(block)
        tgr[block, :] = jnp.where(masked, 0.0, value).astype(B16)
        s.vec_acc[3:4, :] += jnp.sum(jnp.where(masked, value, 0.0), axis=0, keepdims=True)

    chunks(first_back)

    for k in range(width // LANES):
        s.vec_out[k] = s.vec_acc[:, k * LANES : (k + 1) * LANES]
    tell(1, lambda to: s.vec_out.at[(to * part) // LANES], s.vec_in, DP)
    s.vec_in[d] = s.vec_out[(d * part) // LANES]
    slot_pass(0)
    swap_wait(2)
    unpack(2, mid)

    def give_output(block, k):
        out[block, :] = mid[block, :].astype(B16)

    chunks(give_output)
    each(8, 16, slot_end)
    slot_pass(1)
    hear(1, s.vec_in, DP)
    s.vec_mine[...] = total_of(s.vec_in, nd)
    tell(2, lambda to: s.vec_mine, s.vec_side, TP)
    s.vec_side[f] = s.vec_mine[...]
    each(4, 8, slot_end)
    slot_end(3)
    slot_pass(2)
    hear(2, s.vec_side, TP)
    grad_vec = total_of(s.vec_side, nf)
    gvec[...] = grad_vec
    each(0, 3, slot_end)

    lane = lax.broadcasted_iota(jnp.int32, (8, LANES), 1)
    first_lane = (d * part) % LANES
    owned = (lane >= first_lane) & (lane < first_lane + part)
    s.sq_mine[0] += jnp.where(owned, grad_vec * grad_vec, 0.0) * (1.0 / nf)
    tell(3, lambda to: s.sq_mine.at[0], s.sq_side, TP)
    s.sq_side[f] = s.sq_mine[0]
    hear(3, s.sq_side, TP)
    s.sq_mine[1] = total_of(s.sq_side, nf)
    tell(4, lambda to: s.sq_mine.at[1], s.sq_all, DP)
    s.sq_all[d] = s.sq_mine[1]
    for g in range(4):
        gather_end(g)
    for k in range(6):
        spread_end(k)
    for k in range(4):
        swap_end(k)
    hear(4, s.sq_all, DP)
    total = jnp.sum(total_of(s.sq_all, nd), keepdims=True)
    nrm[...] = jnp.broadcast_to(jnp.sqrt(total), (8, LANES))


def adamw_step(weight, first, second, grad, rate):
    first = BETA_FIRST * first + (1.0 - BETA_FIRST) * grad
    second = BETA_SECOND * second + (1.0 - BETA_SECOND) * grad * grad
    fix_first = 1.0 / (1.0 - BETA_FIRST**STEP)
    fix_second = 1.0 / (1.0 - BETA_SECOND**STEP)
    update = (rate * fix_first) * first / (jnp.sqrt(second * fix_second) + ADAM_EPS)
    return (weight * (1.0 - rate * DECAY_RATE) - update, first, second)


def updates(*refs):
    grad_in, grad_out, grad_vec, norm, out, tgr = refs[:6]
    state = refs[6:15]
    new = refs[15:24]
    new_out, new_tgr, new_norm = refs[24:]
    j = pl.program_id(0)
    grad_norm = norm[0:1, 0:1]
    factor = CLIP_AT / jnp.maximum(grad_norm, CLIP_AT)

    def update(n, grad, rate):
        values = adamw_step(*(state[3 * n + k][...] for k in range(3)), grad * factor, rate)
        for k in range(3):
            new[3 * n + k][...] = values[k]

    update(0, grad_in[...], RATE_INPUT)

    update(1, jnp.stack([grad_out[n].T for n in range(3)]), RATE_OUTPUT)

    @pl.when(j == 1)
    def _():
        update(2, grad_vec[0:4, :], RATE_VECTOR)
        new_out[...] = out[...]
        new_tgr[...] = tgr[...]
        new_norm[...] = grad_norm


def local(tokens, masks, cotangent, w_in, w_out, vectors, m_in, m_out, m_vec, v_in, v_out, v_vec):
    frames, here, width = tokens.shape
    part, _, hidden = w_in.shape
    nd, nf = lax.axis_size(DP), lax.axis_size(TP)
    z = SimpleNamespace(
        rows=frames * here,
        width=width,
        hidden=hidden,
        span=FRAMES // frames,
        nd=nd,
        nf=nf,
        part=part,
        heads=hidden // HDIM,
        frames=frames,
        here=here,
    )
    rows = frames * here
    lane0 = (lax.axis_index(DP) * part) % LANES

    def as_tile(value):
        if part == LANES:
            return value
        return lax.dynamic_update_slice(jnp.zeros((4, LANES), F32), value, (0, lane0))

    def of_tile(value):
        return value if part == LANES else lax.dynamic_slice(value, (0, lane0), (4, part))

    def by_slot(value):
        return value.transpose(1, 0, 2)

    vec = as_tile(vectors)
    scratch = scratch_of(z)
    in_vmem = pl.BlockSpec(memory_space=pltpu.VMEM)
    output, token_grad, norm, grad_in, grad_out, grad_vec = pl.pallas_call(
        functools.partial(layer, z, list(scratch)),
        out_shape=(
            jax.ShapeDtypeStruct((rows, width), B16),
            jax.ShapeDtypeStruct((rows, width), B16),
            jax.ShapeDtypeStruct((8, LANES), F32),
            jax.ShapeDtypeStruct((10, part, hidden), F32),
            jax.ShapeDtypeStruct((6, part, hidden), F32),
            jax.ShapeDtypeStruct((8, LANES), F32),
        ),
        in_specs=[in_vmem] * 3 + [pl.BlockSpec(memory_space=pl.ANY)] * 2 + [in_vmem],
        out_specs=[in_vmem] * 6,
        scratch_shapes=list(scratch.values()),
        compiler_params=pltpu.CompilerParams(
            collective_id=0, has_side_effects=True, vmem_limit_bytes=VMEM_BYTES
        ),
    )(
        tokens.reshape(rows, width),
        masks,
        cotangent.reshape(rows, width),
        by_slot(w_in),
        w_out,
        vec,
    )

    def whole(shape):
        return pl.BlockSpec(shape, lambda j: (0,) * len(shape))

    slot_in = pl.BlockSpec((5, part, hidden), lambda j: (j, 0, 0))
    slot_out = pl.BlockSpec((3, hidden, part), lambda j: (j, 0, 0))
    state_specs = [slot_in] * 3 + [slot_out] * 3 + [whole((4, LANES))] * 3
    row_specs = [whole((rows, width))] * 2
    state = (
        by_slot(w_in),
        by_slot(m_in),
        by_slot(v_in),
        w_out,
        m_out,
        v_out,
        vec,
        as_tile(m_vec),
        as_tile(v_vec),
    )
    new = pl.pallas_call(
        updates,
        grid=(2,),
        out_shape=tuple(jax.ShapeDtypeStruct(a.shape, F32) for a in state)
        + (jax.ShapeDtypeStruct((rows, width), B16),) * 2
        + (jax.ShapeDtypeStruct((1, 1), F32),),
        in_specs=[
            slot_in,
            pl.BlockSpec((3, part, hidden), lambda j: (j, 0, 0)),
            whole((8, LANES)),
            whole((8, LANES)),
        ]
        + row_specs
        + state_specs,
        out_specs=state_specs + row_specs + [whole((1, 1))],
    )(grad_in, grad_out, grad_vec, norm, output, token_grad, *state)
    new_w_in, new_m_in, new_v_in, new_w_out, new_m_out, new_v_out = new[:6]
    new_vectors, new_m_vec, new_v_vec, output, token_grad, norm = new[6:]
    return (
        output.reshape(frames, here, width),
        token_grad.reshape(frames, here, width),
        norm.reshape(()),
        by_slot(new_w_in),
        new_w_out,
        of_tile(new_vectors),
        by_slot(new_m_in),
        new_m_out,
        of_tile(new_m_vec),
        by_slot(new_v_in),
        new_v_out,
        of_tile(new_v_vec),
    )


def solution(mesh):
    in_specs = (
        P(DP, TP, None),
        P(DP, TP),
        P(DP, TP, None),
        P(DP, None, TP),
        P(None, TP, DP),
        P(None, DP),
        P(DP, None, TP),
        P(None, TP, DP),
        P(None, DP),
        P(DP, None, TP),
        P(None, TP, DP),
        P(None, DP),
    )
    out_specs = (P(DP, TP, None), P(DP, TP, None), P()) + in_specs[3:]
    return jax.shard_map(local, mesh=mesh, in_specs=in_specs, out_specs=out_specs, check_vma=False)
```

```python
import functools
from types import SimpleNamespace

import jax
import jax.numpy as jnp
from jax import lax
from jax.experimental import pallas as pl
from jax.experimental.pallas import tpu as pltpu
from jax.sharding import PartitionSpec as P

FRAMES = 16
STEP = 10
HDIM = 64


EPS_NORM = 1e-05
CLIP_AT = 1.0
BETA_FIRST = 0.9
BETA_SECOND = 0.95
ADAM_EPS = 1e-08
DECAY_RATE = 0.1
RATE_INPUT = 0.02
RATE_OUTPUT = 0.08
RATE_VECTOR = 1.0
NEG_FILL = -1e30
GELU_A = 0.7978845608028654
GELU_B = 0.044715

F32 = jnp.float32
B16 = jnp.bfloat16
MESH = pl.DeviceIdType.MESH
CHUNK = 16
DP = "dp"
TP = "fsdp"
LANES = 128
VMEM_BYTES = 63 << 20


def at(dp, fsdp):
    return {DP: dp, TP: fsdp}


def nn(a, b):
    return lax.dot_general(a, b, (((1,), (0,)), ((), ())), preferred_element_type=F32)


def nt(a, b):
    return lax.dot_general(a, b, (((1,), (1,)), ((), ())), preferred_element_type=F32)


def tn(a, b):
    return lax.dot_general(a, b, (((0,), (0,)), ((), ())), preferred_element_type=F32)


def loop(low, high, step):
    def body(k, carry):
        step(k)
        return carry

    lax.fori_loop(low, high, body, 0)


def each(low, high, step):
    if high - low <= 8:
        for k in range(low, high):
            step(k)
    else:
        loop(low, high, step)


def scratch_of(z):
    rows, width, hidden, span = z.rows, z.width, z.hidden, z.span
    nd, nf, part, heads = z.nd, z.nf, z.part, z.heads
    outer = nd // 2
    flat = (nf, z.frames, z.here, hidden)
    vmem = pltpu.VMEM
    dma = pltpu.SemaphoreType.DMA
    return dict(
        stage_in=vmem((10, part, hidden), F32),
        stage_out=vmem((6, hidden, part), F32),
        shard=vmem((4, 4, part, hidden), B16),
        tile=vmem((8, LANES), F32),
        masked=vmem((rows, LANES), F32),
        weights=vmem((4, 4, width, hidden), B16),
        gathered=vmem((6, nf, rows, width), B16),
        gains=vmem((8, width), F32),
        tiles=vmem((nd, 8, LANES), F32),
        hats=vmem((3, rows, width), F32),
        rstds=vmem((3, rows, LANES), F32),
        work=vmem((rows, width), F32),
        mid=vmem((rows, width), F32),
        swap_out=vmem((4, span, CHUNK, width), B16),
        swap_in=vmem((4, span, CHUNK, width), B16),
        part_sum=vmem((2, 2, rows, width), F32),
        sib_out=vmem((2, 2, rows, width), B16),
        sib_in=vmem((2, 2, rows, width), B16),
        far_out=vmem((2, rows, width), B16),
        far_in=vmem((2, rows, width), B16),
        qkv=vmem((2, 3) + flat, B16),
        mixed=vmem((2,) + flat, B16),
        grad_mixed=vmem(flat, B16),
        grad_qkv=vmem((3,) + flat, B16),
        probs_a=vmem((z.frames * heads, nf * z.here, nf * z.here), F32),
        probs_b=vmem((nf * heads, rows, rows), F32),
        act=vmem((4,) + flat, B16),
        slope=vmem((4,) + flat, F32),
        grad_pre=vmem((4,) + flat, B16),
        product=vmem((outer, 2, part, hidden), F32),
        own_sum=vmem((16, outer, part, hidden), B16),
        pair_out=vmem((16, outer, part, hidden), B16),
        pair_in=vmem((16, outer, part, hidden), B16),
        line_in=vmem((16, outer, part, hidden), B16),
        vec_acc=vmem((8, width), F32),
        vec_out=vmem((width // LANES, 8, LANES), F32),
        vec_in=vmem((nd, 8, LANES), F32),
        vec_mine=vmem((8, LANES), F32),
        vec_side=vmem((nf, 8, LANES), F32),
        sq_mine=vmem((2, 8, LANES), F32),
        sq_side=vmem((nf, 8, LANES), F32),
        sq_all=vmem((nd, 8, LANES), F32),
        small_s=dma((5,)),
        small_r=dma((5,)),
        line_ws=dma((4,)),
        line_wr=dma((4, outer)),
        pair_ws=dma((4,)),
        pair_wr=dma((4,)),
        pair_wo=dma((4,)),
        own_ws=dma((4,)),
        near_ws=dma((4,)),
        near_wr=dma((4,)),
        far_ws=dma((4,)),
        copy_w=dma((4,)),
        row_s=dma((6, 5)),
        row_r=dma((6, 5)),
        sum_s=dma((6, 5)),
        sum_r=dma((6, 5)),
        swap_s=dma((4,)),
        swap_r=dma((4,)),
        stage_s=dma((16,)),
        pair_gs=dma((16,)),
        pair_gr=dma((16,)),
        line_gs=dma((16,)),
        line_gr=dma((16,)),
    )


def layer(z, names, *refs):
    tok, msk, cot, w_in, w_out, vec = refs[:6]
    out, tgr, nrm, gin, gout, gvec = refs[6:12]
    s = SimpleNamespace(**dict(zip(names, refs[12:])))
    rows, width, hidden, span = z.rows, z.width, z.hidden, z.span
    nd, nf, part, heads = z.nd, z.nf, z.part, z.heads
    frames, here = z.frames, z.here
    outer = nd // 2
    piece = here // span
    n_pairs = heads // 2
    scale = HDIM**-0.5
    gathered, weights, gains = s.gathered, s.weights, s.gains
    work, mid, shard = s.work, s.mid, s.shard
    swap_out, swap_in = s.swap_out, s.swap_in

    d, f = lax.axis_index(DP), lax.axis_index(TP)
    o, i = d // 2, d % 2
    y, c = f // 2, f % 2
    place = d % span
    base = d - place
    f_sib, f_far, f_last = y * 2 + 1 - c, (1 - y) * 2 + c, (1 - y) * 2 + 1 - c
    mate = at(o * 2 + 1 - i, f)
    sib = at(d, f_sib)
    far = at(d, f_far)

    def rcopy(src, dst, ssem, rsem, dev):
        return pltpu.make_async_remote_copy(
            src_ref=src, dst_ref=dst, send_sem=ssem, recv_sem=rsem, device_id=dev, device_id_type=MESH
        )

    in_slots = {0: [0, 1, 2], 1: [3, 4, 5], 2: [6, 7, 8, 9], 3: []}
    out_slots = {0: [0], 1: [1], 2: [], 3: [2, 3, 4, 5]}

    def stage(g):
        for n in in_slots[g]:
            yield pltpu.make_async_copy(w_in.at[n], s.stage_in.at[n], s.stage_s.at[n])
        for n in out_slots[g]:
            yield pltpu.make_async_copy(w_out.at[n], s.stage_out.at[n], s.stage_s.at[10 + n])

    def round_group(g):
        for cp in stage(g):
            cp.wait()
        for j, n in enumerate(in_slots[g]):
            shard[g, j] = s.stage_in[n].astype(B16)
        for j, n in enumerate(out_slots[g]):
            shard[g, len(in_slots[g]) + j] = s.stage_out[n].T.astype(B16)

    for g in range(4):
        for cp in stage(g):
            cp.start()
    s.tile[...] = jnp.zeros_like(s.tile)
    s.tile[0:4, :] = vec[...].astype(B16).astype(F32)

    same = lax.broadcasted_iota(jnp.int32, (here, here), 0) == lax.broadcasted_iota(
        jnp.int32, (here, here), 1
    )
    for fr in range(frames):
        line = jnp.broadcast_to(msk[fr : fr + 1, :], (here, here)).astype(F32)
        column = jnp.sum(jnp.where(same, line, 0.0), axis=1, keepdims=True)
        s.masked[fr * here : (fr + 1) * here, :] = jnp.broadcast_to(column, (here, LANES))

    bar = pltpu.get_barrier_semaphore()

    def greet(q):
        dev = at((d + q) % nd, f)
        pl.semaphore_signal(bar, inc=1, device_id=dev, device_id_type=MESH)

    each(1, nd, greet)
    for q in range(1, nf):
        dev = at(d, (f + q) % nf)
        pl.semaphore_signal(bar, inc=1, device_id=dev, device_id_type=MESH)
    pl.semaphore_wait(bar, nd - 1 + nf - 1)


    def tell(n, src_of, dst, axis):
        count, me = (nd, d) if axis == DP else (nf, f)

        def go(q):
            to = (me + q) % count
            dev = at(to, f) if axis == DP else at(d, to)
            rcopy(src_of(to), dst.at[me], s.small_s.at[n], s.small_r.at[n], dev).start()

        each(1, count, go)

    def hear(n, dst, axis):
        count = nd if axis == DP else nf
        others = dst.at[pl.ds(0, count - 1)]
        cp = rcopy(others, others, s.small_s.at[n], s.small_r.at[n], mate)
        cp.wait_recv()
        cp.wait_send()

    def total_of(ref, count):
        total = ref[0]
        if count <= 8:
            for k in range(1, count):
                total = total + ref[k]
            return total
        return lax.fori_loop(1, count, lambda k, t: t + ref[k], total)

    tell(0, lambda to: s.tile, s.tiles, DP)

    four = outer == 4
    near_row = o + 1 - 2 * (o % 2)
    next_row = jnp.where(o < 2, 2, 1)
    last_row = jnp.where(o < 2, 3, 0)
    middle = (o == 1) | (o == 2)

    def shard_rows(owner):
        return pl.ds(pl.multiple_of(owner * part, part), part)

    def shard_of(g, row, col):
        return weights.at[g, :, shard_rows(row * 2 + col), :]

    def gather_own(g):
        mine = shard_of(g, o, i)
        pltpu.make_async_copy(shard.at[g], mine, s.copy_w.at[g]).start()
        rcopy(shard.at[g], mine, s.own_ws.at[g], s.pair_wo.at[g], mate).start()

    def gather_line(g, low, high):
        def go(q):
            to = (o + q) % outer

            def start():
                rcopy(
                    shard.at[g],
                    shard_of(g, o, i),
                    s.line_ws.at[g],
                    s.line_wr.at[g, o],
                    at(to * 2 + i, f),
                ).start()

            if four:
                pl.when(jnp.abs(to - o) < 3)(start)
            else:
                start()

        each(low, high, go)

    def gather_from(g, row):
        block = shard_of(g, row, i)
        rcopy(block, block, s.line_ws.at[g], s.line_wr.at[g, row], mate).wait_recv()
        return block

    def gather_pass(g, low, high):
        if not four:

            def go(q):
                block = gather_from(g, (o + outer - q) % outer)
                rcopy(block, block, s.pair_ws.at[g], s.pair_wr.at[g], mate).start()

            each(low, high, go)
            return
        for q in range(low, high):
            if q == 1:
                block = shard_of(g, o, 1 - i)
                rcopy(block, block, s.pair_ws.at[g], s.pair_wo.at[g], mate).wait_recv()
                half = block.at[pl.ds(2, 2)]
                dev = at(near_row * 2 + i, f)
                rcopy(half, half, s.near_ws.at[g], s.near_wr.at[g], dev).start()
                half = gather_from(g, near_row).at[pl.ds(0, 2)]
                rcopy(half, half, s.pair_ws.at[g], s.pair_wr.at[g], mate).start()
            else:
                row = next_row if q == 2 else last_row
                block = gather_from(g, row)

                @pl.when(middle & (row == last_row))
                def _():
                    dev = at((3 - last_row) * 2 + i, f)
                    rcopy(block, block, s.far_ws.at[g], s.line_wr.at[g, row], dev).start()

                rcopy(block, block, s.pair_ws.at[g], s.pair_wr.at[g], mate).start()

    def gather_ready(g):
        mine = shard_of(g, o, i)
        pltpu.make_async_copy(shard.at[g], mine, s.copy_w.at[g]).wait()
        if not four:
            block = shard_of(g, o, 1 - i)
            rcopy(block, block, s.pair_ws.at[g], s.pair_wo.at[g], mate).wait_recv()
        if four:
            half = weights.at[g, pl.ds(0, 2), pl.ds(0, part), :]
            rcopy(half, half, s.near_ws.at[g], s.near_wr.at[g], mate).wait_recv()
        halves = 5 if four else 2 * (outer - 1)
        both = half_shards(g, halves)
        rcopy(both, both, s.pair_ws.at[g], s.pair_wr.at[g], mate).wait_recv()

    def half_shards(g, count):
        return weights.at[g, pl.ds(0, 2), pl.ds(0, count * part), :]

    def gather_end(g):
        def sent(sem, halves):
            both = half_shards(g, halves)
            rcopy(both, both, sem.at[g], s.pair_wr.at[g], mate).wait_send()

        if not four:
            sent(s.pair_ws, nd - 2)
            sent(s.line_ws, nd - 2)
            rest = shard_of(g, o, i)
            rcopy(rest, rest, s.own_ws.at[g], s.pair_wr.at[g], mate).wait_send()
            return
        sent(s.own_ws, 2)
        sent(s.pair_ws, 5)
        sent(s.near_ws, 1)

        @pl.when(middle)
        def _():
            sent(s.line_ws, 6)
            sent(s.far_ws, 2)

        @pl.when(jnp.logical_not(middle))
        def _():
            sent(s.line_ws, 4)

    def half_rows(h):
        return pl.ds(h * here, here)


    def spread_start(k, h):
        half = gathered.at[k, f, half_rows(h)]
        rcopy(half, half, s.row_s.at[k, 1 + h], s.row_r.at[k, 1 + h], far).start()
        if h == 1:
            block = gathered.at[k, f]
            rcopy(block, block, s.row_s.at[k, 0], s.row_r.at[k, 0], sib).start()

    def spread_near(k):
        block = gathered.at[k, f_sib]
        rcopy(block, block, s.row_s.at[k, 0], s.row_r.at[k, 0], sib).wait_recv()

    def spread_pass(k):
        for h in range(2):
            half = gathered.at[k, f_far, half_rows(h)]
            rcopy(half, half, s.row_s.at[k, 1 + h], s.row_r.at[k, 1 + h], far).wait_recv()
            rcopy(half, half, s.row_s.at[k, 3 + h], s.row_r.at[k, 3 + h], sib).start()

    def spread_far(k):
        for h in range(2):
            half = gathered.at[k, f_last, half_rows(h)]
            rcopy(half, half, s.row_s.at[k, 3 + h], s.row_r.at[k, 3 + h], sib).wait_recv()

    def spread_end(k):
        block = gathered.at[k, f]
        rcopy(block, block, s.row_s.at[k, 0], s.row_r.at[k, 0], sib).wait_send()
        half = gathered.at[k, f, half_rows(0)]
        for n in range(1, 5):
            rcopy(half, half, s.row_s.at[k, n], s.row_r.at[k, n], sib).wait_send()


    def partial(terms, pick, slot, part_rows):
        for t in range(width // hidden):
            cols = slice(t * hidden, (t + 1) * hidden)
            total = None
            for b_ref, g, j in terms:
                b = pick(b_ref)
                value = nt(b, weights[g, j, cols, :])
                total = value if total is None else total + value
            s.part_sum[slot, :, part_rows, cols] = total.reshape(2, -1, hidden)

    def collect_start(k, terms):
        par = k % 2

        def to_sib(slot, part_rows, n):
            s.sib_out[par, slot, part_rows] = s.part_sum[slot, 1 - c, part_rows].astype(B16)
            rcopy(
                s.sib_out.at[par, slot, part_rows],
                s.sib_in.at[par, slot, part_rows],
                s.sum_s.at[k, n],
                s.sum_r.at[k, n],
                sib,
            ).start()

        for h in range(2):

            def remote(ref, h=h):
                return ref[pl.ds((1 - y) * 2, 2), h].reshape(2 * here, hidden)

            partial(terms, remote, 0, half_rows(h))
            to_sib(0, half_rows(h), h)
        for h in range(2):
            half = half_rows(h)
            back = s.sib_in.at[par, 0, half]
            rcopy(back, back, s.sum_s.at[k, h], s.sum_r.at[k, h], sib).wait_recv()
            total = s.part_sum[0, c, half] + s.sib_in[par, 0, half].astype(F32)
            s.far_out[par, half] = total.astype(B16)
            rcopy(
                s.far_out.at[par, half],
                s.far_in.at[par, half],
                s.sum_s.at[k, 3 + h],
                s.sum_r.at[k, 3 + h],
                far,
            ).start()
        partial(
            terms, lambda ref: ref[pl.ds(y * 2, 2)].reshape(2 * rows, hidden), 1, pl.ds(0, rows)
        )
        to_sib(1, pl.ds(0, rows), 2)

    def collect_end(k, h):
        par = k % 2
        half = half_rows(h)
        if h == 0:
            near = s.sib_in.at[par, 1]
            rcopy(near, near, s.sum_s.at[k, 2], s.sum_r.at[k, 2], sib).wait_recv()
            rcopy(near, near, s.sum_s.at[k, 2], s.sum_r.at[k, 2], sib).wait_send()
        away = s.far_in.at[par, half]
        rcopy(away, away, s.sum_s.at[k, 3 + h], s.sum_r.at[k, 3 + h], far).wait_recv()
        for n in (h, 3 + h):
            rcopy(away, away, s.sum_s.at[k, n], s.sum_r.at[k, n], sib).wait_send()

    def collected(k, block):
        par = k % 2
        return (
            s.part_sum[1, c, block]
            + s.sib_in[par, 1, block].astype(F32)
            + s.far_in[par, block].astype(F32)
        )


    def swap_start(k):
        def go(q):
            to = (place + q) % span
            rcopy(
                swap_out.at[k, to],
                swap_in.at[k, place],
                s.swap_s.at[k],
                s.swap_r.at[k],
                at(base + to, f),
            ).start()

        each(1, span, go)
        swap_in[k, place] = swap_out[k, place]

    def swap_wait(k):
        others = swap_in.at[k, pl.ds(0, span - 1)]
        rcopy(others, others, s.swap_s.at[k], s.swap_r.at[k], mate).wait_recv()

    def swap_end(k):
        others = swap_in.at[k, pl.ds(0, span - 1)]
        rcopy(others, others, s.swap_s.at[k], s.swap_r.at[k], mate).wait_send()

    def token_rows(fr, j):
        return pl.ds(pl.multiple_of(fr * here + j * piece, piece), piece)

    def pack(k, src):
        def step(j):
            parts = [src[token_rows(fr, j), :] for fr in range(frames)]
            swap_out[k, j] = jnp.concatenate(parts, axis=0).astype(B16)

        loop(0, span, step)

    def unpack(k, dst):
        def step(j):
            value = swap_in[k, j].astype(F32)
            for fr in range(frames):
                dst[token_rows(fr, j), :] = value[fr * piece : (fr + 1) * piece]

        loop(0, span, step)

    def chunks(step, h):
        first = h * here // CHUNK
        each(first, first + here // CHUNK, lambda k: step(pl.ds(k * CHUNK, CHUNK), k))

    def norm_rows(n, value, block):
        centered = value - jnp.mean(value, axis=-1, keepdims=True)
        rstd = lax.rsqrt(jnp.mean(centered * centered, axis=-1, keepdims=True) + EPS_NORM)
        hat = centered * rstd
        s.hats[n, block] = hat
        s.rstds[n, block] = jnp.broadcast_to(rstd, (CHUNK, LANES))
        return (hat * gains[n : n + 1, :]).astype(B16)

    def norm_back(n, grad, block):
        hat = s.hats[n, block]
        rstd = s.rstds[n, block][:, 0:1]
        grad_hat = grad * gains[n : n + 1, :]
        first = jnp.mean(grad_hat, axis=-1, keepdims=True)
        second = jnp.mean(grad_hat * hat, axis=-1, keepdims=True)
        s.vec_acc[n : n + 1, :] += jnp.sum(grad * hat, axis=0, keepdims=True)
        return rstd * (grad_hat - first - hat * second)


    def pair_rows(k, pair):
        return gathered[k, pl.ds(pair * 2, 2)].reshape(2 * rows, width)

    def as_flat(value):
        return value.reshape(2, frames, here, hidden)

    def project(k, g, dst, pair):
        def step(j):
            dst[j, pl.ds(pair * 2, 2)] = as_flat(nn(pair_rows(k, pair), weights[g, j]).astype(B16))

        each(0, 3, step)

    def attend(block):
        spatial = block == 0
        n = nf * here if spatial else rows

        def load(ref, g, lanes):
            value = ref[:, g, :, lanes] if spatial else ref[g, :, :, lanes]
            return value.reshape(n, 2 * HDIM)

        def store(ref, g, lanes, value):
            if spatial:
                ref[:, g, :, lanes] = value.reshape(nf, here, 2 * HDIM)
            else:
                ref[g, :, :, lanes] = value.reshape(frames, here, 2 * HDIM)

        return n, load, store, (s.probs_a if spatial else s.probs_b)

    def head_lanes(n):
        return lax.broadcasted_iota(jnp.int32, (n, 2 * HDIM), 1) < HDIM

    def kept(n):
        query = lax.broadcasted_iota(jnp.int32, (n, n), 0)
        key = lax.broadcasted_iota(jnp.int32, (n, n), 1)
        return (query % piece == key % piece) & (key // piece <= query // piece)

    def each_pair(block, step):
        def go(k):
            first = (k % n_pairs) * 2 * HDIM
            step(k, k // n_pairs, slice(first, first + 2 * HDIM))

        each(0, (frames if block == 0 else nf) * n_pairs, go)

    def attention(block):
        n, load, store, probs = attend(block)
        qkv = s.qkv.at[block]

        def step(k, g, lanes):
            query, key, value = (load(qkv.at[j], g, lanes) for j in range(3))
            low = head_lanes(n)
            found = []
            for h in range(2):
                mine = jnp.where(low if h == 0 else ~low, query, jnp.zeros_like(query))
                scores = nt(mine, key) * scale
                if block == 1:
                    scores = jnp.where(kept(n), scores, NEG_FILL)
                expd = jnp.exp(scores - jnp.max(scores, axis=-1, keepdims=True))
                prob = expd / jnp.sum(expd, axis=-1, keepdims=True)
                probs[k * 2 + h] = prob
                found.append(nn(prob.astype(B16), value))
            store(s.mixed.at[block], g, lanes, jnp.where(low, found[0], found[1]).astype(B16))

        each_pair(block, step)

    def attention_back(block):
        n, load, store, probs = attend(block)
        qkv = s.qkv.at[block]

        def step(k, g, lanes):
            query, key, value = (load(qkv.at[j], g, lanes) for j in range(3))
            grad = load(s.grad_mixed, g, lanes)
            low = head_lanes(n)
            found = []
            for h in range(2):
                mine = jnp.where(low if h == 0 else ~low, grad, jnp.zeros_like(grad))
                prob = probs[k * 2 + h]
                grad_prob = nt(mine, value)
                inner = jnp.sum(prob * grad_prob, axis=-1, keepdims=True)
                grad_score = (prob * (grad_prob - inner)).astype(B16)
                found.append(
                    (
                        nn(grad_score, key) * scale,
                        tn(grad_score, query) * scale,
                        tn(prob.astype(B16), grad),
                    )
                )
            for j in range(3):
                both = jnp.where(low, found[0][j], found[1][j]).astype(B16)
                store(s.grad_qkv.at[j], g, lanes, both)

        each_pair(block, step)

    def mixed_back(k, g):
        def half(pair):
            value = nn(pair_rows(k, pair), weights[g, 3])
            s.grad_mixed[pl.ds(pair * 2, 2)] = as_flat(value.astype(B16))

        spread_near(k)
        half(y)
        spread_pass(k)
        spread_far(k)
        half(1 - y)


    def slot_make(slot, k, b_ref):
        value = tn(gathered[k].reshape(nf * rows, width), b_ref[...].reshape(nf * rows, hidden))
        s.product[...] = value.reshape(outer, 2, part, hidden)
        s.pair_out[slot] = s.product[:, 1 - i].astype(B16)
        s.own_sum[slot] = s.product[:, i].astype(B16)

    def slot_send(slot):
        rcopy(
            s.pair_out.at[slot],
            s.pair_in.at[slot],
            s.pair_gs.at[slot],
            s.pair_gr.at[slot],
            mate,
        ).start()

    def slot_sum(slot):
        g, j = slot // 4, slot % 4
        if g < 2:
            return gin.at[g * 3 + j] if j < 3 else gout.at[g]
        return gin.at[6 + j] if g == 2 else gout.at[2 + j]

    def slot_pass(slot):
        block = s.pair_in.at[slot]
        cp = rcopy(block, block, s.pair_gs.at[slot], s.pair_gr.at[slot], mate)
        cp.wait_recv()
        cp.wait_send()

        def both(owner):
            return s.own_sum[slot, owner].astype(F32) + s.pair_in[slot, owner].astype(F32)

        def go(q):
            to = (o + q) % outer
            s.pair_out[slot, q] = both(to).astype(B16)
            rcopy(
                s.pair_out.at[slot, q],
                s.line_in.at[slot, q],
                s.line_gs.at[slot],
                s.line_gr.at[slot],
                at(to * 2 + i, f),
            ).start()

        each(1, outer, go)
        slot_sum(slot)[...] = both(o)

    def slot_end(slot):
        block = s.line_in.at[slot, pl.ds(1, outer - 1)]
        cp = rcopy(block, block, s.line_gs.at[slot], s.line_gr.at[slot], mate)
        cp.wait_recv()
        cp.wait_send()
        total = slot_sum(slot)[...]
        if outer <= 8:
            for q in range(1, outer):
                total = total + s.line_in[slot, q].astype(F32)
        else:
            total = lax.fori_loop(
                1, outer, lambda q, t: t + s.line_in[slot, q].astype(F32), total
            )
        slot_sum(slot)[...] = total
        folded = jnp.sum((total * total).reshape(part // 8, 8, hidden), axis=0)
        for k in range(hidden // LANES):
            s.sq_mine[0] += folded[:, k * LANES : (k + 1) * LANES]

    round_group(0)
    gather_line(0, 1, outer)
    gather_own(0)
    hear(0, s.tiles, DP)
    s.tiles[d] = s.tile[...]
    per_tile = LANES // part
    for k in range(width // LANES):
        gains[:, k * LANES : (k + 1) * LANES] = total_of(
            s.tiles.at[pl.ds(k * per_tile, per_tile)], per_tile
        )
    s.vec_acc[...] = jnp.zeros_like(s.vec_acc)
    s.sq_mine[...] = jnp.zeros_like(s.sq_mine)

    def masked_rows(block):
        return jnp.broadcast_to(s.masked[block, 0:1], (CHUNK, width)) > 0.5

    def first_norm(block, k):
        value = jnp.where(masked_rows(block), gains[3:4, :], tok[block, :].astype(F32))
        work[block, :] = value
        gathered[0, f, block] = norm_rows(0, value, block)

    for h in range(2):
        chunks(first_norm, h)
        spread_start(0, h)
    round_group(1)
    gather_line(1, 1, outer)
    gather_own(1)
    gather_pass(0, 1, 2)

    def widen(block, k):
        s.part_sum[0, 0, block, :] = cot[block, :].astype(F32)

    for h in range(2):
        chunks(widen, h)
    pack(0, s.part_sum.at[0, 0])
    swap_start(0)

    gather_pass(0, 2, outer - 1)
    spread_near(0)
    spread_pass(0)
    gather_pass(0, outer - 1, outer)
    round_group(2)
    gather_ready(0)
    project(0, 0, s.qkv.at[0], y)
    spread_far(0)
    project(0, 0, s.qkv.at[0], 1 - y)
    gather_pass(1, 1, 2)
    attention(0)
    gather_pass(1, 2, outer - 1)
    collect_start(0, [(s.mixed.at[0], 0, 3)])
    gather_pass(1, outer - 1, outer)
    round_group(3)

    def take_branch(block, k):
        work[block, :] = work[block, :] + collected(0, block)

    for h in range(2):
        collect_end(0, h)
        chunks(take_branch, h)
    pack(1, work)
    swap_start(1)
    gather_line(2, 1, outer)
    gather_line(3, 1, outer)
    gather_own(2)
    gather_own(3)

    swap_wait(0)
    gathered[1, f] = swap_in[0].reshape(rows, width)
    spread_start(1, 0)
    spread_start(1, 1)
    swap_wait(1)

    def second_norm(block, k):
        value = swap_in[1, k].astype(F32)
        mid[block, :] = value
        gathered[2, f, block] = norm_rows(1, value, block)

    for h in range(2):
        chunks(second_norm, h)
        spread_start(2, h)
    spread_near(1)
    spread_pass(1)
    gather_ready(1)
    spread_near(2)
    project(2, 1, s.qkv.at[1], y)
    gather_pass(2, 1, 2)
    spread_pass(2)
    gather_pass(2, 2, outer - 1)
    spread_far(2)
    project(2, 1, s.qkv.at[1], 1 - y)
    attention(1)
    gather_pass(2, outer - 1, outer)
    collect_start(1, [(s.mixed.at[1], 1, 3)])
    gather_pass(3, 1, 2)

    def third_norm(block, k):
        value = mid[block, :] + collected(1, block)
        mid[block, :] = value
        gathered[3, f, block] = norm_rows(2, value, block)

    for h in range(2):
        collect_end(1, h)
        chunks(third_norm, h)
        spread_start(3, h)
    spread_far(1)
    gather_pass(3, 2, outer - 1)


    def up(pair):
        def step(n):
            u = nn(pair_rows(3, pair), weights[2, n])
            t = jnp.tanh(GELU_A * (u + GELU_B * u * u * u))
            half = 0.5 * (1.0 + t)
            s.act[n, pl.ds(pair * 2, 2)] = as_flat((u * half).astype(B16))
            bend = GELU_A * (1.0 + 3.0 * GELU_B * u * u)
            s.slope[n, pl.ds(pair * 2, 2)] = as_flat(half + 0.5 * u * (1.0 - t * t) * bend)

        each(0, 4, step)

    def down(pair):
        def step(n):
            grad = nn(pair_rows(1, pair), weights[3, n])
            slope = s.slope[n, pl.ds(pair * 2, 2)].reshape(2 * rows, hidden)
            s.grad_pre[n, pl.ds(pair * 2, 2)] = as_flat((grad * slope).astype(B16))

        each(0, 4, step)

    gather_ready(2)
    spread_near(3)
    up(y)
    spread_pass(3)
    gather_pass(3, outer - 1, outer)
    spread_far(3)
    up(1 - y)
    each(0, 4, lambda n: slot_make(12 + n, 1, s.act.at[n]))
    slot_send(12)
    slot_send(13)
    gather_ready(3)

    down(1 - y)
    down(y)
    slot_make(8, 3, s.grad_pre.at[0])
    slot_send(8)
    collect_start(2, [(s.grad_pre.at[n], 2, n) for n in range(4)])
    slot_pass(12)
    each(1, 4, lambda n: slot_make(8 + n, 3, s.grad_pre.at[n]))
    slot_send(9)
    slot_send(14)
    slot_send(10)
    slot_send(15)
    slot_send(11)
    slot_pass(13)

    def third_back(block, k):
        value = swap_in[0, k].astype(F32) + norm_back(2, collected(2, block), block)
        work[block, :] = value
        gathered[4, f, block] = value.astype(B16)

    for h in range(2):
        collect_end(2, h)
        chunks(third_back, h)
        spread_start(4, h)
    slot_pass(8)
    collect_start(3, [(s.act.at[n], 3, n) for n in range(4)])
    slot_pass(9)

    mixed_back(4, 1)
    slot_make(7, 4, s.mixed.at[1])
    slot_pass(14)
    slot_send(7)

    def take_output(block, k):
        swap_out[2, k] = (mid[block, :] + collected(3, block)).astype(B16)

    for h in range(2):
        collect_end(3, h)
        chunks(take_output, h)
    swap_start(2)
    attention_back(1)
    slot_pass(10)
    collect_start(4, [(s.grad_qkv.at[j], 1, j) for j in range(3)])
    slot_pass(15)
    each(0, 3, lambda j: slot_make(4 + j, 2, s.grad_qkv.at[j]))

    def second_back(block, k):
        swap_out[3, k] = (work[block, :] + norm_back(1, collected(4, block), block)).astype(B16)

    for h in range(2):
        collect_end(4, h)
        chunks(second_back, h)
    swap_start(3)
    slot_pass(11)
    slot_send(4)
    slot_send(5)
    slot_send(6)

    swap_wait(3)
    unpack(3, work)

    def take_carry(block, k):
        gathered[5, f, block] = work[block, :].astype(B16)

    for h in range(2):
        chunks(take_carry, h)
        spread_start(5, h)
    slot_pass(7)
    mixed_back(5, 0)
    slot_make(3, 5, s.mixed.at[0])
    slot_send(3)
    attention_back(0)

    def spatial_slot(j):
        slot_make(j, 0, s.grad_qkv.at[j])
        slot_send(j)

    loop(0, 3, spatial_slot)
    slot_pass(4)
    slot_pass(5)
    collect_start(5, [(s.grad_qkv.at[j], 0, j) for j in range(3)])
    slot_pass(6)
    slot_pass(3)

    def first_back(block, k):
        value = work[block, :] + norm_back(0, collected(5, block), block)
        masked = masked_rows(block)
        tgr[block, :] = jnp.where(masked, 0.0, value).astype(B16)
        s.vec_acc[3:4, :] += jnp.sum(jnp.where(masked, value, 0.0), axis=0, keepdims=True)

    for h in range(2):
        collect_end(5, h)
        chunks(first_back, h)

    for k in range(width // LANES):
        s.vec_out[k] = s.vec_acc[:, k * LANES : (k + 1) * LANES]
    tell(1, lambda to: s.vec_out.at[(to * part) // LANES], s.vec_in, DP)
    s.vec_in[d] = s.vec_out[(d * part) // LANES]
    slot_pass(0)
    swap_wait(2)
    unpack(2, mid)

    def give_output(block, k):
        out[block, :] = mid[block, :].astype(B16)

    for h in range(2):
        chunks(give_output, h)
    each(8, 16, slot_end)
    slot_pass(1)
    hear(1, s.vec_in, DP)
    s.vec_mine[...] = total_of(s.vec_in, nd)
    tell(2, lambda to: s.vec_mine, s.vec_side, TP)
    s.vec_side[f] = s.vec_mine[...]
    each(4, 8, slot_end)
    slot_end(3)
    slot_pass(2)
    hear(2, s.vec_side, TP)
    grad_vec = total_of(s.vec_side, nf)
    gvec[...] = grad_vec
    each(0, 3, slot_end)

    lane = lax.broadcasted_iota(jnp.int32, (8, LANES), 1)
    first_lane = (d * part) % LANES
    owned = (lane >= first_lane) & (lane < first_lane + part)
    s.sq_mine[0] += jnp.where(owned, grad_vec * grad_vec, 0.0) * (1.0 / nf)
    tell(3, lambda to: s.sq_mine.at[0], s.sq_side, TP)
    s.sq_side[f] = s.sq_mine[0]
    hear(3, s.sq_side, TP)
    s.sq_mine[1] = total_of(s.sq_side, nf)
    tell(4, lambda to: s.sq_mine.at[1], s.sq_all, DP)
    s.sq_all[d] = s.sq_mine[1]
    for g in range(4):
        gather_end(g)
    for k in range(6):
        spread_end(k)
    for k in range(4):
        swap_end(k)
    hear(4, s.sq_all, DP)
    total = jnp.sum(total_of(s.sq_all, nd), keepdims=True)
    nrm[...] = jnp.broadcast_to(jnp.sqrt(total), (8, LANES))


def adamw_step(weight, first, second, grad, rate):
    first = BETA_FIRST * first + (1.0 - BETA_FIRST) * grad
    second = BETA_SECOND * second + (1.0 - BETA_SECOND) * grad * grad
    fix_first = 1.0 / (1.0 - BETA_FIRST**STEP)
    fix_second = 1.0 / (1.0 - BETA_SECOND**STEP)
    update = (rate * fix_first) * first / (jnp.sqrt(second * fix_second) + ADAM_EPS)
    return (weight * (1.0 - rate * DECAY_RATE) - update, first, second)


def updates(*refs):
    grad_in, grad_out, grad_vec, norm, out, tgr = refs[:6]
    state = refs[6:15]
    new = refs[15:24]
    new_out, new_tgr, new_norm = refs[24:]
    j = pl.program_id(0)
    grad_norm = norm[0:1, 0:1]
    factor = CLIP_AT / jnp.maximum(grad_norm, CLIP_AT)

    def update(n, grad, rate):
        values = adamw_step(*(state[3 * n + k][...] for k in range(3)), grad * factor, rate)
        for k in range(3):
            new[3 * n + k][...] = values[k]

    update(0, grad_in[...], RATE_INPUT)

    update(1, jnp.stack([grad_out[n].T for n in range(3)]), RATE_OUTPUT)

    @pl.when(j == 1)

    def _():
        update(2, grad_vec[0:4, :], RATE_VECTOR)
        new_out[...] = out[...]
        new_tgr[...] = tgr[...]
        new_norm[...] = grad_norm


def local(tokens, masks, cotangent, w_in, w_out, vectors, m_in, m_out, m_vec, v_in, v_out, v_vec):
    frames, here, width = tokens.shape
    part, _, hidden = w_in.shape
    nd, nf = lax.axis_size(DP), lax.axis_size(TP)
    z = SimpleNamespace(
        rows=frames * here,
        width=width,
        hidden=hidden,
        span=FRAMES // frames,
        nd=nd,
        nf=nf,
        part=part,
        heads=hidden // HDIM,
        frames=frames,
        here=here,
    )
    rows = frames * here
    lane0 = (lax.axis_index(DP) * part) % LANES

    def as_tile(value):
        if part == LANES:
            return value
        return lax.dynamic_update_slice(jnp.zeros((4, LANES), F32), value, (0, lane0))

    def of_tile(value):
        return value if part == LANES else lax.dynamic_slice(value, (0, lane0), (4, part))

    def by_slot(value):
        return value.transpose(1, 0, 2)

    vec = as_tile(vectors)
    scratch = scratch_of(z)
    in_vmem = pl.BlockSpec(memory_space=pltpu.VMEM)
    output, token_grad, norm, grad_in, grad_out, grad_vec = pl.pallas_call(
        functools.partial(layer, z, list(scratch)),
        out_shape=(
            jax.ShapeDtypeStruct((rows, width), B16),
            jax.ShapeDtypeStruct((rows, width), B16),
            jax.ShapeDtypeStruct((8, LANES), F32),
            jax.ShapeDtypeStruct((10, part, hidden), F32),
            jax.ShapeDtypeStruct((6, part, hidden), F32),
            jax.ShapeDtypeStruct((8, LANES), F32),
        ),
        in_specs=[in_vmem] * 3 + [pl.BlockSpec(memory_space=pl.ANY)] * 2 + [in_vmem],
        out_specs=[in_vmem] * 6,
        scratch_shapes=list(scratch.values()),
        compiler_params=pltpu.CompilerParams(
            collective_id=0, has_side_effects=True, vmem_limit_bytes=VMEM_BYTES
        ),
    )(
        tokens.reshape(rows, width),
        masks,
        cotangent.reshape(rows, width),
        by_slot(w_in),
        w_out,
        vec,
    )

    def whole(shape):
        return pl.BlockSpec(shape, lambda j: (0,) * len(shape))

    slot_in = pl.BlockSpec((5, part, hidden), lambda j: (j, 0, 0))
    slot_out = pl.BlockSpec((3, hidden, part), lambda j: (j, 0, 0))
    state_specs = [slot_in] * 3 + [slot_out] * 3 + [whole((4, LANES))] * 3
    row_specs = [whole((rows, width))] * 2
    state = (
        by_slot(w_in),
        by_slot(m_in),
        by_slot(v_in),
        w_out,
        m_out,
        v_out,
        vec,
        as_tile(m_vec),
        as_tile(v_vec),
    )
    new = pl.pallas_call(
        updates,
        grid=(2,),
        out_shape=tuple(jax.ShapeDtypeStruct(a.shape, F32) for a in state)
        + (jax.ShapeDtypeStruct((rows, width), B16),) * 2
        + (jax.ShapeDtypeStruct((1, 1), F32),),
        in_specs=[
            slot_in,
            pl.BlockSpec((3, part, hidden), lambda j: (j, 0, 0)),
            whole((8, LANES)),
            whole((8, LANES)),
        ]
        + row_specs
        + state_specs,
        out_specs=state_specs + row_specs + [whole((1, 1))],
    )(grad_in, grad_out, grad_vec, norm, output, token_grad, *state)
    new_w_in, new_m_in, new_v_in, new_w_out, new_m_out, new_v_out = new[:6]
    new_vectors, new_m_vec, new_v_vec, output, token_grad, norm = new[6:]
    return (
        output.reshape(frames, here, width),
        token_grad.reshape(frames, here, width),
        norm.reshape(()),
        by_slot(new_w_in),
        new_w_out,
        of_tile(new_vectors),
        by_slot(new_m_in),
        new_m_out,
        of_tile(new_m_vec),
        by_slot(new_v_in),
        new_v_out,
        of_tile(new_v_vec),
    )


def solution(mesh):
    in_specs = (
        P(DP, TP, None),
        P(DP, TP),
        P(DP, TP, None),
        P(DP, None, TP),
        P(None, TP, DP),
        P(None, DP),
        P(DP, None, TP),
        P(None, TP, DP),
        P(None, DP),
        P(DP, None, TP),
        P(None, TP, DP),
        P(None, DP),
    )
    out_specs = (P(DP, TP, None), P(DP, TP, None), P()) + in_specs[3:]
    return jax.shard_map(local, mesh=mesh, in_specs=in_specs, out_specs=out_specs, check_vma=False)
```

```python
import functools
from types import SimpleNamespace

import jax
import jax.numpy as jnp
from jax import lax
from jax.experimental import pallas as pl
from jax.experimental.pallas import tpu as pltpu
from jax.sharding import PartitionSpec as P

FRAMES = 16
STEP = 10
HDIM = 64


EPS_NORM = 1e-05
CLIP_AT = 1.0
BETA_FIRST = 0.9
BETA_SECOND = 0.95
ADAM_EPS = 1e-08
DECAY_RATE = 0.1
RATE_INPUT = 0.02
RATE_OUTPUT = 0.08
RATE_VECTOR = 1.0
NEG_FILL = -1e30
GELU_A = 0.7978845608028654
GELU_B = 0.044715

F32 = jnp.float32
B16 = jnp.bfloat16
MESH = pl.DeviceIdType.MESH
CHUNK = 16
DP = "dp"
TP = "fsdp"
LANES = 128
VMEM_BYTES = 63 << 20


def at(dp, fsdp):
    return {DP: dp, TP: fsdp}


def nn(a, b):
    return lax.dot_general(a, b, (((1,), (0,)), ((), ())), preferred_element_type=F32)


def nt(a, b):
    return lax.dot_general(a, b, (((1,), (1,)), ((), ())), preferred_element_type=F32)


def tn(a, b):
    return lax.dot_general(a, b, (((0,), (0,)), ((), ())), preferred_element_type=F32)


def loop(low, high, step):
    def body(k, carry):
        step(k)
        return carry

    lax.fori_loop(low, high, body, 0)


def each(low, high, step):
    if high - low <= 8:
        for k in range(low, high):
            step(k)
    else:
        loop(low, high, step)


def scratch_of(z):
    rows, width, hidden, span = z.rows, z.width, z.hidden, z.span
    nd, nf, part, heads = z.nd, z.nf, z.part, z.heads
    outer = nd // 2
    flat = (nf, z.frames, z.here, hidden)
    vmem = pltpu.VMEM
    dma = pltpu.SemaphoreType.DMA
    return dict(
        stage_in=vmem((10, part, hidden), F32),
        stage_out=vmem((6, hidden, part), F32),
        shard=vmem((4, 4, part, hidden), B16),
        tile=vmem((8, LANES), F32),
        masked=vmem((rows, LANES), F32),
        weights=vmem((4, 4, width, hidden), B16),
        gathered=vmem((6, nf, rows, width), B16),
        gains=vmem((8, width), F32),
        tiles=vmem((nd, 8, LANES), F32),
        hats=vmem((3, rows, width), F32),
        rstds=vmem((3, rows, LANES), F32),
        work=vmem((rows, width), F32),
        mid=vmem((rows, width), F32),
        swap_out=vmem((4, span, CHUNK, width), B16),
        swap_in=vmem((4, span, CHUNK, width), B16),
        part_sum=vmem((2, 2, rows, width), F32),
        sib_out=vmem((2, 2, rows, width), B16),
        sib_in=vmem((2, 2, rows, width), B16),
        far_out=vmem((2, rows, width), B16),
        far_in=vmem((2, rows, width), B16),
        qkv=vmem((2, 3) + flat, B16),
        mixed=vmem((2,) + flat, B16),
        grad_mixed=vmem(flat, B16),
        grad_qkv=vmem((3,) + flat, B16),
        probs_a=vmem((z.frames * heads, nf * z.here, nf * z.here), F32),
        probs_b=vmem((nf * heads, rows, rows), F32),
        act=vmem((4,) + flat, B16),
        slope=vmem((4,) + flat, F32),
        grad_pre=vmem((4,) + flat, B16),
        product=vmem((outer, 2, part, hidden), F32),
        own_sum=vmem((16, outer, part, hidden), B16),
        pair_out=vmem((16, outer, part, hidden), B16),
        pair_in=vmem((16, outer, part, hidden), B16),
        line_in=vmem((16, outer, part, hidden), B16),
        vec_acc=vmem((8, width), F32),
        vec_out=vmem((width // LANES, 8, LANES), F32),
        vec_in=vmem((nd, 8, LANES), F32),
        vec_mine=vmem((8, LANES), F32),
        vec_side=vmem((nf, 8, LANES), F32),
        sq_mine=vmem((2, 8, LANES), F32),
        sq_side=vmem((nf, 8, LANES), F32),
        sq_all=vmem((nd, 8, LANES), F32),
        small_s=dma((5,)),
        small_r=dma((5,)),
        line_ws=dma((4,)),
        line_wr=dma((4, outer)),
        pair_ws=dma((4,)),
        pair_wr=dma((4,)),
        pair_wo=dma((4,)),
        own_ws=dma((4,)),
        near_ws=dma((4,)),
        near_wr=dma((4,)),
        far_ws=dma((4,)),
        copy_w=dma((4,)),
        row_s=dma((6, 5)),
        row_r=dma((6, 5)),
        sum_s=dma((6, 5)),
        sum_r=dma((6, 5)),
        swap_s=dma((4,)),
        swap_r=dma((4,)),
        stage_s=dma((16,)),
        pair_gs=dma((16,)),
        pair_gr=dma((16,)),
        line_gs=dma((16,)),
        line_gr=dma((16,)),
    )


def layer(z, names, *refs):
    tok, msk, cot, w_in, w_out, vec = refs[:6]
    out, tgr, nrm, gin, gout, gvec = refs[6:12]
    s = SimpleNamespace(**dict(zip(names, refs[12:])))
    rows, width, hidden, span = z.rows, z.width, z.hidden, z.span
    nd, nf, part, heads = z.nd, z.nf, z.part, z.heads
    frames, here = z.frames, z.here
    outer = nd // 2
    piece = here // span
    n_pairs = heads // 2
    scale = HDIM**-0.5
    gathered, weights, gains = s.gathered, s.weights, s.gains
    work, mid, shard = s.work, s.mid, s.shard
    swap_out, swap_in = s.swap_out, s.swap_in

    d, f = lax.axis_index(DP), lax.axis_index(TP)
    o, i = d // 2, d % 2
    y, c = f // 2, f % 2
    place = d % span
    base = d - place
    f_sib, f_far, f_last = y * 2 + 1 - c, (1 - y) * 2 + c, (1 - y) * 2 + 1 - c
    mate = at(o * 2 + 1 - i, f)
    sib = at(d, f_sib)
    far = at(d, f_far)

    def rcopy(src, dst, ssem, rsem, dev):
        return pltpu.make_async_remote_copy(
            src_ref=src, dst_ref=dst, send_sem=ssem, recv_sem=rsem, device_id=dev, device_id_type=MESH
        )

    in_slots = {0: [0, 1, 2], 1: [3, 4, 5], 2: [6, 7, 8, 9], 3: []}
    out_slots = {0: [0], 1: [1], 2: [], 3: [2, 3, 4, 5]}

    def stage(g):
        for n in in_slots[g]:
            yield pltpu.make_async_copy(w_in.at[n], s.stage_in.at[n], s.stage_s.at[n])
        for n in out_slots[g]:
            yield pltpu.make_async_copy(w_out.at[n], s.stage_out.at[n], s.stage_s.at[10 + n])

    def round_group(g):
        for cp in stage(g):
            cp.wait()
        for j, n in enumerate(in_slots[g]):
            shard[g, j] = s.stage_in[n].astype(B16)
        for j, n in enumerate(out_slots[g]):
            shard[g, len(in_slots[g]) + j] = s.stage_out[n].T.astype(B16)

    for g in range(4):
        for cp in stage(g):
            cp.start()
    s.tile[...] = jnp.zeros_like(s.tile)
    s.tile[0:4, :] = vec[...].astype(B16).astype(F32)

    same = lax.broadcasted_iota(jnp.int32, (here, here), 0) == lax.broadcasted_iota(
        jnp.int32, (here, here), 1
    )
    for fr in range(frames):
        line = jnp.broadcast_to(msk[fr : fr + 1, :], (here, here)).astype(F32)
        column = jnp.sum(jnp.where(same, line, 0.0), axis=1, keepdims=True)
        s.masked[fr * here : (fr + 1) * here, :] = jnp.broadcast_to(column, (here, LANES))

    bar = pltpu.get_barrier_semaphore()

    def greet(q):
        dev = at((d + q) % nd, f)
        pl.semaphore_signal(bar, inc=1, device_id=dev, device_id_type=MESH)

    each(1, nd, greet)
    for q in range(1, nf):
        dev = at(d, (f + q) % nf)
        pl.semaphore_signal(bar, inc=1, device_id=dev, device_id_type=MESH)
    pl.semaphore_wait(bar, nd - 1 + nf - 1)


    def tell(n, src_of, dst, axis):
        count, me = (nd, d) if axis == DP else (nf, f)

        def go(q):
            to = (me + q) % count
            dev = at(to, f) if axis == DP else at(d, to)
            rcopy(src_of(to), dst.at[me], s.small_s.at[n], s.small_r.at[n], dev).start()

        each(1, count, go)

    def hear(n, dst, axis):
        count = nd if axis == DP else nf
        others = dst.at[pl.ds(0, count - 1)]
        cp = rcopy(others, others, s.small_s.at[n], s.small_r.at[n], mate)
        cp.wait_recv()
        cp.wait_send()

    def total_of(ref, count):
        total = ref[0]
        if count <= 8:
            for k in range(1, count):
                total = total + ref[k]
            return total
        return lax.fori_loop(1, count, lambda k, t: t + ref[k], total)

    tell(0, lambda to: s.tile, s.tiles, DP)

    four = outer == 4
    near_row = o + 1 - 2 * (o % 2)
    next_row = jnp.where(o < 2, 2, 1)
    last_row = jnp.where(o < 2, 3, 0)
    middle = (o == 1) | (o == 2)

    def shard_rows(owner):
        return pl.ds(pl.multiple_of(owner * part, part), part)

    def shard_of(g, row, col):
        return weights.at[g, :, shard_rows(row * 2 + col), :]

    def gather_own(g):
        mine = shard_of(g, o, i)
        pltpu.make_async_copy(shard.at[g], mine, s.copy_w.at[g]).start()
        rcopy(shard.at[g], mine, s.own_ws.at[g], s.pair_wo.at[g], mate).start()

    def gather_line(g, low, high):
        def go(q):
            to = (o + q) % outer

            def start():
                rcopy(
                    shard.at[g],
                    shard_of(g, o, i),
                    s.line_ws.at[g],
                    s.line_wr.at[g, o],
                    at(to * 2 + i, f),
                ).start()

            if four:
                pl.when(jnp.abs(to - o) < 3)(start)
            else:
                start()

        each(low, high, go)

    def gather_from(g, row):
        block = shard_of(g, row, i)
        rcopy(block, block, s.line_ws.at[g], s.line_wr.at[g, row], mate).wait_recv()
        return block

    def gather_pass(g, low, high):
        if not four:

            def go(q):
                block = gather_from(g, (o + outer - q) % outer)
                rcopy(block, block, s.pair_ws.at[g], s.pair_wr.at[g], mate).start()

            each(low, high, go)
            return
        for q in range(low, high):
            if q == 1:
                block = shard_of(g, o, 1 - i)
                rcopy(block, block, s.pair_ws.at[g], s.pair_wo.at[g], mate).wait_recv()
                half = block.at[pl.ds(2, 2)]
                dev = at(near_row * 2 + i, f)
                rcopy(half, half, s.near_ws.at[g], s.near_wr.at[g], dev).start()
                half = gather_from(g, near_row).at[pl.ds(0, 2)]
                rcopy(half, half, s.pair_ws.at[g], s.pair_wr.at[g], mate).start()
            else:
                row = next_row if q == 2 else last_row
                block = gather_from(g, row)

                @pl.when(middle & (row == last_row))
                def _():
                    dev = at((3 - last_row) * 2 + i, f)
                    rcopy(block, block, s.far_ws.at[g], s.line_wr.at[g, row], dev).start()

                rcopy(block, block, s.pair_ws.at[g], s.pair_wr.at[g], mate).start()

    def gather_ready(g):
        mine = shard_of(g, o, i)
        pltpu.make_async_copy(shard.at[g], mine, s.copy_w.at[g]).wait()
        if not four:
            block = shard_of(g, o, 1 - i)
            rcopy(block, block, s.pair_ws.at[g], s.pair_wo.at[g], mate).wait_recv()
        if four:
            half = weights.at[g, pl.ds(0, 2), pl.ds(0, part), :]
            rcopy(half, half, s.near_ws.at[g], s.near_wr.at[g], mate).wait_recv()
        halves = 5 if four else 2 * (outer - 1)
        both = half_shards(g, halves)
        rcopy(both, both, s.pair_ws.at[g], s.pair_wr.at[g], mate).wait_recv()

    def half_shards(g, count):
        return weights.at[g, pl.ds(0, 2), pl.ds(0, count * part), :]

    def gather_end(g):
        def sent(sem, halves):
            both = half_shards(g, halves)
            rcopy(both, both, sem.at[g], s.pair_wr.at[g], mate).wait_send()

        if not four:
            sent(s.pair_ws, nd - 2)
            sent(s.line_ws, nd - 2)
            rest = shard_of(g, o, i)
            rcopy(rest, rest, s.own_ws.at[g], s.pair_wr.at[g], mate).wait_send()
            return
        sent(s.own_ws, 2)
        sent(s.pair_ws, 5)
        sent(s.near_ws, 1)

        @pl.when(middle)
        def _():
            sent(s.line_ws, 6)
            sent(s.far_ws, 2)

        @pl.when(jnp.logical_not(middle))
        def _():
            sent(s.line_ws, 4)

    def half_rows(h):
        return pl.ds(h * here, here)


    def spread_start(k, h):
        half = gathered.at[k, f, half_rows(h)]
        rcopy(half, half, s.row_s.at[k, 1 + h], s.row_r.at[k, 1 + h], far).start()
        if h == 1:
            block = gathered.at[k, f]
            rcopy(block, block, s.row_s.at[k, 0], s.row_r.at[k, 0], sib).start()

    def spread_near(k):
        block = gathered.at[k, f_sib]
        rcopy(block, block, s.row_s.at[k, 0], s.row_r.at[k, 0], sib).wait_recv()

    def spread_pass(k):
        for h in range(2):
            half = gathered.at[k, f_far, half_rows(h)]
            rcopy(half, half, s.row_s.at[k, 1 + h], s.row_r.at[k, 1 + h], far).wait_recv()
            rcopy(half, half, s.row_s.at[k, 3 + h], s.row_r.at[k, 3 + h], sib).start()

    def spread_far(k):
        for h in range(2):
            half = gathered.at[k, f_last, half_rows(h)]
            rcopy(half, half, s.row_s.at[k, 3 + h], s.row_r.at[k, 3 + h], sib).wait_recv()

    def spread_end(k):
        block = gathered.at[k, f]
        rcopy(block, block, s.row_s.at[k, 0], s.row_r.at[k, 0], sib).wait_send()
        half = gathered.at[k, f, half_rows(0)]
        for n in range(1, 5):
            rcopy(half, half, s.row_s.at[k, n], s.row_r.at[k, n], sib).wait_send()


    def partial(terms, pick, slot, part_rows):
        for t in range(width // hidden):
            cols = slice(t * hidden, (t + 1) * hidden)
            total = None
            for b_ref, g, j in terms:
                b = pick(b_ref)
                value = nt(b, weights[g, j, cols, :])
                total = value if total is None else total + value
            s.part_sum[slot, :, part_rows, cols] = total.reshape(2, -1, hidden)

    def collect_start(k, terms):
        par = k % 2

        def to_sib(slot, part_rows, n):
            s.sib_out[par, slot, part_rows] = s.part_sum[slot, 1 - c, part_rows].astype(B16)
            rcopy(
                s.sib_out.at[par, slot, part_rows],
                s.sib_in.at[par, slot, part_rows],
                s.sum_s.at[k, n],
                s.sum_r.at[k, n],
                sib,
            ).start()

        for h in range(2):

            def remote(ref, h=h):
                return ref[pl.ds((1 - y) * 2, 2), h].reshape(2 * here, hidden)

            partial(terms, remote, 0, half_rows(h))
            to_sib(0, half_rows(h), h)
        for h in range(2):
            half = half_rows(h)
            back = s.sib_in.at[par, 0, half]
            rcopy(back, back, s.sum_s.at[k, h], s.sum_r.at[k, h], sib).wait_recv()
            total = s.part_sum[0, c, half] + s.sib_in[par, 0, half].astype(F32)
            s.far_out[par, half] = total.astype(B16)
            rcopy(
                s.far_out.at[par, half],
                s.far_in.at[par, half],
                s.sum_s.at[k, 3 + h],
                s.sum_r.at[k, 3 + h],
                far,
            ).start()
        partial(
            terms, lambda ref: ref[pl.ds(y * 2, 2)].reshape(2 * rows, hidden), 1, pl.ds(0, rows)
        )
        to_sib(1, pl.ds(0, rows), 2)

    def collect_end(k, h):
        par = k % 2
        half = half_rows(h)
        if h == 0:
            near = s.sib_in.at[par, 1]
            rcopy(near, near, s.sum_s.at[k, 2], s.sum_r.at[k, 2], sib).wait_recv()
            rcopy(near, near, s.sum_s.at[k, 2], s.sum_r.at[k, 2], sib).wait_send()
        away = s.far_in.at[par, half]
        rcopy(away, away, s.sum_s.at[k, 3 + h], s.sum_r.at[k, 3 + h], far).wait_recv()
        for n in (h, 3 + h):
            rcopy(away, away, s.sum_s.at[k, n], s.sum_r.at[k, n], sib).wait_send()

    def collected(k, block):
        par = k % 2
        return (
            s.part_sum[1, c, block]
            + s.sib_in[par, 1, block].astype(F32)
            + s.far_in[par, block].astype(F32)
        )


    def swap_start(k):
        def go(q):
            to = (place + q) % span
            rcopy(
                swap_out.at[k, to],
                swap_in.at[k, place],
                s.swap_s.at[k],
                s.swap_r.at[k],
                at(base + to, f),
            ).start()

        each(1, span, go)
        swap_in[k, place] = swap_out[k, place]

    def swap_wait(k):
        others = swap_in.at[k, pl.ds(0, span - 1)]
        rcopy(others, others, s.swap_s.at[k], s.swap_r.at[k], mate).wait_recv()

    def swap_end(k):
        others = swap_in.at[k, pl.ds(0, span - 1)]
        rcopy(others, others, s.swap_s.at[k], s.swap_r.at[k], mate).wait_send()

    def token_rows(fr, j):
        return pl.ds(pl.multiple_of(fr * here + j * piece, piece), piece)

    def pack(k, src):
        def step(j):
            parts = [src[token_rows(fr, j), :] for fr in range(frames)]
            swap_out[k, j] = jnp.concatenate(parts, axis=0).astype(B16)

        loop(0, span, step)

    def unpack(k, dst):
        def step(j):
            value = swap_in[k, j].astype(F32)
            for fr in range(frames):
                dst[token_rows(fr, j), :] = value[fr * piece : (fr + 1) * piece]

        loop(0, span, step)

    def chunks(step, h):
        first = h * here // CHUNK
        each(first, first + here // CHUNK, lambda k: step(pl.ds(k * CHUNK, CHUNK), k))

    def norm_rows(n, value, block):
        centered = value - jnp.mean(value, axis=-1, keepdims=True)
        rstd = lax.rsqrt(jnp.mean(centered * centered, axis=-1, keepdims=True) + EPS_NORM)
        hat = centered * rstd
        s.hats[n, block] = hat
        s.rstds[n, block] = jnp.broadcast_to(rstd, (CHUNK, LANES))
        return (hat * gains[n : n + 1, :]).astype(B16)

    def norm_back(n, grad, block):
        hat = s.hats[n, block]
        rstd = s.rstds[n, block][:, 0:1]
        grad_hat = grad * gains[n : n + 1, :]
        first = jnp.mean(grad_hat, axis=-1, keepdims=True)
        second = jnp.mean(grad_hat * hat, axis=-1, keepdims=True)
        s.vec_acc[n : n + 1, :] += jnp.sum(grad * hat, axis=0, keepdims=True)
        return rstd * (grad_hat - first - hat * second)


    def pair_rows(k, pair):
        return gathered[k, pl.ds(pair * 2, 2)].reshape(2 * rows, width)

    def as_flat(value):
        return value.reshape(2, frames, here, hidden)

    def project(k, g, dst, pair):
        def step(j):
            dst[j, pl.ds(pair * 2, 2)] = as_flat(nn(pair_rows(k, pair), weights[g, j]).astype(B16))

        each(0, 3, step)

    def attend(block):
        spatial = block == 0
        n = nf * here if spatial else rows

        def load(ref, g, lanes):
            value = ref[:, g, :, lanes] if spatial else ref[g, :, :, lanes]
            return value.reshape(n, 2 * HDIM)

        def store(ref, g, lanes, value):
            if spatial:
                ref[:, g, :, lanes] = value.reshape(nf, here, 2 * HDIM)
            else:
                ref[g, :, :, lanes] = value.reshape(frames, here, 2 * HDIM)

        return n, load, store, (s.probs_a if spatial else s.probs_b)

    def head_lanes(n):
        return lax.broadcasted_iota(jnp.int32, (n, 2 * HDIM), 1) < HDIM

    def kept(n):
        query = lax.broadcasted_iota(jnp.int32, (n, n), 0)
        key = lax.broadcasted_iota(jnp.int32, (n, n), 1)
        return (query % piece == key % piece) & (key // piece <= query // piece)

    def each_pair(block, step):
        def go(k):
            first = (k % n_pairs) * 2 * HDIM
            step(k, k // n_pairs, slice(first, first + 2 * HDIM))

        each(0, (frames if block == 0 else nf) * n_pairs, go)

    def attention(block):
        n, load, store, probs = attend(block)
        qkv = s.qkv.at[block]

        def step(k, g, lanes):
            query, key, value = (load(qkv.at[j], g, lanes) for j in range(3))
            low = head_lanes(n)
            found = []
            for h in range(2):
                mine = jnp.where(low if h == 0 else ~low, query, jnp.zeros_like(query))
                scores = nt(mine, key) * scale
                if block == 1:
                    scores = jnp.where(kept(n), scores, NEG_FILL)
                expd = jnp.exp(scores - jnp.max(scores, axis=-1, keepdims=True))
                prob = expd / jnp.sum(expd, axis=-1, keepdims=True)
                probs[k * 2 + h] = prob
                found.append(nn(prob.astype(B16), value))
            store(s.mixed.at[block], g, lanes, jnp.where(low, found[0], found[1]).astype(B16))

        each_pair(block, step)

    def attention_back(block):
        n, load, store, probs = attend(block)
        qkv = s.qkv.at[block]

        def step(k, g, lanes):
            query, key, value = (load(qkv.at[j], g, lanes) for j in range(3))
            grad = load(s.grad_mixed, g, lanes)
            low = head_lanes(n)
            found = []
            for h in range(2):
                mine = jnp.where(low if h == 0 else ~low, grad, jnp.zeros_like(grad))
                prob = probs[k * 2 + h]
                grad_prob = nt(mine, value)
                inner = jnp.sum(prob * grad_prob, axis=-1, keepdims=True)
                grad_score = (prob * (grad_prob - inner)).astype(B16)
                found.append(
                    (
                        nn(grad_score, key) * scale,
                        tn(grad_score, query) * scale,
                        tn(prob.astype(B16), grad),
                    )
                )
            for j in range(3):
                both = jnp.where(low, found[0][j], found[1][j]).astype(B16)
                store(s.grad_qkv.at[j], g, lanes, both)

        each_pair(block, step)

    def mixed_back(k, g):
        def half(pair):
            value = nn(pair_rows(k, pair), weights[g, 3])
            s.grad_mixed[pl.ds(pair * 2, 2)] = as_flat(value.astype(B16))

        spread_near(k)
        half(y)
        spread_pass(k)
        spread_far(k)
        half(1 - y)


    def slot_make(slot, k, b_ref):
        value = tn(gathered[k].reshape(nf * rows, width), b_ref[...].reshape(nf * rows, hidden))
        s.product[...] = value.reshape(outer, 2, part, hidden)
        s.pair_out[slot] = s.product[:, 1 - i].astype(B16)
        s.own_sum[slot] = s.product[:, i].astype(B16)

    def slot_send(slot):
        rcopy(
            s.pair_out.at[slot],
            s.pair_in.at[slot],
            s.pair_gs.at[slot],
            s.pair_gr.at[slot],
            mate,
        ).start()

    def slot_sum(slot):
        g, j = slot // 4, slot % 4
        if g < 2:
            return gin.at[g * 3 + j] if j < 3 else gout.at[g]
        return gin.at[6 + j] if g == 2 else gout.at[2 + j]

    def slot_pass(slot):
        block = s.pair_in.at[slot]
        cp = rcopy(block, block, s.pair_gs.at[slot], s.pair_gr.at[slot], mate)
        cp.wait_recv()
        cp.wait_send()

        def both(owner):
            return s.own_sum[slot, owner].astype(F32) + s.pair_in[slot, owner].astype(F32)

        def go(q):
            to = (o + q) % outer
            s.pair_out[slot, q] = both(to).astype(B16)
            rcopy(
                s.pair_out.at[slot, q],
                s.line_in.at[slot, q],
                s.line_gs.at[slot],
                s.line_gr.at[slot],
                at(to * 2 + i, f),
            ).start()

        each(1, outer, go)
        slot_sum(slot)[...] = both(o)

    def slot_end(slot):
        block = s.line_in.at[slot, pl.ds(1, outer - 1)]
        cp = rcopy(block, block, s.line_gs.at[slot], s.line_gr.at[slot], mate)
        cp.wait_recv()
        cp.wait_send()
        total = slot_sum(slot)[...]
        if outer <= 8:
            for q in range(1, outer):
                total = total + s.line_in[slot, q].astype(F32)
        else:
            total = lax.fori_loop(
                1, outer, lambda q, t: t + s.line_in[slot, q].astype(F32), total
            )
        slot_sum(slot)[...] = total
        folded = jnp.sum((total * total).reshape(part // 8, 8, hidden), axis=0)
        for k in range(hidden // LANES):
            s.sq_mine[0] += folded[:, k * LANES : (k + 1) * LANES]

    round_group(0)
    gather_line(0, 1, outer)
    gather_own(0)
    hear(0, s.tiles, DP)
    s.tiles[d] = s.tile[...]
    per_tile = LANES // part
    for k in range(width // LANES):
        gains[:, k * LANES : (k + 1) * LANES] = total_of(
            s.tiles.at[pl.ds(k * per_tile, per_tile)], per_tile
        )
    s.vec_acc[...] = jnp.zeros_like(s.vec_acc)
    s.sq_mine[...] = jnp.zeros_like(s.sq_mine)

    def masked_rows(block):
        return jnp.broadcast_to(s.masked[block, 0:1], (CHUNK, width)) > 0.5

    def first_norm(block, k):
        value = jnp.where(masked_rows(block), gains[3:4, :], tok[block, :].astype(F32))
        work[block, :] = value
        gathered[0, f, block] = norm_rows(0, value, block)

    for h in range(2):
        chunks(first_norm, h)
        spread_start(0, h)
    round_group(1)
    gather_line(1, 1, outer)
    gather_own(1)
    gather_pass(0, 1, 2)

    def widen(block, k):
        s.part_sum[0, 0, block, :] = cot[block, :].astype(F32)

    for h in range(2):
        chunks(widen, h)
    pack(0, s.part_sum.at[0, 0])
    swap_start(0)

    gather_pass(0, 2, outer - 1)
    spread_near(0)
    spread_pass(0)
    gather_pass(0, outer - 1, outer)
    round_group(2)
    gather_ready(0)
    project(0, 0, s.qkv.at[0], y)
    spread_far(0)
    project(0, 0, s.qkv.at[0], 1 - y)
    gather_pass(1, 1, 2)
    attention(0)
    gather_pass(1, 2, outer - 1)
    collect_start(0, [(s.mixed.at[0], 0, 3)])
    gather_pass(1, outer - 1, outer)
    round_group(3)

    def take_branch(block, k):
        work[block, :] = work[block, :] + collected(0, block)

    for h in range(2):
        collect_end(0, h)
        chunks(take_branch, h)
    pack(1, work)
    swap_start(1)
    gather_line(2, 1, outer)
    gather_line(3, 1, outer)
    gather_own(2)
    gather_own(3)

    swap_wait(0)
    gathered[1, f] = swap_in[0].reshape(rows, width)
    spread_start(1, 0)
    spread_start(1, 1)
    swap_wait(1)

    def second_norm(block, k):
        value = swap_in[1, k].astype(F32)
        mid[block, :] = value
        gathered[2, f, block] = norm_rows(1, value, block)

    for h in range(2):
        chunks(second_norm, h)
        spread_start(2, h)
    spread_near(1)
    spread_pass(1)
    gather_ready(1)
    spread_near(2)
    project(2, 1, s.qkv.at[1], y)
    gather_pass(2, 1, 2)
    spread_pass(2)
    gather_pass(2, 2, outer - 1)
    spread_far(2)
    project(2, 1, s.qkv.at[1], 1 - y)
    attention(1)
    gather_pass(2, outer - 1, outer)
    collect_start(1, [(s.mixed.at[1], 1, 3)])
    gather_pass(3, 1, 2)

    def third_norm(block, k):
        value = mid[block, :] + collected(1, block)
        mid[block, :] = value
        gathered[3, f, block] = norm_rows(2, value, block)

    for h in range(2):
        collect_end(1, h)
        chunks(third_norm, h)
        spread_start(3, h)
    spread_far(1)
    gather_pass(3, 2, outer - 1)


    def up(pair):
        def step(n):
            u = nn(pair_rows(3, pair), weights[2, n])
            t = jnp.tanh(GELU_A * (u + GELU_B * u * u * u))
            half = 0.5 * (1.0 + t)
            s.act[n, pl.ds(pair * 2, 2)] = as_flat((u * half).astype(B16))
            bend = GELU_A * (1.0 + 3.0 * GELU_B * u * u)
            s.slope[n, pl.ds(pair * 2, 2)] = as_flat(half + 0.5 * u * (1.0 - t * t) * bend)

        each(0, 4, step)

    def down(pair):
        def step(n):
            grad = nn(pair_rows(1, pair), weights[3, n])
            slope = s.slope[n, pl.ds(pair * 2, 2)].reshape(2 * rows, hidden)
            s.grad_pre[n, pl.ds(pair * 2, 2)] = as_flat((grad * slope).astype(B16))

        each(0, 4, step)

    gather_ready(2)
    spread_near(3)
    up(y)
    spread_pass(3)
    gather_pass(3, outer - 1, outer)
    spread_far(3)
    up(1 - y)
    each(0, 4, lambda n: slot_make(12 + n, 1, s.act.at[n]))
    slot_send(12)
    slot_send(13)
    gather_ready(3)

    down(1 - y)
    down(y)
    slot_make(8, 3, s.grad_pre.at[0])
    slot_send(8)
    collect_start(2, [(s.grad_pre.at[n], 2, n) for n in range(4)])
    slot_pass(12)
    each(1, 4, lambda n: slot_make(8 + n, 3, s.grad_pre.at[n]))
    slot_send(9)
    slot_send(14)
    slot_send(10)
    slot_send(15)
    slot_send(11)
    slot_pass(13)

    def third_back(block, k):
        value = swap_in[0, k].astype(F32) + norm_back(2, collected(2, block), block)
        work[block, :] = value
        gathered[4, f, block] = value.astype(B16)

    for h in range(2):
        collect_end(2, h)
        chunks(third_back, h)
        spread_start(4, h)
    slot_pass(8)
    collect_start(3, [(s.act.at[n], 3, n) for n in range(4)])
    slot_pass(9)

    mixed_back(4, 1)
    slot_make(7, 4, s.mixed.at[1])
    slot_pass(14)
    slot_send(7)

    def take_output(block, k):
        swap_out[2, k] = (mid[block, :] + collected(3, block)).astype(B16)

    for h in range(2):
        collect_end(3, h)
        chunks(take_output, h)
    attention_back(1)
    slot_pass(10)
    collect_start(4, [(s.grad_qkv.at[j], 1, j) for j in range(3)])
    slot_pass(15)
    each(0, 3, lambda j: slot_make(4 + j, 2, s.grad_qkv.at[j]))

    def second_back(block, k):
        swap_out[3, k] = (work[block, :] + norm_back(1, collected(4, block), block)).astype(B16)

    for h in range(2):
        collect_end(4, h)
        chunks(second_back, h)
    swap_start(3)
    slot_pass(11)
    swap_start(2)
    slot_send(4)
    slot_send(5)
    slot_send(6)

    swap_wait(3)
    unpack(3, work)

    def take_carry(block, k):
        gathered[5, f, block] = work[block, :].astype(B16)

    for h in range(2):
        chunks(take_carry, h)
        spread_start(5, h)
    slot_pass(7)
    mixed_back(5, 0)
    slot_make(3, 5, s.mixed.at[0])
    slot_send(3)
    slot_pass(4)
    attention_back(0)

    def spatial_slot(j):
        slot_make(j, 0, s.grad_qkv.at[j])
        slot_send(j)

    loop(0, 3, spatial_slot)
    slot_pass(5)
    collect_start(5, [(s.grad_qkv.at[j], 0, j) for j in range(3)])
    slot_pass(6)
    slot_pass(3)

    def first_back(block, k):
        value = work[block, :] + norm_back(0, collected(5, block), block)
        masked = masked_rows(block)
        tgr[block, :] = jnp.where(masked, 0.0, value).astype(B16)
        s.vec_acc[3:4, :] += jnp.sum(jnp.where(masked, value, 0.0), axis=0, keepdims=True)

    for h in range(2):
        collect_end(5, h)
        chunks(first_back, h)

    for k in range(width // LANES):
        s.vec_out[k] = s.vec_acc[:, k * LANES : (k + 1) * LANES]
    tell(1, lambda to: s.vec_out.at[(to * part) // LANES], s.vec_in, DP)
    s.vec_in[d] = s.vec_out[(d * part) // LANES]
    slot_pass(0)
    swap_wait(2)
    unpack(2, mid)

    def give_output(block, k):
        out[block, :] = mid[block, :].astype(B16)

    for h in range(2):
        chunks(give_output, h)
    each(8, 16, slot_end)
    slot_pass(1)
    hear(1, s.vec_in, DP)
    s.vec_mine[...] = total_of(s.vec_in, nd)
    tell(2, lambda to: s.vec_mine, s.vec_side, TP)
    s.vec_side[f] = s.vec_mine[...]
    each(4, 8, slot_end)
    slot_end(3)
    slot_pass(2)
    hear(2, s.vec_side, TP)
    grad_vec = total_of(s.vec_side, nf)
    gvec[...] = grad_vec
    each(0, 3, slot_end)

    lane = lax.broadcasted_iota(jnp.int32, (8, LANES), 1)
    first_lane = (d * part) % LANES
    owned = (lane >= first_lane) & (lane < first_lane + part)
    s.sq_mine[0] += jnp.where(owned, grad_vec * grad_vec, 0.0) * (1.0 / nf)
    tell(3, lambda to: s.sq_mine.at[0], s.sq_side, TP)
    s.sq_side[f] = s.sq_mine[0]
    hear(3, s.sq_side, TP)
    s.sq_mine[1] = total_of(s.sq_side, nf)
    tell(4, lambda to: s.sq_mine.at[1], s.sq_all, DP)
    s.sq_all[d] = s.sq_mine[1]
    for g in range(4):
        gather_end(g)
    for k in range(6):
        spread_end(k)
    for k in range(4):
        swap_end(k)
    hear(4, s.sq_all, DP)
    total = jnp.sum(total_of(s.sq_all, nd), keepdims=True)
    nrm[...] = jnp.broadcast_to(jnp.sqrt(total), (8, LANES))


def adamw_step(weight, first, second, grad, rate):
    first = BETA_FIRST * first + (1.0 - BETA_FIRST) * grad
    second = BETA_SECOND * second + (1.0 - BETA_SECOND) * grad * grad
    fix_first = 1.0 / (1.0 - BETA_FIRST**STEP)
    fix_second = 1.0 / (1.0 - BETA_SECOND**STEP)
    update = (rate * fix_first) * first / (jnp.sqrt(second * fix_second) + ADAM_EPS)
    return (weight * (1.0 - rate * DECAY_RATE) - update, first, second)


def updates(*refs):
    grad_in, grad_out, grad_vec, norm, out, tgr = refs[:6]
    state = refs[6:15]
    new = refs[15:24]
    new_out, new_tgr, new_norm = refs[24:]
    j = pl.program_id(0)
    grad_norm = norm[0:1, 0:1]
    factor = CLIP_AT / jnp.maximum(grad_norm, CLIP_AT)

    def update(n, grad, rate):
        values = adamw_step(*(state[3 * n + k][...] for k in range(3)), grad * factor, rate)
        for k in range(3):
            new[3 * n + k][...] = values[k]

    update(0, grad_in[...], RATE_INPUT)

    update(1, jnp.stack([grad_out[n].T for n in range(3)]), RATE_OUTPUT)

    @pl.when(j == 1)

    def _():
        update(2, grad_vec[0:4, :], RATE_VECTOR)
        new_out[...] = out[...]
        new_tgr[...] = tgr[...]
        new_norm[...] = grad_norm


def local(tokens, masks, cotangent, w_in, w_out, vectors, m_in, m_out, m_vec, v_in, v_out, v_vec):
    frames, here, width = tokens.shape
    part, _, hidden = w_in.shape
    nd, nf = lax.axis_size(DP), lax.axis_size(TP)
    z = SimpleNamespace(
        rows=frames * here,
        width=width,
        hidden=hidden,
        span=FRAMES // frames,
        nd=nd,
        nf=nf,
        part=part,
        heads=hidden // HDIM,
        frames=frames,
        here=here,
    )
    rows = frames * here
    lane0 = (lax.axis_index(DP) * part) % LANES

    def as_tile(value):
        if part == LANES:
            return value
        return lax.dynamic_update_slice(jnp.zeros((4, LANES), F32), value, (0, lane0))

    def of_tile(value):
        return value if part == LANES else lax.dynamic_slice(value, (0, lane0), (4, part))

    def by_slot(value):
        return value.transpose(1, 0, 2)

    vec = as_tile(vectors)
    scratch = scratch_of(z)
    in_vmem = pl.BlockSpec(memory_space=pltpu.VMEM)
    output, token_grad, norm, grad_in, grad_out, grad_vec = pl.pallas_call(
        functools.partial(layer, z, list(scratch)),
        out_shape=(
            jax.ShapeDtypeStruct((rows, width), B16),
            jax.ShapeDtypeStruct((rows, width), B16),
            jax.ShapeDtypeStruct((8, LANES), F32),
            jax.ShapeDtypeStruct((10, part, hidden), F32),
            jax.ShapeDtypeStruct((6, part, hidden), F32),
            jax.ShapeDtypeStruct((8, LANES), F32),
        ),
        in_specs=[in_vmem] * 3 + [pl.BlockSpec(memory_space=pl.ANY)] * 2 + [in_vmem],
        out_specs=[in_vmem] * 6,
        scratch_shapes=list(scratch.values()),
        compiler_params=pltpu.CompilerParams(
            collective_id=0, has_side_effects=True, vmem_limit_bytes=VMEM_BYTES
        ),
    )(
        tokens.reshape(rows, width),
        masks,
        cotangent.reshape(rows, width),
        by_slot(w_in),
        w_out,
        vec,
    )

    def whole(shape):
        return pl.BlockSpec(shape, lambda j: (0,) * len(shape))

    slot_in = pl.BlockSpec((5, part, hidden), lambda j: (j, 0, 0))
    slot_out = pl.BlockSpec((3, hidden, part), lambda j: (j, 0, 0))
    state_specs = [slot_in] * 3 + [slot_out] * 3 + [whole((4, LANES))] * 3
    row_specs = [whole((rows, width))] * 2
    state = (
        by_slot(w_in),
        by_slot(m_in),
        by_slot(v_in),
        w_out,
        m_out,
        v_out,
        vec,
        as_tile(m_vec),
        as_tile(v_vec),
    )
    new = pl.pallas_call(
        updates,
        grid=(2,),
        out_shape=tuple(jax.ShapeDtypeStruct(a.shape, F32) for a in state)
        + (jax.ShapeDtypeStruct((rows, width), B16),) * 2
        + (jax.ShapeDtypeStruct((1, 1), F32),),
        in_specs=[
            slot_in,
            pl.BlockSpec((3, part, hidden), lambda j: (j, 0, 0)),
            whole((8, LANES)),
            whole((8, LANES)),
        ]
        + row_specs
        + state_specs,
        out_specs=state_specs + row_specs + [whole((1, 1))],
    )(grad_in, grad_out, grad_vec, norm, output, token_grad, *state)
    new_w_in, new_m_in, new_v_in, new_w_out, new_m_out, new_v_out = new[:6]
    new_vectors, new_m_vec, new_v_vec, output, token_grad, norm = new[6:]
    return (
        output.reshape(frames, here, width),
        token_grad.reshape(frames, here, width),
        norm.reshape(()),
        by_slot(new_w_in),
        new_w_out,
        of_tile(new_vectors),
        by_slot(new_m_in),
        new_m_out,
        of_tile(new_m_vec),
        by_slot(new_v_in),
        new_v_out,
        of_tile(new_v_vec),
    )


def solution(mesh):
    in_specs = (
        P(DP, TP, None),
        P(DP, TP),
        P(DP, TP, None),
        P(DP, None, TP),
        P(None, TP, DP),
        P(None, DP),
        P(DP, None, TP),
        P(None, TP, DP),
        P(None, DP),
        P(DP, None, TP),
        P(None, TP, DP),
        P(None, DP),
    )
    out_specs = (P(DP, TP, None), P(DP, TP, None), P()) + in_specs[3:]
    return jax.shard_map(local, mesh=mesh, in_specs=in_specs, out_specs=out_specs, check_vma=False)
```

```python
import functools
from types import SimpleNamespace

import jax
import jax.numpy as jnp
from jax import lax
from jax.experimental import pallas as pl
from jax.experimental.pallas import tpu as pltpu
from jax.sharding import PartitionSpec as P

FRAMES = 16
STEP = 10
HDIM = 64


EPS_NORM = 1e-05
CLIP_AT = 1.0
BETA_FIRST = 0.9
BETA_SECOND = 0.95
ADAM_EPS = 1e-08
DECAY_RATE = 0.1
RATE_INPUT = 0.02
RATE_OUTPUT = 0.08
RATE_VECTOR = 1.0
NEG_FILL = -1e30
GELU_A = 0.7978845608028654
GELU_B = 0.044715

F32 = jnp.float32
B16 = jnp.bfloat16
MESH = pl.DeviceIdType.MESH
CHUNK = 16
DP = "dp"
TP = "fsdp"
LANES = 128
VMEM_BYTES = 63 << 20


def at(dp, fsdp):
    return {DP: dp, TP: fsdp}


def nn(a, b):
    return lax.dot_general(a, b, (((1,), (0,)), ((), ())), preferred_element_type=F32)


def nt(a, b):
    return lax.dot_general(a, b, (((1,), (1,)), ((), ())), preferred_element_type=F32)


def tn(a, b):
    return lax.dot_general(a, b, (((0,), (0,)), ((), ())), preferred_element_type=F32)


def loop(low, high, step):
    def body(k, carry):
        step(k)
        return carry

    lax.fori_loop(low, high, body, 0)


def each(low, high, step):
    if high - low <= 8:
        for k in range(low, high):
            step(k)
    else:
        loop(low, high, step)


def scratch_of(z):
    rows, width, hidden, span = z.rows, z.width, z.hidden, z.span
    nd, nf, part, heads = z.nd, z.nf, z.part, z.heads
    outer = nd // 2
    flat = (nf, z.frames, z.here, hidden)
    vmem = pltpu.VMEM
    dma = pltpu.SemaphoreType.DMA
    return dict(
        stage_in=vmem((10, part, hidden), F32),
        stage_out=vmem((6, hidden, part), F32),
        shard=vmem((4, 4, part, hidden), B16),
        tile=vmem((8, LANES), F32),
        masked=vmem((rows, LANES), F32),
        weights=vmem((4, 4, width, hidden), B16),
        gathered=vmem((6, nf, rows, width), B16),
        gains=vmem((8, width), F32),
        tiles=vmem((nd, 8, LANES), F32),
        hats=vmem((3, rows, width), F32),
        rstds=vmem((3, rows, LANES), F32),
        work=vmem((rows, width), F32),
        mid=vmem((rows, width), F32),
        swap_out=vmem((4, span, CHUNK, width), B16),
        swap_in=vmem((4, span, CHUNK, width), B16),
        part_sum=vmem((2, 2, rows, width), F32),
        sib_out=vmem((2, 2, rows, width), B16),
        sib_in=vmem((2, 2, rows, width), B16),
        far_out=vmem((2, rows, width), B16),
        far_in=vmem((2, rows, width), B16),
        qkv=vmem((2, 3) + flat, B16),
        mixed=vmem((2,) + flat, B16),
        grad_mixed=vmem(flat, B16),
        grad_qkv=vmem((3,) + flat, B16),
        probs_a=vmem((z.frames * heads, nf * z.here, nf * z.here), F32),
        probs_b=vmem((nf * heads, rows, rows), F32),
        act=vmem((4,) + flat, B16),
        slope=vmem((4,) + flat, F32),
        grad_pre=vmem((4,) + flat, B16),
        product=vmem((outer, 2, part, hidden), F32),
        own_sum=vmem((16, outer, part, hidden), B16),
        pair_out=vmem((16, outer, part, hidden), B16),
        pair_in=vmem((16, outer, part, hidden), B16),
        line_in=vmem((16, outer, part, hidden), B16),
        vec_acc=vmem((8, width), F32),
        vec_out=vmem((width // LANES, 8, LANES), F32),
        vec_in=vmem((nd, 8, LANES), F32),
        vec_mine=vmem((8, LANES), F32),
        vec_side=vmem((nf, 8, LANES), F32),
        sq_mine=vmem((2, 8, LANES), F32),
        sq_side=vmem((nf, 8, LANES), F32),
        sq_all=vmem((nd, 8, LANES), F32),
        small_s=dma((5,)),
        small_r=dma((5,)),
        line_ws=dma((4,)),
        line_wr=dma((4, outer)),
        pair_ws=dma((4,)),
        pair_wr=dma((4,)),
        pair_wo=dma((4,)),
        own_ws=dma((4,)),
        near_ws=dma((4,)),
        near_wr=dma((4,)),
        far_ws=dma((4,)),
        copy_w=dma((4,)),
        row_s=dma((6, 5)),
        row_r=dma((6, 5)),
        sum_s=dma((6, 5)),
        sum_r=dma((6, 5)),
        swap_s=dma((4,)),
        swap_r=dma((4,)),
        stage_s=dma((16,)),
        pair_gs=dma((16,)),
        pair_gr=dma((16,)),
        line_gs=dma((16,)),
        line_gr=dma((16,)),
    )


def layer(z, names, *refs):
    tok, msk, cot, w_in, w_out, vec = refs[:6]
    out, tgr, nrm, gin, gout, gvec = refs[6:12]
    s = SimpleNamespace(**dict(zip(names, refs[12:])))
    rows, width, hidden, span = z.rows, z.width, z.hidden, z.span
    nd, nf, part, heads = z.nd, z.nf, z.part, z.heads
    frames, here = z.frames, z.here
    outer = nd // 2
    piece = here // span
    n_pairs = heads // 2
    scale = HDIM**-0.5
    gathered, weights, gains = s.gathered, s.weights, s.gains
    work, mid, shard = s.work, s.mid, s.shard
    swap_out, swap_in = s.swap_out, s.swap_in

    d, f = lax.axis_index(DP), lax.axis_index(TP)
    o, i = d // 2, d % 2
    y, c = f // 2, f % 2
    place = d % span
    base = d - place
    f_sib, f_far, f_last = y * 2 + 1 - c, (1 - y) * 2 + c, (1 - y) * 2 + 1 - c
    mate = at(o * 2 + 1 - i, f)
    sib = at(d, f_sib)
    far = at(d, f_far)

    def rcopy(src, dst, ssem, rsem, dev):
        return pltpu.make_async_remote_copy(
            src_ref=src, dst_ref=dst, send_sem=ssem, recv_sem=rsem, device_id=dev, device_id_type=MESH
        )

    in_slots = {0: [0, 1, 2], 1: [3, 4, 5], 2: [6, 7, 8, 9], 3: []}
    out_slots = {0: [0], 1: [1], 2: [], 3: [2, 3, 4, 5]}

    def stage(g):
        for n in in_slots[g]:
            yield pltpu.make_async_copy(w_in.at[n], s.stage_in.at[n], s.stage_s.at[n])
        for n in out_slots[g]:
            yield pltpu.make_async_copy(w_out.at[n], s.stage_out.at[n], s.stage_s.at[10 + n])

    def round_group(g):
        for cp in stage(g):
            cp.wait()
        for j, n in enumerate(in_slots[g]):
            shard[g, j] = s.stage_in[n].astype(B16)
        for j, n in enumerate(out_slots[g]):
            shard[g, len(in_slots[g]) + j] = s.stage_out[n].T.astype(B16)

    for g in range(4):
        for cp in stage(g):
            cp.start()
    s.tile[...] = jnp.zeros_like(s.tile)
    s.tile[0:4, :] = vec[...].astype(B16).astype(F32)

    same = lax.broadcasted_iota(jnp.int32, (here, here), 0) == lax.broadcasted_iota(
        jnp.int32, (here, here), 1
    )
    for fr in range(frames):
        line = jnp.broadcast_to(msk[fr : fr + 1, :], (here, here)).astype(F32)
        column = jnp.sum(jnp.where(same, line, 0.0), axis=1, keepdims=True)
        s.masked[fr * here : (fr + 1) * here, :] = jnp.broadcast_to(column, (here, LANES))

    bar = pltpu.get_barrier_semaphore()

    def greet(q):
        dev = at((d + q) % nd, f)
        pl.semaphore_signal(bar, inc=1, device_id=dev, device_id_type=MESH)

    each(1, nd, greet)
    for q in range(1, nf):
        dev = at(d, (f + q) % nf)
        pl.semaphore_signal(bar, inc=1, device_id=dev, device_id_type=MESH)
    pl.semaphore_wait(bar, nd - 1 + nf - 1)


    def tell(n, src_of, dst, axis):
        count, me = (nd, d) if axis == DP else (nf, f)

        def go(q):
            to = (me + q) % count
            dev = at(to, f) if axis == DP else at(d, to)
            rcopy(src_of(to), dst.at[me], s.small_s.at[n], s.small_r.at[n], dev).start()

        each(1, count, go)

    def hear(n, dst, axis):
        count = nd if axis == DP else nf
        others = dst.at[pl.ds(0, count - 1)]
        cp = rcopy(others, others, s.small_s.at[n], s.small_r.at[n], mate)
        cp.wait_recv()
        cp.wait_send()

    def total_of(ref, count):
        total = ref[0]
        if count <= 8:
            for k in range(1, count):
                total = total + ref[k]
            return total
        return lax.fori_loop(1, count, lambda k, t: t + ref[k], total)

    tell(0, lambda to: s.tile, s.tiles, DP)

    four = outer == 4
    near_row = o + 1 - 2 * (o % 2)
    next_row = jnp.where(o < 2, 2, 1)
    last_row = jnp.where(o < 2, 3, 0)
    middle = (o == 1) | (o == 2)

    def shard_rows(owner):
        return pl.ds(pl.multiple_of(owner * part, part), part)

    def shard_of(g, row, col):
        return weights.at[g, :, shard_rows(row * 2 + col), :]

    def gather_own(g):
        mine = shard_of(g, o, i)
        pltpu.make_async_copy(shard.at[g], mine, s.copy_w.at[g]).start()
        rcopy(shard.at[g], mine, s.own_ws.at[g], s.pair_wo.at[g], mate).start()

    def gather_line(g, low, high):
        def go(q):
            to = (o + q) % outer

            def start():
                rcopy(
                    shard.at[g],
                    shard_of(g, o, i),
                    s.line_ws.at[g],
                    s.line_wr.at[g, o],
                    at(to * 2 + i, f),
                ).start()

            if four:
                pl.when(jnp.abs(to - o) < 3)(start)
            else:
                start()

        each(low, high, go)

    def gather_from(g, row):
        block = shard_of(g, row, i)
        rcopy(block, block, s.line_ws.at[g], s.line_wr.at[g, row], mate).wait_recv()
        return block

    def gather_pass(g, low, high):
        if not four:

            def go(q):
                block = gather_from(g, (o + outer - q) % outer)
                rcopy(block, block, s.pair_ws.at[g], s.pair_wr.at[g], mate).start()

            each(low, high, go)
            return
        for q in range(low, high):
            if q == 1:
                block = shard_of(g, o, 1 - i)
                rcopy(block, block, s.pair_ws.at[g], s.pair_wo.at[g], mate).wait_recv()
                half = block.at[pl.ds(2, 2)]
                dev = at(near_row * 2 + i, f)
                rcopy(half, half, s.near_ws.at[g], s.near_wr.at[g], dev).start()
                half = gather_from(g, near_row).at[pl.ds(0, 2)]
                rcopy(half, half, s.pair_ws.at[g], s.pair_wr.at[g], mate).start()
            else:
                row = next_row if q == 2 else last_row
                block = gather_from(g, row)

                @pl.when(middle & (row == last_row))
                def _():
                    dev = at((3 - last_row) * 2 + i, f)
                    rcopy(block, block, s.far_ws.at[g], s.line_wr.at[g, row], dev).start()

                rcopy(block, block, s.pair_ws.at[g], s.pair_wr.at[g], mate).start()

    def gather_ready(g):
        mine = shard_of(g, o, i)
        pltpu.make_async_copy(shard.at[g], mine, s.copy_w.at[g]).wait()
        if not four:
            block = shard_of(g, o, 1 - i)
            rcopy(block, block, s.pair_ws.at[g], s.pair_wo.at[g], mate).wait_recv()
        if four:
            half = weights.at[g, pl.ds(0, 2), pl.ds(0, part), :]
            rcopy(half, half, s.near_ws.at[g], s.near_wr.at[g], mate).wait_recv()
        halves = 5 if four else 2 * (outer - 1)
        both = half_shards(g, halves)
        rcopy(both, both, s.pair_ws.at[g], s.pair_wr.at[g], mate).wait_recv()

    def half_shards(g, count):
        return weights.at[g, pl.ds(0, 2), pl.ds(0, count * part), :]

    def gather_end(g):
        def sent(sem, halves):
            both = half_shards(g, halves)
            rcopy(both, both, sem.at[g], s.pair_wr.at[g], mate).wait_send()

        if not four:
            sent(s.pair_ws, nd - 2)
            sent(s.line_ws, nd - 2)
            rest = shard_of(g, o, i)
            rcopy(rest, rest, s.own_ws.at[g], s.pair_wr.at[g], mate).wait_send()
            return
        sent(s.own_ws, 2)
        sent(s.pair_ws, 5)
        sent(s.near_ws, 1)

        @pl.when(middle)
        def _():
            sent(s.line_ws, 6)
            sent(s.far_ws, 2)

        @pl.when(jnp.logical_not(middle))
        def _():
            sent(s.line_ws, 4)

    def half_rows(h):
        return pl.ds(h * here, here)


    def spread_start(k, h):
        half = gathered.at[k, f, half_rows(h)]
        rcopy(half, half, s.row_s.at[k, 1 + h], s.row_r.at[k, 1 + h], far).start()
        if h == 1:
            block = gathered.at[k, f]
            rcopy(block, block, s.row_s.at[k, 0], s.row_r.at[k, 0], sib).start()

    def spread_near(k):
        block = gathered.at[k, f_sib]
        rcopy(block, block, s.row_s.at[k, 0], s.row_r.at[k, 0], sib).wait_recv()

    def spread_pass(k):
        for h in range(2):
            half = gathered.at[k, f_far, half_rows(h)]
            rcopy(half, half, s.row_s.at[k, 1 + h], s.row_r.at[k, 1 + h], far).wait_recv()
            rcopy(half, half, s.row_s.at[k, 3 + h], s.row_r.at[k, 3 + h], sib).start()

    def spread_far(k):
        for h in range(2):
            half = gathered.at[k, f_last, half_rows(h)]
            rcopy(half, half, s.row_s.at[k, 3 + h], s.row_r.at[k, 3 + h], sib).wait_recv()

    def spread_end(k):
        block = gathered.at[k, f]
        rcopy(block, block, s.row_s.at[k, 0], s.row_r.at[k, 0], sib).wait_send()
        half = gathered.at[k, f, half_rows(0)]
        for n in range(1, 5):
            rcopy(half, half, s.row_s.at[k, n], s.row_r.at[k, n], sib).wait_send()


    def partial(terms, pick, slot, part_rows):
        for t in range(width // hidden):
            cols = slice(t * hidden, (t + 1) * hidden)
            total = None
            for b_ref, g, j in terms:
                b = pick(b_ref)
                value = nt(b, weights[g, j, cols, :])
                total = value if total is None else total + value
            s.part_sum[slot, :, part_rows, cols] = total.reshape(2, -1, hidden)

    def collect_start(k, terms):
        par = k % 2

        def to_sib(slot, part_rows, n):
            s.sib_out[par, slot, part_rows] = s.part_sum[slot, 1 - c, part_rows].astype(B16)
            rcopy(
                s.sib_out.at[par, slot, part_rows],
                s.sib_in.at[par, slot, part_rows],
                s.sum_s.at[k, n],
                s.sum_r.at[k, n],
                sib,
            ).start()

        for h in range(2):

            def remote(ref, h=h):
                return ref[pl.ds((1 - y) * 2, 2), h].reshape(2 * here, hidden)

            partial(terms, remote, 0, half_rows(h))
            to_sib(0, half_rows(h), h)
        for h in range(2):
            half = half_rows(h)
            back = s.sib_in.at[par, 0, half]
            rcopy(back, back, s.sum_s.at[k, h], s.sum_r.at[k, h], sib).wait_recv()
            total = s.part_sum[0, c, half] + s.sib_in[par, 0, half].astype(F32)
            s.far_out[par, half] = total.astype(B16)
            rcopy(
                s.far_out.at[par, half],
                s.far_in.at[par, half],
                s.sum_s.at[k, 3 + h],
                s.sum_r.at[k, 3 + h],
                far,
            ).start()
        partial(
            terms, lambda ref: ref[pl.ds(y * 2, 2)].reshape(2 * rows, hidden), 1, pl.ds(0, rows)
        )
        to_sib(1, pl.ds(0, rows), 2)

    def collect_end(k, h):
        par = k % 2
        half = half_rows(h)
        if h == 0:
            near = s.sib_in.at[par, 1]
            rcopy(near, near, s.sum_s.at[k, 2], s.sum_r.at[k, 2], sib).wait_recv()
            rcopy(near, near, s.sum_s.at[k, 2], s.sum_r.at[k, 2], sib).wait_send()
        away = s.far_in.at[par, half]
        rcopy(away, away, s.sum_s.at[k, 3 + h], s.sum_r.at[k, 3 + h], far).wait_recv()
        for n in (h, 3 + h):
            rcopy(away, away, s.sum_s.at[k, n], s.sum_r.at[k, n], sib).wait_send()

    def collected(k, block):
        par = k % 2
        return (
            s.part_sum[1, c, block]
            + s.sib_in[par, 1, block].astype(F32)
            + s.far_in[par, block].astype(F32)
        )


    def swap_start(k):
        def go(q):
            to = (place + q) % span
            rcopy(
                swap_out.at[k, to],
                swap_in.at[k, place],
                s.swap_s.at[k],
                s.swap_r.at[k],
                at(base + to, f),
            ).start()

        each(1, span, go)
        swap_in[k, place] = swap_out[k, place]

    def swap_wait(k):
        others = swap_in.at[k, pl.ds(0, span - 1)]
        rcopy(others, others, s.swap_s.at[k], s.swap_r.at[k], mate).wait_recv()

    def swap_end(k):
        others = swap_in.at[k, pl.ds(0, span - 1)]
        rcopy(others, others, s.swap_s.at[k], s.swap_r.at[k], mate).wait_send()

    def token_rows(fr, j):
        return pl.ds(pl.multiple_of(fr * here + j * piece, piece), piece)

    def pack(k, src):
        def step(j):
            parts = [src[token_rows(fr, j), :] for fr in range(frames)]
            swap_out[k, j] = jnp.concatenate(parts, axis=0).astype(B16)

        loop(0, span, step)

    def unpack(k, dst):
        def step(j):
            value = swap_in[k, j].astype(F32)
            for fr in range(frames):
                dst[token_rows(fr, j), :] = value[fr * piece : (fr + 1) * piece]

        loop(0, span, step)

    def chunks(step, h):
        first = h * here // CHUNK
        each(first, first + here // CHUNK, lambda k: step(pl.ds(k * CHUNK, CHUNK), k))

    def norm_rows(n, value, block):
        centered = value - jnp.mean(value, axis=-1, keepdims=True)
        rstd = lax.rsqrt(jnp.mean(centered * centered, axis=-1, keepdims=True) + EPS_NORM)
        hat = centered * rstd
        s.hats[n, block] = hat
        s.rstds[n, block] = jnp.broadcast_to(rstd, (CHUNK, LANES))
        return (hat * gains[n : n + 1, :]).astype(B16)

    def norm_back(n, grad, block):
        hat = s.hats[n, block]
        rstd = s.rstds[n, block][:, 0:1]
        grad_hat = grad * gains[n : n + 1, :]
        first = jnp.mean(grad_hat, axis=-1, keepdims=True)
        second = jnp.mean(grad_hat * hat, axis=-1, keepdims=True)
        s.vec_acc[n : n + 1, :] += jnp.sum(grad * hat, axis=0, keepdims=True)
        return rstd * (grad_hat - first - hat * second)


    def pair_rows(k, pair):
        return gathered[k, pl.ds(pair * 2, 2)].reshape(2 * rows, width)

    def as_flat(value):
        return value.reshape(2, frames, here, hidden)

    def project(k, g, dst, pair):
        def step(j):
            dst[j, pl.ds(pair * 2, 2)] = as_flat(nn(pair_rows(k, pair), weights[g, j]).astype(B16))

        each(0, 3, step)

    def attend(block):
        spatial = block == 0
        n = nf * here if spatial else rows

        def load(ref, g, lanes):
            value = ref[:, g, :, lanes] if spatial else ref[g, :, :, lanes]
            return value.reshape(n, 2 * HDIM)

        def store(ref, g, lanes, value):
            if spatial:
                ref[:, g, :, lanes] = value.reshape(nf, here, 2 * HDIM)
            else:
                ref[g, :, :, lanes] = value.reshape(frames, here, 2 * HDIM)

        return n, load, store, (s.probs_a if spatial else s.probs_b)

    def head_lanes(n):
        return lax.broadcasted_iota(jnp.int32, (n, 2 * HDIM), 1) < HDIM

    def kept(n):
        query = lax.broadcasted_iota(jnp.int32, (n, n), 0)
        key = lax.broadcasted_iota(jnp.int32, (n, n), 1)
        return (query % piece == key % piece) & (key // piece <= query // piece)

    def each_pair(block, step):
        def go(k):
            first = (k % n_pairs) * 2 * HDIM
            step(k, k // n_pairs, slice(first, first + 2 * HDIM))

        each(0, (frames if block == 0 else nf) * n_pairs, go)

    def attention(block):
        n, load, store, probs = attend(block)
        qkv = s.qkv.at[block]

        def step(k, g, lanes):
            query, key, value = (load(qkv.at[j], g, lanes) for j in range(3))
            low = head_lanes(n)
            found = []
            for h in range(2):
                mine = jnp.where(low if h == 0 else ~low, query, jnp.zeros_like(query))
                scores = nt(mine, key) * scale
                if block == 1:
                    scores = jnp.where(kept(n), scores, NEG_FILL)
                expd = jnp.exp(scores - jnp.max(scores, axis=-1, keepdims=True))
                prob = expd / jnp.sum(expd, axis=-1, keepdims=True)
                probs[k * 2 + h] = prob
                found.append(nn(prob.astype(B16), value))
            store(s.mixed.at[block], g, lanes, jnp.where(low, found[0], found[1]).astype(B16))

        each_pair(block, step)

    def attention_back(block):
        n, load, store, probs = attend(block)
        qkv = s.qkv.at[block]

        def step(k, g, lanes):
            query, key, value = (load(qkv.at[j], g, lanes) for j in range(3))
            grad = load(s.grad_mixed, g, lanes)
            low = head_lanes(n)
            found = []
            for h in range(2):
                mine = jnp.where(low if h == 0 else ~low, grad, jnp.zeros_like(grad))
                prob = probs[k * 2 + h]
                grad_prob = nt(mine, value)
                inner = jnp.sum(prob * grad_prob, axis=-1, keepdims=True)
                grad_score = (prob * (grad_prob - inner)).astype(B16)
                found.append(
                    (
                        nn(grad_score, key) * scale,
                        tn(grad_score, query) * scale,
                        tn(prob.astype(B16), grad),
                    )
                )
            for j in range(3):
                both = jnp.where(low, found[0][j], found[1][j]).astype(B16)
                store(s.grad_qkv.at[j], g, lanes, both)

        each_pair(block, step)

    def mixed_back(k, g):
        def half(pair):
            value = nn(pair_rows(k, pair), weights[g, 3])
            s.grad_mixed[pl.ds(pair * 2, 2)] = as_flat(value.astype(B16))

        spread_near(k)
        half(y)
        spread_pass(k)
        spread_far(k)
        half(1 - y)


    def slot_make(slot, k, b_ref):
        value = tn(gathered[k].reshape(nf * rows, width), b_ref[...].reshape(nf * rows, hidden))
        s.product[...] = value.reshape(outer, 2, part, hidden)
        s.pair_out[slot] = s.product[:, 1 - i].astype(B16)
        s.own_sum[slot] = s.product[:, i].astype(B16)

    def slot_send(slot):
        rcopy(
            s.pair_out.at[slot],
            s.pair_in.at[slot],
            s.pair_gs.at[slot],
            s.pair_gr.at[slot],
            mate,
        ).start()

    def slot_sum(slot):
        g, j = slot // 4, slot % 4
        if g < 2:
            return gin.at[g * 3 + j] if j < 3 else gout.at[g]
        return gin.at[6 + j] if g == 2 else gout.at[2 + j]

    def slot_pass(slot):
        block = s.pair_in.at[slot]
        cp = rcopy(block, block, s.pair_gs.at[slot], s.pair_gr.at[slot], mate)
        cp.wait_recv()
        cp.wait_send()

        def both(owner):
            return s.own_sum[slot, owner].astype(F32) + s.pair_in[slot, owner].astype(F32)

        def go(q):
            to = (o + q) % outer
            s.pair_out[slot, q] = both(to).astype(B16)
            rcopy(
                s.pair_out.at[slot, q],
                s.line_in.at[slot, q],
                s.line_gs.at[slot],
                s.line_gr.at[slot],
                at(to * 2 + i, f),
            ).start()

        each(1, outer, go)
        slot_sum(slot)[...] = both(o)

    def slot_end(slot):
        block = s.line_in.at[slot, pl.ds(1, outer - 1)]
        cp = rcopy(block, block, s.line_gs.at[slot], s.line_gr.at[slot], mate)
        cp.wait_recv()
        cp.wait_send()
        total = slot_sum(slot)[...]
        if outer <= 8:
            for q in range(1, outer):
                total = total + s.line_in[slot, q].astype(F32)
        else:
            total = lax.fori_loop(
                1, outer, lambda q, t: t + s.line_in[slot, q].astype(F32), total
            )
        slot_sum(slot)[...] = total
        folded = jnp.sum((total * total).reshape(part // 8, 8, hidden), axis=0)
        for k in range(hidden // LANES):
            s.sq_mine[0] += folded[:, k * LANES : (k + 1) * LANES]

    round_group(0)
    gather_line(0, 1, outer)
    gather_own(0)
    hear(0, s.tiles, DP)
    s.tiles[d] = s.tile[...]
    per_tile = LANES // part
    for k in range(width // LANES):
        gains[:, k * LANES : (k + 1) * LANES] = total_of(
            s.tiles.at[pl.ds(k * per_tile, per_tile)], per_tile
        )
    s.vec_acc[...] = jnp.zeros_like(s.vec_acc)
    s.sq_mine[...] = jnp.zeros_like(s.sq_mine)

    def masked_rows(block):
        return jnp.broadcast_to(s.masked[block, 0:1], (CHUNK, width)) > 0.5

    def first_norm(block, k):
        value = jnp.where(masked_rows(block), gains[3:4, :], tok[block, :].astype(F32))
        work[block, :] = value
        gathered[0, f, block] = norm_rows(0, value, block)

    for h in range(2):
        chunks(first_norm, h)
        spread_start(0, h)
    round_group(1)
    gather_line(1, 1, outer)
    gather_own(1)
    gather_pass(0, 1, 2)

    def widen(block, k):
        s.part_sum[0, 0, block, :] = cot[block, :].astype(F32)

    for h in range(2):
        chunks(widen, h)
    pack(0, s.part_sum.at[0, 0])
    swap_start(0)

    gather_pass(0, 2, outer - 1)
    spread_near(0)
    spread_pass(0)
    gather_pass(0, outer - 1, outer)
    round_group(2)
    gather_ready(0)
    project(0, 0, s.qkv.at[0], y)
    spread_far(0)
    project(0, 0, s.qkv.at[0], 1 - y)
    gather_pass(1, 1, 2)
    attention(0)
    gather_pass(1, 2, outer - 1)
    collect_start(0, [(s.mixed.at[0], 0, 3)])
    gather_pass(1, outer - 1, outer)
    round_group(3)

    def take_branch(block, k):
        work[block, :] = work[block, :] + collected(0, block)

    for h in range(2):
        collect_end(0, h)
        chunks(take_branch, h)
    pack(1, work)
    swap_start(1)
    gather_line(2, 1, outer)
    gather_line(3, 1, outer)
    gather_own(2)
    gather_own(3)

    swap_wait(0)
    gathered[1, f] = swap_in[0].reshape(rows, width)
    spread_start(1, 0)
    spread_start(1, 1)
    swap_wait(1)

    def second_norm(block, k):
        value = swap_in[1, k].astype(F32)
        mid[block, :] = value
        gathered[2, f, block] = norm_rows(1, value, block)

    for h in range(2):
        chunks(second_norm, h)
        spread_start(2, h)
    spread_near(1)
    spread_pass(1)
    gather_ready(1)
    spread_near(2)
    project(2, 1, s.qkv.at[1], y)
    gather_pass(2, 1, 2)
    spread_pass(2)
    gather_pass(2, 2, outer - 1)
    spread_far(2)
    project(2, 1, s.qkv.at[1], 1 - y)
    attention(1)
    gather_pass(2, outer - 1, outer)
    collect_start(1, [(s.mixed.at[1], 1, 3)])
    gather_pass(3, 1, 2)

    def third_norm(block, k):
        value = mid[block, :] + collected(1, block)
        mid[block, :] = value
        gathered[3, f, block] = norm_rows(2, value, block)

    for h in range(2):
        collect_end(1, h)
        chunks(third_norm, h)
        spread_start(3, h)
    spread_far(1)
    gather_pass(3, 2, outer - 1)


    def up(pair):
        def step(n):
            u = nn(pair_rows(3, pair), weights[2, n])
            t = jnp.tanh(GELU_A * (u + GELU_B * u * u * u))
            half = 0.5 * (1.0 + t)
            s.act[n, pl.ds(pair * 2, 2)] = as_flat((u * half).astype(B16))
            bend = GELU_A * (1.0 + 3.0 * GELU_B * u * u)
            s.slope[n, pl.ds(pair * 2, 2)] = as_flat(half + 0.5 * u * (1.0 - t * t) * bend)

        each(0, 4, step)

    def down(pair):
        def step(n):
            grad = nn(pair_rows(1, pair), weights[3, n])
            slope = s.slope[n, pl.ds(pair * 2, 2)].reshape(2 * rows, hidden)
            s.grad_pre[n, pl.ds(pair * 2, 2)] = as_flat((grad * slope).astype(B16))

        each(0, 4, step)

    gather_ready(2)
    spread_near(3)
    up(y)
    spread_pass(3)
    gather_pass(3, outer - 1, outer)
    spread_far(3)
    up(1 - y)
    each(0, 4, lambda n: slot_make(12 + n, 1, s.act.at[n]))
    slot_send(12)
    slot_send(13)
    gather_ready(3)

    down(1 - y)
    down(y)
    slot_make(8, 3, s.grad_pre.at[0])
    slot_send(8)
    collect_start(2, [(s.grad_pre.at[n], 2, n) for n in range(4)])
    slot_pass(12)
    each(1, 4, lambda n: slot_make(8 + n, 3, s.grad_pre.at[n]))
    slot_send(9)
    slot_send(14)
    slot_send(10)
    slot_send(15)
    slot_send(11)
    slot_pass(13)

    def third_back(block, k):
        value = swap_in[0, k].astype(F32) + norm_back(2, collected(2, block), block)
        work[block, :] = value
        gathered[4, f, block] = value.astype(B16)

    for h in range(2):
        collect_end(2, h)
        chunks(third_back, h)
        spread_start(4, h)
    slot_pass(8)
    collect_start(3, [(s.act.at[n], 3, n) for n in range(4)])
    slot_pass(9)

    mixed_back(4, 1)
    slot_make(7, 4, s.mixed.at[1])
    slot_pass(14)
    slot_send(7)

    def take_output(block, k):
        swap_out[2, k] = (mid[block, :] + collected(3, block)).astype(B16)

    for h in range(2):
        collect_end(3, h)
        chunks(take_output, h)
    attention_back(1)
    slot_pass(10)
    collect_start(4, [(s.grad_qkv.at[j], 1, j) for j in range(3)])
    slot_pass(15)
    each(0, 3, lambda j: slot_make(4 + j, 2, s.grad_qkv.at[j]))

    def second_back(block, k):
        swap_out[3, k] = (work[block, :] + norm_back(1, collected(4, block), block)).astype(B16)

    for h in range(2):
        collect_end(4, h)
        chunks(second_back, h)
    swap_start(3)
    slot_pass(11)
    swap_start(2)
    slot_send(4)
    slot_send(5)
    slot_send(6)

    swap_wait(3)
    unpack(3, work)

    def take_carry(block, k):
        gathered[5, f, block] = work[block, :].astype(B16)

    for h in range(2):
        chunks(take_carry, h)
        spread_start(5, h)
    slot_pass(7)
    mixed_back(5, 0)
    slot_make(3, 5, s.mixed.at[0])
    slot_send(3)
    slot_pass(4)
    attention_back(0)

    def spatial_slot(j):
        slot_make(j, 0, s.grad_qkv.at[j])
        slot_send(j)

    loop(0, 3, spatial_slot)
    slot_pass(5)
    collect_start(5, [(s.grad_qkv.at[j], 0, j) for j in range(3)])
    slot_pass(6)
    slot_pass(3)

    def first_back(block, k):
        value = work[block, :] + norm_back(0, collected(5, block), block)
        masked = masked_rows(block)
        tgr[block, :] = jnp.where(masked, 0.0, value).astype(B16)
        s.vec_acc[3:4, :] += jnp.sum(jnp.where(masked, value, 0.0), axis=0, keepdims=True)

    for h in range(2):
        collect_end(5, h)
        chunks(first_back, h)

    for k in range(width // LANES):
        s.vec_out[k] = s.vec_acc[:, k * LANES : (k + 1) * LANES]
    tell(1, lambda to: s.vec_out.at[(to * part) // LANES], s.vec_in, DP)
    s.vec_in[d] = s.vec_out[(d * part) // LANES]
    slot_pass(0)
    swap_wait(2)
    unpack(2, mid)

    def give_output(block, k):
        out[block, :] = mid[block, :].astype(B16)

    for h in range(2):
        chunks(give_output, h)
    each(8, 16, slot_end)
    slot_pass(1)
    hear(1, s.vec_in, DP)
    s.vec_mine[...] = total_of(s.vec_in, nd)
    tell(2, lambda to: s.vec_mine, s.vec_side, TP)
    s.vec_side[f] = s.vec_mine[...]
    each(4, 8, slot_end)
    slot_end(3)
    slot_pass(2)
    hear(2, s.vec_side, TP)
    grad_vec = total_of(s.vec_side, nf)
    gvec[...] = grad_vec
    each(0, 3, slot_end)

    lane = lax.broadcasted_iota(jnp.int32, (8, LANES), 1)
    first_lane = (d * part) % LANES
    owned = (lane >= first_lane) & (lane < first_lane + part)
    s.sq_mine[0] += jnp.where(owned, grad_vec * grad_vec, 0.0) * (1.0 / nf)
    tell(3, lambda to: s.sq_mine.at[0], s.sq_side, TP)
    s.sq_side[f] = s.sq_mine[0]
    hear(3, s.sq_side, TP)
    s.sq_mine[1] = total_of(s.sq_side, nf)
    tell(4, lambda to: s.sq_mine.at[1], s.sq_all, DP)
    s.sq_all[d] = s.sq_mine[1]
    for g in range(4):
        gather_end(g)
    for k in range(6):
        spread_end(k)
    for k in range(4):
        swap_end(k)
    hear(4, s.sq_all, DP)
    total = jnp.sum(total_of(s.sq_all, nd), keepdims=True)
    nrm[...] = jnp.broadcast_to(jnp.sqrt(total), (8, LANES))


def adamw_step(weight, first, second, grad, rate):
    first = BETA_FIRST * first + (1.0 - BETA_FIRST) * grad
    second = BETA_SECOND * second + (1.0 - BETA_SECOND) * grad * grad
    fix_first = 1.0 / (1.0 - BETA_FIRST**STEP)
    fix_second = 1.0 / (1.0 - BETA_SECOND**STEP)
    update = (rate * fix_first) * first / (jnp.sqrt(second * fix_second) + ADAM_EPS)
    return (weight * (1.0 - rate * DECAY_RATE) - update, first, second)


def updates(*refs):
    grad_in, grad_out, grad_vec, norm, out, tgr = refs[:6]
    state = refs[6:15]
    new = refs[15:24]
    new_out, new_tgr, new_norm = refs[24:27]
    held = refs[27:35]
    in_s, out_s = refs[35:]
    pieces = [(0, 2 * n) for n in range(5)] + [(1, 2 * n) for n in range(3)]

    def load(p, k):
        kind, first = pieces[p]
        slots = pl.ds(first, 2)
        source = state[3 * kind + k] if k < 3 else (grad_out if kind else grad_in)
        return pltpu.make_async_copy(source.at[slots], held[4 * kind + k].at[slots], in_s.at[p, k])

    def store(p, k):
        kind, first = pieces[p]
        slots = pl.ds(first, 2)
        return pltpu.make_async_copy(
            held[4 * kind + k].at[slots], new[3 * kind + k].at[slots], out_s.at[p, k]
        )

    for p in range(len(pieces)):
        for k in range(4):
            load(p, k).start()
    grad_norm = norm[0:1, 0:1]
    factor = CLIP_AT / jnp.maximum(grad_norm, CLIP_AT)
    new_norm[...] = grad_norm
    new_out[...] = out[...]
    new_tgr[...] = tgr[...]
    values = adamw_step(*(state[6 + k][...] for k in range(3)), grad_vec[0:4, :] * factor, RATE_VECTOR)
    for k in range(3):
        new[6 + k][...] = values[k]
    for p, (kind, first) in enumerate(pieces):
        for k in range(4):
            load(p, k).wait()
        for n in range(first, first + 2):
            weight, one, two, grad = (held[4 * kind + k][n] for k in range(4))
            grad = (grad.T if kind else grad) * factor
            values = adamw_step(weight, one, two, grad, RATE_OUTPUT if kind else RATE_INPUT)
            for k in range(3):
                held[4 * kind + k][n] = values[k]
        for k in range(3):
            store(p, k).start()
    for p in range(len(pieces)):
        for k in range(3):
            store(p, k).wait()


def local(tokens, masks, cotangent, w_in, w_out, vectors, m_in, m_out, m_vec, v_in, v_out, v_vec):
    frames, here, width = tokens.shape
    part, _, hidden = w_in.shape
    nd, nf = lax.axis_size(DP), lax.axis_size(TP)
    z = SimpleNamespace(
        rows=frames * here,
        width=width,
        hidden=hidden,
        span=FRAMES // frames,
        nd=nd,
        nf=nf,
        part=part,
        heads=hidden // HDIM,
        frames=frames,
        here=here,
    )
    rows = frames * here
    lane0 = (lax.axis_index(DP) * part) % LANES

    def as_tile(value):
        if part == LANES:
            return value
        return lax.dynamic_update_slice(jnp.zeros((4, LANES), F32), value, (0, lane0))

    def of_tile(value):
        return value if part == LANES else lax.dynamic_slice(value, (0, lane0), (4, part))

    def by_slot(value):
        return value.transpose(1, 0, 2)

    vec = as_tile(vectors)
    scratch = scratch_of(z)
    in_vmem = pl.BlockSpec(memory_space=pltpu.VMEM)
    output, token_grad, norm, grad_in, grad_out, grad_vec = pl.pallas_call(
        functools.partial(layer, z, list(scratch)),
        out_shape=(
            jax.ShapeDtypeStruct((rows, width), B16),
            jax.ShapeDtypeStruct((rows, width), B16),
            jax.ShapeDtypeStruct((8, LANES), F32),
            jax.ShapeDtypeStruct((10, part, hidden), F32),
            jax.ShapeDtypeStruct((6, part, hidden), F32),
            jax.ShapeDtypeStruct((8, LANES), F32),
        ),
        in_specs=[in_vmem] * 3 + [pl.BlockSpec(memory_space=pl.ANY)] * 2 + [in_vmem],
        out_specs=[in_vmem] * 6,
        scratch_shapes=list(scratch.values()),
        compiler_params=pltpu.CompilerParams(
            collective_id=0, has_side_effects=True, vmem_limit_bytes=VMEM_BYTES
        ),
    )(
        tokens.reshape(rows, width),
        masks,
        cotangent.reshape(rows, width),
        by_slot(w_in),
        w_out,
        vec,
    )

    anywhere = pl.BlockSpec(memory_space=pl.ANY)
    state = (
        by_slot(w_in),
        by_slot(m_in),
        by_slot(v_in),
        w_out,
        m_out,
        v_out,
        vec,
        as_tile(m_vec),
        as_tile(v_vec),
    )
    new = pl.pallas_call(
        updates,
        out_shape=tuple(jax.ShapeDtypeStruct(a.shape, F32) for a in state)
        + (jax.ShapeDtypeStruct((rows, width), B16),) * 2
        + (jax.ShapeDtypeStruct((1, 1), F32),),
        in_specs=[anywhere] * 2 + [in_vmem] * 4 + [anywhere] * 6 + [in_vmem] * 3,
        out_specs=[anywhere] * 6 + [in_vmem] * 6,
        scratch_shapes=[pltpu.VMEM((10, part, hidden), F32)] * 4
        + [pltpu.VMEM((6, hidden, part), F32)] * 3
        + [pltpu.VMEM((6, part, hidden), F32)]
        + [pltpu.SemaphoreType.DMA((8, 4)), pltpu.SemaphoreType.DMA((8, 3))],
        compiler_params=pltpu.CompilerParams(vmem_limit_bytes=40 << 20),
    )(grad_in, grad_out, grad_vec, norm, output, token_grad, *state)
    new_w_in, new_m_in, new_v_in, new_w_out, new_m_out, new_v_out = new[:6]
    new_vectors, new_m_vec, new_v_vec, output, token_grad, norm = new[6:]
    return (
        output.reshape(frames, here, width),
        token_grad.reshape(frames, here, width),
        norm.reshape(()),
        by_slot(new_w_in),
        new_w_out,
        of_tile(new_vectors),
        by_slot(new_m_in),
        new_m_out,
        of_tile(new_m_vec),
        by_slot(new_v_in),
        new_v_out,
        of_tile(new_v_vec),
    )


def solution(mesh):
    in_specs = (
        P(DP, TP, None),
        P(DP, TP),
        P(DP, TP, None),
        P(DP, None, TP),
        P(None, TP, DP),
        P(None, DP),
        P(DP, None, TP),
        P(None, TP, DP),
        P(None, DP),
        P(DP, None, TP),
        P(None, TP, DP),
        P(None, DP),
    )
    out_specs = (P(DP, TP, None), P(DP, TP, None), P()) + in_specs[3:]
    return jax.shard_map(local, mesh=mesh, in_specs=in_specs, out_specs=out_specs, check_vma=False)
```
